512 devices in a mesh: band: 32 (over z, core), col: 16 (over y, x).
Axes of the slice: x: 4, y: 4, z: 16, core: 2. Of those that a mesh axis runs over, the one named last changes fastest.
Arguments:
- atm_state: bfloat16 [128, 1440, 384], P('band', 'col'), may hold values from -6 to 6
- spec_gain: float32 [2, 720, 384], P(None, None, 'col'), may hold values from -4 to 4
- mlp_in: bfloat16 [384, 768], replicated, may hold values from -0.3125 to 0.3125
- mlp_out: bfloat16 [768, 384], replicated, may hold values from -0.21875 to 0.21875
- flux_proj: bfloat16 [384, 16], replicated, may hold values from -0.3125 to 0.3125
- pair_rows: int32 [32, 32, 4], P(None, 'band'), may hold values from 0 to 3, as said below
- pair_count: int32 [32, 32], P(None, 'band'), may hold values from 0 to 4, as said below
- pair_weight: float32 [192, 32, 4], P('band'), may hold values from 0.05 to 1
- ocean_state: bfloat16 [192, 1440, 200], P('band', 'col'), may hold values from -6 to 6
- force_proj: bfloat16 [16, 200], replicated, may hold values from -1.5 to 1.5
- depth_kernel: float32 [7, 7, 200], replicated, may hold values from -0.875 to 0.875
- ocean_in: bfloat16 [200, 800], replicated, may hold values from -0.4375 to 0.4375
- ocean_out: bfloat16 [800, 200], replicated, may hold values from -0.21875 to 0.21875
- surf_proj: bfloat16 [200, 16], replicated, may hold values from -0.4375 to 0.4375
- land_mask: int32 [192, 1440], P('band', 'col'), may hold values 0 or 1
Outputs:
- atm_next: bfloat16 [128, 1440, 384], P('band', 'col')
- ocean_next: bfloat16 [192, 1440, 200], P('band', 'col')
- atm_surface: bfloat16 [128, 1440, 16], P('band', 'col')
The draws below stay inside these ranges and needn't reach their ends.
Inputs may be any that keep to these rules, and one draw needn't show every extreme that they name: `pair_rows`: for each pair, 4 distinct local row numbers of the atmosphere band; only the first pair_count of them are used. pair_count[r, s] is 0 unless 0 <= s - r < 4; in every draw some pair uses all 4 slots.
All inputs are finite; a program needn't handle non-finite values. No bound on the sum of `land_mask` on one device may be relied on, other than what follows from the above.
Results may differ from the reference program's by a relative error of at most 0.02.
Values may be sent and summed in bfloat16 or wider, within the bound.
A program may use at most 64 MiB of HBM per device.

```python
import jax
import jax.numpy as jnp
from jax import lax

C = 384
HID_A = 768
LON = 1440
MM = 720
F = 16
G = 16
HO = 200
HFF_O = 800
RIM = 3
KS = 7
SPAN = 4
AL_DEV = 4
OR_DEV = 6
P_SIZE = 4
ALAT = 128
OROWS = 192
N_BAND = 32


def cover_lists(key):
    first, second, third = jax.random.split(key, 3)
    keys = jax.random.split(first, N_BAND * N_BAND)
    rows = jax.vmap(lambda single: jax.random.permutation(single, AL_DEV))(keys)
    rows = rows.reshape(N_BAND, N_BAND, AL_DEV).astype(jnp.int32)
    counts = jax.random.randint(second, (N_BAND, N_BAND), 0, AL_DEV + 1)
    target = jnp.arange(N_BAND, dtype=jnp.int32)[:, None]
    source = jnp.arange(N_BAND, dtype=jnp.int32)[None, :]
    offset = source - target
    counts = jnp.where((offset >= 0) & (offset < SPAN), counts, 0)
    chosen = jax.random.randint(third, (), 0, N_BAND)
    counts = jnp.where((target == chosen) & (source == chosen), AL_DEV, counts)
    return (rows, counts.astype(jnp.int32))


def draw_pair_rows(key, part):
    return cover_lists(key)[0]


def draw_pair_count(key, part):
    return cover_lists(key)[1]


def plant(array, own_key, smallest, high):
    dims = array.shape
    spot = [jax.random.randint(jax.random.fold_in(own_key, axis), (), 0, dims[axis]) for axis in range(len(dims))]
    array = array.at[tuple(spot)].set(smallest)
    longest = dims.index(max(dims))
    spot[longest] = (spot[longest] + 1) % dims[longest]
    return array.at[tuple(spot)].set(high)


def level_of(key, extent, cuts, smallest, largest):
    level, own = 1.0, jax.random.fold_in(key, 6)
    for axis_at, shards_of in cuts:
        heights = jnp.exp(jax.random.uniform(jax.random.fold_in(own, axis_at), (shards_of,), jnp.float32, smallest / len(cuts), largest / len(cuts)))
        level = level * jnp.repeat(heights, extent[axis_at] // shards_of).reshape([-1 if axis == axis_at else 1 for axis in range(len(extent))])
    return level


def bell_draw(stream_key, extent, scale, limit, cuts=(), kind=jnp.bfloat16):
    entries = scale * jax.random.normal(stream_key, extent, jnp.float32)
    if cuts:
        entries = entries * level_of(stream_key, extent, cuts, -0.22, 0.18)
    return jnp.clip(entries, -limit, limit).astype(kind)


def setup_inputs(seed: int = 0) -> dict:
    splits = jax.random.split(jax.random.key(seed), 16)
    atm_state = bell_draw(splits[0], (ALAT, LON, C), 1.0, 6.0, ((0, 32), (1, 16)))
    spec_gain = bell_draw(splits[1], (2, MM, C), 0.7, 4.0, ((2, 16),), jnp.float32)
    mlp_in = bell_draw(splits[2], (C, HID_A), C ** -0.5, 0.3125)
    mlp_out = bell_draw(splits[3], (HID_A, C), HID_A ** -0.5, 0.21875)
    flux_proj = bell_draw(splits[4], (C, F), C ** -0.5, 0.3125)
    pair_rows = draw_pair_rows(jax.random.fold_in(splits[15], 71), 0)
    pair_count = draw_pair_count(jax.random.fold_in(splits[15], 71), 0)
    pair_weight = jnp.clip(0.05 + 0.95 * jax.random.uniform(splits[7], (OROWS, N_BAND, P_SIZE), jnp.float32) ** level_of(splits[7], (OROWS, N_BAND, P_SIZE), ((0, 32),), -0.2, 0.2), 0.05, 1.0)
    ocean_state = bell_draw(splits[8], (OROWS, LON, HO), 1.0, 6.0, ((0, 32), (1, 16)))
    force_proj = bell_draw(splits[9], (F, HO), F ** -0.5, 1.5)
    depth_kernel = bell_draw(splits[10], (KS, KS, HO), (KS * KS) ** -0.5, 0.875, (), jnp.float32)
    ocean_in = bell_draw(splits[11], (HO, HFF_O), HO ** -0.5, 0.4375)
    ocean_out = bell_draw(splits[12], (HFF_O, HO), HFF_O ** -0.5, 0.21875)
    surf_proj = bell_draw(splits[13], (HO, G), HO ** -0.5, 0.4375)
    land_mask = plant((jax.random.randint(splits[14], (OROWS, LON), 0, 10) < 7).astype(jnp.int32), jax.random.fold_in(splits[14], 1), 0, 1)
    return dict(atm_state=atm_state, spec_gain=spec_gain, mlp_in=mlp_in, mlp_out=mlp_out, flux_proj=flux_proj, pair_rows=pair_rows, pair_count=pair_count, pair_weight=pair_weight, ocean_state=ocean_state, force_proj=force_proj, depth_kernel=depth_kernel, ocean_in=ocean_in, ocean_out=ocean_out, surf_proj=surf_proj, land_mask=land_mask)


HIGH = lax.Precision.HIGHEST

def layer_norm(values):
    mean = lax.optimization_barrier(jnp.mean(values, axis=-1, keepdims=True))
    centred = values - mean
    spread = lax.optimization_barrier(jnp.mean(centred * centred, axis=-1, keepdims=True))
    return centred * lax.rsqrt(spread + 1e-05)

def atmos_band(block, spec_gain, mlp_in, mlp_out, flux_proj):
    values = block.astype(jnp.float32)
    spectra = jnp.fft.rfft(values, axis=1)[:, :MM, :]
    cos_part = jnp.real(spectra)
    sin_part = -jnp.imag(spectra)
    new_cos = spec_gain[0] * cos_part + spec_gain[1] * sin_part
    new_sin = spec_gain[0] * sin_part - spec_gain[1] * cos_part
    padded = jnp.zeros((values.shape[0], LON // 2 + 1, values.shape[2]), spectra.dtype)
    padded = padded.at[:, :MM, :].set(new_cos - 1j * new_sin)
    zonal = jnp.fft.irfft(padded, n=LON, axis=1) + new_cos[:, :1, :] / LON
    zonal = lax.optimization_barrier(zonal.astype(jnp.bfloat16)).astype(jnp.float32)
    mixed = values + zonal
    normed = layer_norm(mixed).astype(jnp.bfloat16)
    inner = jax.nn.gelu(jnp.dot(normed, mlp_in, preferred_element_type=jnp.float32)).astype(jnp.bfloat16)
    state = (mixed + jnp.dot(inner, mlp_out, preferred_element_type=jnp.float32)).astype(jnp.bfloat16)
    flux = jnp.dot(state, flux_proj, preferred_element_type=jnp.float32).astype(jnp.bfloat16)
    return (state, flux)

def reference(atm_state, spec_gain, mlp_in, mlp_out, flux_proj, pair_rows, pair_count, pair_weight, ocean_state, force_proj, depth_kernel, ocean_in, ocean_out, surf_proj, land_mask):
    bands = atm_state.reshape(N_BAND, AL_DEV, LON, C)
    atm_next, flux = lax.map(lambda piece: atmos_band(piece, spec_gain, mlp_in, mlp_out, flux_proj), bands)
    atm_next = atm_next.reshape(ALAT, LON, C)
    flux = flux.reshape(ALAT, LON, F)
    slot = jnp.arange(P_SIZE, dtype=jnp.int32)
    start = (jnp.arange(N_BAND, dtype=jnp.int32) * AL_DEV)[:, None]
    weights = pair_weight.reshape(N_BAND, OR_DEV, N_BAND, P_SIZE)
    band_ids = jnp.arange(N_BAND, dtype=jnp.int32)

    def forward(band):
        valid = slot[None, :] < pair_count[band][:, None]
        where_rows = (start + pair_rows[band]).reshape(-1)
        picked = jnp.take(flux, where_rows, axis=0).reshape(N_BAND, P_SIZE, LON, F).astype(jnp.float32)
        picked = jnp.where(valid[:, :, None, None], picked, 0.0)
        return jnp.einsum('isp,splf->ilf', weights[band], picked, precision=HIGH)
    forcing = lax.map(forward, band_ids).reshape(OROWS, LON, F).astype(jnp.bfloat16)
    lifted = (ocean_state.astype(jnp.float32) + jnp.dot(forcing, force_proj, preferred_element_type=jnp.float32)).astype(jnp.bfloat16)
    framed = jnp.pad(lifted, ((RIM, RIM), (0, 0), (0, 0)))
    framed = jnp.concatenate([framed[:, LON - RIM:], framed, framed[:, :RIM]], axis=1)

    def ocean_band(band):
        block = lax.dynamic_slice_in_dim(framed, band * OR_DEV, OR_DEV + 2 * RIM, 0).astype(jnp.float32)
        stencil = jnp.zeros((OR_DEV, LON, HO), jnp.float32)
        for down in range(KS):
            for across in range(KS):
                stencil = stencil + depth_kernel[down, across] * block[down:down + OR_DEV, across:across + LON]
        normed = layer_norm(stencil).astype(jnp.bfloat16)
        hidden = jax.nn.gelu(jnp.dot(normed, ocean_in, preferred_element_type=jnp.float32)).astype(jnp.bfloat16)
        centre = block[RIM:RIM + OR_DEV, RIM:RIM + LON]
        sea = lax.dynamic_slice_in_dim(land_mask, band * OR_DEV, OR_DEV, 0).astype(jnp.float32)
        result = ((centre + jnp.dot(hidden, ocean_out, preferred_element_type=jnp.float32)) * sea[:, :, None]).astype(jnp.bfloat16)
        surface = jnp.dot(result, surf_proj, preferred_element_type=jnp.float32).astype(jnp.bfloat16)
        return (result, surface)
    ocean_next, surface = lax.map(ocean_band, band_ids)

    def backward(total, band):
        valid = slot[None, :] < pair_count[band][:, None]
        where_rows = (start + pair_rows[band]).reshape(-1)
        back = jnp.einsum('isp,ilg->splg', weights[band], surface[band].astype(jnp.float32), precision=HIGH)
        back = lax.optimization_barrier(back.astype(jnp.bfloat16)).astype(jnp.float32)
        back = jnp.where(valid[:, :, None, None], back, 0.0)
        total = total.at[where_rows].add(back.reshape(N_BAND * P_SIZE, LON, G))
        return (total, None)
    gathered, _ = lax.scan(backward, jnp.zeros((ALAT, LON, G), jnp.float32), band_ids)
    return (atm_next, ocean_next.reshape(OROWS, LON, HO), gathered.astype(jnp.bfloat16))
```

```python
import functools

import jax
import jax.numpy as jnp
import numpy as np
from jax import lax
from jax.experimental import pallas as pl
from jax.experimental.pallas import tpu as pltpu
from jax.sharding import PartitionSpec as P

F32 = jnp.float32
BF16 = jnp.bfloat16
MESH = pl.DeviceIdType.MESH
ANY = pl.ANY

SPAN = 4
LATS = 4
SLOTS = 4
LON = 1440
WAVES = 720
LOCAL = 90
PAD = 96
RIM = 3
KS = 7
CH = 384
OWN = 24
HALF = LON // 2
BLOCKS = 8
TAB = BLOCKS * PAD
WPAD = TAB // 2
ROWS = 6
HO = 200
HP = 256
FIELDS = 16
NT = (((1,), (1,)), ((), ()))


def tables():
    place = np.arange(PAD)
    block = np.arange(BLOCKS)
    inside = np.broadcast_to(place < LOCAL, (BLOCKS, PAD)).reshape(-1)
    lon_in = (LOCAL * block[:, None] + place[None]).reshape(-1)
    rim = np.where(place < LOCAL + RIM, place, place - PAD)
    lon_out = (LOCAL * block[:, None] + rim[None]).reshape(-1)
    forward = np.zeros((2, TAB, TAB), np.float64)
    inverse = np.zeros((2, TAB, TAB), np.float64)
    deal = np.zeros((2 * WPAD, TAB), np.float64)
    count = WAVES // 2
    for parity in range(2):
        wave = 2 * np.arange(count) + parity
        angle = 2 * np.pi * (wave[:, None] * lon_in[None] % LON) / LON
        forward[parity, :count] = np.cos(angle) * inside
        forward[parity, WPAD : WPAD + count] = np.sin(angle) * inside
        angle = 2 * np.pi * (lon_out[:, None] * wave[None] % LON) / LON
        inverse[parity, :, :count] = np.cos(angle)
        inverse[parity, :, WPAD : WPAD + count] = np.sin(angle)
        deal[parity * WPAD + np.arange(count), wave] = 1.0
    return [t.astype(np.float32).astype(jnp.bfloat16) for t in (forward, inverse, deal)]


def iota(shape, axis):
    return lax.broadcasted_iota(jnp.int32, shape, axis)


def one_hot(condition):
    return jnp.where(condition, 1.0, 0.0).astype(BF16)


def dot(a, b):
    return jnp.dot(a, b, preferred_element_type=F32)


def dot_nt(a, b):
    return lax.dot_general(a, b, NT, preferred_element_type=F32)


def windows(tile):
    out = []
    for d in range(16):
        lo, hi = max(OWN * d, 128 * tile), min(OWN * d + OWN, 128 * tile + 128)
        if lo < hi:
            out.append((d, lo, hi - lo))
    return out


def body(
    bands,
    cols,
    atm,
    gain,
    w_in,
    w_out,
    flux_t,
    p_rows,
    p_count,
    p_weight,
    ocean,
    force,
    kernel_w,
    o_in,
    o_out_t,
    surf_t,
    land,
    tab_f,
    tab_i,
    deal,
    atm_out,
    ocean_out,
    surf_out,
    xv,
    st,
    x32,
    rolled,
    send1,
    recv1,
    send2,
    recv2,
    tf,
    ti,
    dl,
    gv,
    gx,
    gt,
    w1,
    w2,
    fpt,
    ocv,
    oc,
    obs,
    obr,
    ohs,
    ohr,
    ahs,
    ahr,
    sel,
    selr,
    wown,
    wr,
    kv,
    kp,
    fp,
    fpc,
    oin,
    oot,
    spt,
    lm,
    lmp,
    s0,
    biga,
    bigb,
    wst,
    xs,
    fxt,
    sxt,
    mx,
    nx,
    flx,
    flr,
    bks,
    bkr,
    ao,
    oo,
    so,
    ld,
    out_sem,
    a1s,
    a1r,
    a2s,
    a2r,
    sls,
    slr,
    ws,
    wrs,
    ohss,
    ohrs,
    obss,
    obrs,
    ahss,
    ahrs,
    fls,
    flrs,
    bss,
    brs,
):
    me = lax.axis_index("col")
    band = lax.axis_index("band")

    def col_at(k):
        return lax.rem(me + k + cols, cols)

    def band_at(k):
        return lax.rem(band + k + bands, bands)

    def load(src, dst, k):
        c = pltpu.make_async_copy(src, dst, ld.at[k])
        c.start()
        return c

    l_atm = load(atm, xv, 0)
    l_ocean = load(ocean, ocv, 1)
    l_force = load(force, fp, 2)
    l_kernel = load(kernel_w, kv, 3)
    l_gain = load(gain, gv, 4)
    l_deal = load(deal, dl, 5)
    l_tf = load(tab_f, tf, 6)
    l_flux = load(flux_t, fpt, 7)
    l_surf = load(surf_t, spt, 8)
    l_land = load(land, lm, 9)
    l_ti = load(tab_i, ti, 10)
    l_w1 = load(w_in, w1, 11)
    l_w2 = load(w_out, w2, 12)
    l_oin = load(o_in, oin, 13)
    l_oot = load(o_out_t, oot, 14)

    barrier = pltpu.get_barrier_semaphore()
    for k in range(1, cols):
        pl.semaphore_signal(barrier, inc=1, device_id={"col": col_at(k)}, device_id_type=MESH)
    for k in (1, 2, 3, 4):
        for sign in (1, -1):
            pl.semaphore_signal(
                barrier, inc=1, device_id={"band": band_at(sign * k)}, device_id_type=MESH
            )

    def remote(src, dst, send_sem, recv_sem, device):
        return pltpu.make_async_remote_copy(
            src_ref=src,
            dst_ref=dst,
            send_sem=send_sem,
            recv_sem=recv_sem,
            device_id=device,
            device_id_type=MESH,
        )

    lane = iota((PAD, 128), 1)
    st[:, LATS * LOCAL :, :] = jnp.zeros((3, LATS * (PAD - LOCAL), 128), F32)
    l_atm.wait()
    for l in range(LOCAL):
        for t in range(3):
            cut = slice(128 * t, 128 * t + 128)
            st[t, LATS * l : LATS * l + LATS, :] = xv[l, :, cut].astype(F32)
    for a in range(LATS):
        for t in range(3):
            part = st.at[t][pl.ds(a, PAD, stride=LATS), :]
            x32[a, :, 128 * t : 128 * t + 128] = part
            rolled[a, t] = pltpu.roll(part, OWN * a, 1) if a else part
    for d in range(cols):
        out = jnp.zeros((PAD, 128), F32)
        for t in range(3):
            for e, lo, n in windows(t):
                if e == d:
                    for a in range(LATS):
                        mask = ((lane - (lo + OWN * a)) & 127) < n
                        out = jnp.where(mask, rolled[a, t], out)
        send1[d] = out.astype(BF16)
    recv1[me] = send1[me]

    row8 = iota((8, 128), 0)
    lane8 = iota((8, 128), 1)
    zero8 = jnp.zeros((8, 128), F32)
    for q in (0, 1, 6, 7):
        sel[q] = zero8
    for k in range(SPAN):
        other = band - k
        at = jnp.maximum(other, 0)
        used = jnp.where(other >= 0, p_count[0, at], 0)
        vec = zero8
        for p in range(SLOTS):
            target = jnp.where(p < used, SLOTS * p_rows[0, p, at] + p, -1)
            vec = jnp.where(lane8 == target, 1.0, vec)
        sel[5 - k] = vec
    vec = zero8
    for o in range(SPAN):
        at = jnp.minimum(band + o, bands - 1)
        for p in range(SLOTS):
            here = (lane8 // 16 == o) & (lane8 % SLOTS == p)
            for i in range(ROWS):
                vec = jnp.where(here & (row8 == i), p_weight[i, p, at], vec)
    wown[...] = vec

    pl.semaphore_wait(barrier, cols - 1 + 8)

    a1 = []
    for k in range(1, cols):
        d = col_at(k)
        c = remote(send1.at[d], recv1.at[me], a1s.at[k], a1r.at[k], {"col": d})
        c.start()
        a1.append(c)

    l_ocean.wait()
    oc[RIM : RIM + ROWS] = jnp.zeros((ROWS, PAD, HP), F32)
    oc[RIM : RIM + ROWS, 0:LOCAL, 0:HO] = ocv[...].astype(F32)
    for i in range(ROWS):
        ohs[0, i] = pltpu.roll(oc[RIM + i, 0:8, :], 2, 0)
        ohs[1, i] = pltpu.roll(oc[RIM + i, 80:96, :], 6, 0)[8:16]
    oh = []
    for side, k in ((0, -1), (1, 1)):
        c = remote(ohs.at[side], ohr.at[side], ohss.at[side], ohrs.at[side], {"col": col_at(k)})
        c.start()
        oh.append(c)
    small = []
    for o in (0, 2, 3, 4, 5):
        c = remote(
            sel.at[pl.ds(5 - o, 3)], selr.at[o], sls.at[o], slr.at[o], {"band": band_at(1 - o)}
        )
        c.start()
        small.append(c)
    for side, k in ((0, 1), (1, -1)):
        c = remote(wown, wr.at[side], ws.at[side], wrs.at[side], {"band": band_at(k)})
        c.start()
        small.append(c)
    selr[1] = sel[4:7]

    for a in range(LATS):
        ahs[0, a] = pltpu.roll(x32[a, 0:8, :], 2, 0)
        ahs[1, a] = pltpu.roll(x32[a, 80:96, :], 6, 0)[8:16]

    l_gain.wait()
    gx[...] = jnp.zeros(gx.shape, F32)
    for a in range(LATS):
        for q in range(OWN // 8):
            row = pl.multiple_of(lax.rem(OWN * (me + a) + 8 * q, 128), 8)
            gx[:, pl.ds(row, 8), 0:WAVES] = gv[:, 8 * q : 8 * q + 8, :] * (2.0 / LON)
    l_deal.wait()
    for part in range(2):
        g = gx[part]
        high = g.astype(BF16)
        low = (g - high.astype(F32)).astype(BF16)
        both = dot_nt(dl[...], jnp.concatenate([high, low], axis=0))
        gt[part] = both[:, :128] + both[:, 128:]

    l_force.wait()
    l_kernel.wait()
    kp[...] = jnp.zeros(kp.shape, F32)
    kp[:, 0:KS, 0:HO] = kv[...]
    f32_force = fp[...].astype(F32)
    wst[...] = jnp.zeros(wst.shape, BF16)
    fpc[...] = jnp.zeros(fpc.shape, BF16)
    for dj in range(KS):
        for di in range(KS):
            at = 128 * dj + FIELDS * di
            wst[at : at + FIELDS, 0:HO] = (f32_force * kp[di, dj : dj + 1, 0:HO]).astype(BF16)
    fpc[FIELDS * RIM : FIELDS * RIM + FIELDS, 0:HO] = fp[...]

    l_flux.wait()
    r, f = iota((512, FIELDS), 0), iota((512, FIELDS), 1)
    spread = one_hot((r % 64 // 16 == r // 128) & (r % 16 == f))
    fxt[...] = dot(spread, fpt[...]).astype(BF16)
    l_surf.wait()
    r, f = iota((768, FIELDS), 0), iota((768, FIELDS), 1)
    spread = one_hot((r % 128 // 16 == r // 128) & (r % 16 == f))
    sxt[...] = dot(spread, spt[...]).astype(BF16)
    l_land.wait()
    lmp[...] = jnp.zeros(lmp.shape, F32)
    lmp[0:ROWS, 0:LOCAL] = lm[...].astype(F32)

    for c in oh:
        c.wait()
    sub = iota((8, HP), 0)
    for i in range(ROWS):
        tile = oc[RIM + i, 88:96, :]
        oc[RIM + i, 88:96, :] = jnp.where(
            sub < 2, tile, jnp.where(sub < 5, ohr[0, i], ohr[1, i])
        )
    obs[...] = oc[RIM : RIM + ROWS].astype(BF16)
    ob = []
    for side, k in ((1, -1), (0, 1)):
        src = obs.at[pl.ds(RIM * (1 - side), RIM)]
        c = remote(src, obr.at[side], obss.at[side], obrs.at[side], {"band": band_at(k)})
        c.start()
        ob.append(c)

    for c in small:
        c.wait()
    up_ok = jnp.where(band > 0, 1.0, 0.0).astype(F32)
    down_ok = jnp.where(band < bands - 1, 1.0, 0.0).astype(F32)
    blocks = []
    for b in range(3):
        chosen = selr[0, b]
        for o in range(1, 6):
            chosen = chosen + pltpu.roll(selr[o, b], 16 * o, 1)
        if b == 0:
            blocks.append(wr[0] * chosen * up_ok)
        elif b == 1:
            blocks.append(pltpu.roll(wown[...], 16, 1) * chosen)
        else:
            blocks.append(pltpu.roll(wr[1], 32, 1) * chosen * down_ok)
    slots = jnp.concatenate(blocks, axis=0).astype(BF16)
    r, c_ = iota((384, 128), 0), iota((384, 128), 1)
    by_row = dot_nt(one_hot(r // 16 == c_ // 4), slots).astype(BF16)
    r, c_ = iota((24, 768), 0), iota((24, 768), 1)
    tap = c_ % 128 // 16
    need = c_ // 128 + tap
    has = r % 8 + jnp.where(r < 8, -RIM, jnp.where(r < 16, RIM, RIM + ROWS))
    legal = (
        (tap < KS)
        & ((r >= 8) | (r % 8 >= ROWS - RIM))
        & (r % 8 < ROWS)
        & ((r < 16) | (r % 8 < RIM))
    )
    spread = one_hot(legal & (need == has))
    r, c_ = iota((384, 768), 0), iota((384, 768), 1)
    biga[...] = jnp.where(r % 16 == c_ % 16, dot(by_row, spread), 0.0).astype(BF16)
    r, c_ = iota((128, 24), 0), iota((128, 24), 1)
    by_own = dot(one_hot((c_ - 8 == r // 16) & (r // 16 < ROWS)), slots).astype(BF16)
    r, c_ = iota((256, 128), 0), iota((256, 128), 1)
    full = dot_nt(one_hot(c_ // 4 == 4 * (r // 64 + 1) + r % 64 // 16), by_own)
    bigb[...] = jnp.where(r % 16 == c_ % 16, full, 0.0).astype(BF16)

    l_tf.wait()
    for c in a1:
        c.wait_recv()
    ah = []
    for side, k in ((0, -1), (1, 1)):
        c = remote(ahs.at[side], ahr.at[side], ahss.at[side], ahrs.at[side], {"col": col_at(k)})
        c.start()
        ah.append(c)
    first = recv1[0:BLOCKS].reshape(TAB, 128).astype(F32)
    second = recv1[BLOCKS : 2 * BLOCKS].reshape(TAB, 128).astype(F32)
    waves = []
    for parity in range(2):
        mix = first - second if parity else first + second
        spec = dot(tf[parity], mix.astype(BF16))
        real, imag = spec[:WPAD], spec[WPAD:]
        rows = slice(parity * WPAD, parity * WPAD + WPAD)
        g_real, g_imag = gt[0, rows], gt[1, rows]
        waves.append(
            jnp.concatenate(
                [g_real * real + g_imag * imag, g_real * imag - g_imag * real], axis=0
            ).astype(BF16)
        )
    l_ti.wait()
    chunk = 2
    parts = BLOCKS // chunk
    for k in range(parts):
        q = lax.rem(me // chunk + k, parts)
        rows = pl.ds(pl.multiple_of(q * (chunk * PAD), chunk * PAD), chunk * PAD)
        even = dot(ti[0, rows, :], waves[0])
        odd = dot(ti[1, rows, :], waves[1])
        send2[pl.ds(q * chunk, chunk)] = (even + odd).astype(BF16).reshape(chunk, PAD, 128)
        send2[pl.ds(q * chunk + BLOCKS, chunk)] = (
            (even - odd).astype(BF16).reshape(chunk, PAD, 128)
        )
        for n in range(2 * chunk):
            to = q * chunk + n % chunk + BLOCKS * (n // chunk)
            step = lax.rem(to - me + cols, cols)

            @pl.when(to != me)
            def _():
                remote(
                    send2.at[to], recv2.at[me], a2s.at[step], a2r.at[step], {"col": to}
                ).start()

    recv2[me] = send2[me]

    for c in ob:
        c.wait()
    oc[0:RIM] = obr[0].astype(F32) * up_ok
    oc[RIM + ROWS :] = obr[1].astype(F32) * down_ok

    def stencil_row(i, carry):
        for t in range(HP // 128):
            cut = slice(128 * t, 128 * t + 128)
            total = None
            for dj in range(KS):
                line = None
                for di in range(KS):
                    term = kp[di, dj : dj + 1, cut] * oc[i + di, :, cut]
                    line = term if line is None else line + term
                shift = (RIM - dj) % PAD
                line = pltpu.roll(line, shift, 0) if shift else line
                total = line if total is None else total + line
            s0[i, :, cut] = total
        return carry

    lax.fori_loop(0, ROWS, stencil_row, 0)

    for c in ah:
        c.wait()
    sub = iota((8, CH), 0)
    for a in range(LATS):
        tile = x32[a, 88:96, :]
        x32[a, 88:96, :] = jnp.where(sub < 2, tile, jnp.where(sub < 5, ahr[0, a], ahr[1, a]))
    for k in range(1, cols):
        remote(send2.at[0], recv2.at[0], a2s.at[k], a2r.at[k], {"col": col_at(k)}).wait_recv()
    for a in range(LATS):
        for t in range(3):
            cut = slice(128 * t, 128 * t + 128)
            zonal = jnp.zeros((PAD, 128), F32)
            for d, lo, n in windows(t):
                mask = ((lane - (lo + OWN * a)) & 127) < n
                zonal = jnp.where(mask, recv2[d].astype(F32), zonal)
            if a:
                zonal = pltpu.roll(zonal, 128 - OWN * a, 1)
            mx[a * PAD : a * PAD + PAD, cut] = x32[a, :, cut] + zonal
    mixed = mx[...]
    centred = mixed - jnp.mean(mixed, axis=-1, keepdims=True)
    spread = jnp.mean(centred * centred, axis=-1, keepdims=True)
    normed = (centred * lax.rsqrt(spread + 1e-05)).astype(BF16)
    l_w1.wait()
    l_w2.wait()
    inner = jax.nn.gelu(dot(normed, w1[...])).astype(BF16)
    nx[...] = (mx[...] + dot(inner, w2[...])).astype(BF16)
    flux = None
    for a in range(LATS):
        term = dot_nt(nx[a * PAD : a * PAD + PAD, :], fxt[128 * a : 128 * a + 128, :])
        flux = term if flux is None else flux + term
    flx[...] = flux.astype(BF16)
    fl = []
    for o in (0, 2, 3, 4, 5):
        c = remote(flx, flr.at[o], fls.at[o], flrs.at[o], {"band": band_at(1 - o)})
        c.start()
        fl.append(c)
    flr[1] = flx[...]

    for t in range(3):
        cut = slice(128 * t, 128 * t + 128)
        for a in range(LATS):
            part = nx[a * PAD : a * PAD + PAD, cut].astype(F32)
            st.at[t][pl.ds(a, PAD, stride=LATS), :] = part
        for l in range(LOCAL):
            ao[l, :, cut] = st[t, LATS * l : LATS * l + LATS, :].astype(BF16)
    o_atm = pltpu.make_async_copy(ao, atm_out, out_sem.at[0])
    o_atm.start()

    r, c_ = iota((128, 128), 0), iota((128, 128), 1)
    sea = dot_nt(one_hot(r == c_), lmp[...].astype(BF16))
    l_oin.wait()
    l_oot.wait()
    for c in fl:
        c.wait()
    low = iota((PAD, 128), 1) < 64
    tiles = [
        jnp.where(low, flr[2 * q].astype(F32), flr[2 * q + 1].astype(F32)).astype(BF16)
        for q in range(3)
    ]
    forcing = dot(jnp.concatenate(tiles, axis=1), biga[...])
    for i in range(ROWS):
        part = forcing[:, 128 * i : 128 * i + 128]
        for dj in range(KS):
            shift = (RIM - dj) % PAD
            turned = pltpu.roll(part, shift, 0) if shift else part
            xs[PAD * i : PAD * i + PAD, 128 * dj : 128 * dj + 128] = turned.astype(BF16)
    rows = ROWS * PAD
    stencil = (dot(xs[...], wst[...]) + s0[...].reshape(rows, HP))[:, :HO]
    centred = stencil - jnp.mean(stencil, axis=-1, keepdims=True)
    spread = jnp.mean(centred * centred, axis=-1, keepdims=True)
    onorm = (centred * lax.rsqrt(spread + 1e-05)).astype(BF16)
    hidden = jax.nn.gelu(dot(onorm, oin[...])).astype(BF16)
    change = dot_nt(hidden, oot[...])
    pushed = dot(xs[:, 128 * RIM : 128 * RIM + 128], fpc[...])
    lifted = (oc[RIM : RIM + ROWS].reshape(rows, HP) + pushed)[:, :HO].astype(BF16).astype(F32)
    result = lifted + change
    surface = None
    for i in range(ROWS):
        part = (result[PAD * i : PAD * i + PAD] * sea[0:PAD, i : i + 1]).astype(BF16)
        oo[i] = part[:LOCAL]
        term = dot_nt(part, sxt[128 * i : 128 * i + 128, :])
        surface = term if surface is None else surface + term
    back = dot_nt(bigb[...], surface.astype(BF16)).astype(BF16)
    for o in range(SPAN):
        bks[o] = back[64 * o : 64 * o + 64]
    bk = []
    for o in range(1, SPAN):
        c = remote(bks.at[o], bkr.at[o], bss.at[o], brs.at[o], {"band": band_at(o)})
        c.start()
        bk.append(c)
    o_ocean = pltpu.make_async_copy(oo, ocean_out, out_sem.at[1])
    o_ocean.start()
    total = bks[0].astype(F32)
    for c in bk:
        c.wait()
    for o in range(1, SPAN):
        total = total + bkr[o].astype(F32)
    so[...] = total.reshape(LATS, FIELDS, PAD)[:, :, :LOCAL].astype(BF16)
    o_surf = pltpu.make_async_copy(so, surf_out, out_sem.at[2])
    o_surf.start()
    for c in a1:
        c.wait_send()
    for k in range(1, cols):
        remote(send2.at[0], recv2.at[0], a2s.at[k], a2r.at[k], {"col": col_at(k)}).wait_send()
    o_atm.wait()
    o_ocean.wait()
    o_surf.wait()


def per_device(
    bands,
    cols,
    consts,
    atm_state,
    spec_gain,
    mlp_in,
    mlp_out,
    flux_proj,
    pair_rows,
    pair_count,
    pair_weight,
    ocean_state,
    force_proj,
    depth_kernel,
    ocean_in,
    ocean_out,
    surf_proj,
    land_mask,
):
    any_spec = pl.BlockSpec(memory_space=ANY)
    smem = pl.BlockSpec(memory_space=pltpu.SMEM)
    vm = pltpu.VMEM
    dma = pltpu.SemaphoreType.DMA
    scratch = [
        vm((LOCAL, LATS, CH), BF16),
        vm((3, LATS * PAD, 128), F32),
        vm((LATS, PAD, CH), F32),
        vm((LATS, 3, PAD, 128), F32),
        vm((16, PAD, 128), BF16),
        vm((16, PAD, 128), BF16),
        vm((16, PAD, 128), BF16),
        vm((16, PAD, 128), BF16),
        vm((2, TAB, TAB), BF16),
        vm((2, TAB, TAB), BF16),
        vm((TAB, TAB), BF16),
        vm((2, OWN, WAVES), F32),
        vm((2, 128, TAB), F32),
        vm((2, TAB, 128), F32),
        vm((CH, 768), BF16),
        vm((768, CH), BF16),
        vm((FIELDS, CH), BF16),
        vm((ROWS, LOCAL, HO), BF16),
        vm((ROWS + 2 * RIM, PAD, HP), F32),
        vm((ROWS, PAD, HP), BF16),
        vm((2, RIM, PAD, HP), BF16),
        vm((2, ROWS, 8, HP), F32),
        vm((2, ROWS, 8, HP), F32),
        vm((2, LATS, 8, CH), F32),
        vm((2, LATS, 8, CH), F32),
        vm((8, 8, 128), F32),
        vm((6, 3, 8, 128), F32),
        vm((8, 128), F32),
        vm((2, 8, 128), F32),
        vm((KS, KS, HO), F32),
        vm((KS, 8, HP), F32),
        vm((FIELDS, HO), BF16),
        vm((128, HP), BF16),
        vm((HO, 800), BF16),
        vm((HO, 800), BF16),
        vm((FIELDS, HO), BF16),
        vm((ROWS, LOCAL), jnp.int32),
        vm((8, 128), F32),
        vm((ROWS, PAD, HP), F32),
        vm((384, 768), BF16),
        vm((256, 128), BF16),
        vm((KS * 128, HP), BF16),
        vm((ROWS * PAD, KS * 128), BF16),
        vm((512, CH), BF16),
        vm((768, HO), BF16),
        vm((LATS * PAD, CH), F32),
        vm((LATS * PAD, CH), BF16),
        vm((PAD, 128), BF16),
        vm((6, PAD, 128), BF16),
        vm((SPAN, 64, PAD), BF16),
        vm((SPAN, 64, PAD), BF16),
        vm((LOCAL, LATS, CH), BF16),
        vm((ROWS, LOCAL, HO), BF16),
        vm((LATS, FIELDS, LOCAL), BF16),
        dma((15,)),
        dma((3,)),
        dma((16,)),
        dma((16,)),
        dma((16,)),
        dma((16,)),
        dma((6,)),
        dma((6,)),
        dma((2,)),
        dma((2,)),
        dma((2,)),
        dma((2,)),
        dma((2,)),
        dma((2,)),
        dma((2,)),
        dma((2,)),
        dma((6,)),
        dma((6,)),
        dma((4,)),
        dma((4,)),
    ]
    out = pl.pallas_call(
        functools.partial(body, bands, cols),
        out_shape=(
            jax.ShapeDtypeStruct((LOCAL, LATS, CH), BF16),
            jax.ShapeDtypeStruct((ROWS, LOCAL, HO), BF16),
            jax.ShapeDtypeStruct((LATS, FIELDS, LOCAL), BF16),
        ),
        in_specs=[any_spec] * 5 + [smem] * 3 + [any_spec] * 10,
        out_specs=(any_spec,) * 3,
        scratch_shapes=scratch,
        compiler_params=pltpu.CompilerParams(
            collective_id=0, has_side_effects=True, vmem_limit_bytes=56 * 1024 * 1024
        ),
    )(
        jnp.transpose(atm_state, (1, 0, 2)),
        jnp.transpose(spec_gain, (0, 2, 1)),
        mlp_in,
        mlp_out,
        jnp.transpose(flux_proj),
        jnp.transpose(pair_rows, (1, 2, 0)),
        jnp.transpose(pair_count),
        jnp.transpose(pair_weight, (0, 2, 1)),
        ocean_state,
        force_proj,
        depth_kernel,
        ocean_in,
        jnp.transpose(ocean_out),
        jnp.transpose(surf_proj),
        land_mask,
        *consts,
    )
    return (
        jnp.transpose(out[0], (1, 0, 2)),
        out[1],
        jnp.transpose(out[2], (0, 2, 1)),
    )


def solution(mesh):
    placed = (
        P("band", "col", None),
        P(None, None, "col"),
        P(),
        P(),
        P(),
        P(None, "band", None),
        P(None, "band"),
        P("band", None, None),
        P("band", "col", None),
        P(),
        P(),
        P(),
        P(),
        P(),
        P("band", "col"),
    )
    consts = tables()
    step = functools.partial(
        per_device, mesh.shape["band"], mesh.shape["col"], [jnp.asarray(t) for t in consts]
    )
    return jax.shard_map(
        step,
        mesh=mesh,
        in_specs=placed,
        out_specs=(P("band", "col", None), P("band", "col", None), P("band", "col", None)),
        check_vma=False,
    )
```

```python
import functools

import jax
import jax.numpy as jnp
import numpy as np
from jax import lax
from jax.experimental import pallas as pl
from jax.experimental.pallas import tpu as pltpu
from jax.sharding import PartitionSpec as P

F32 = jnp.float32
BF16 = jnp.bfloat16
MESH = pl.DeviceIdType.MESH
ANY = pl.ANY

SPAN = 4
LATS = 4
SLOTS = 4
LON = 1440
WAVES = 720
LOCAL = 90
PAD = 96
RIM = 3
KS = 7
CH = 384
OWN = 24
HALF = LON // 2
BLOCKS = 8
TAB = BLOCKS * PAD
WPAD = TAB // 2
ROWS = 6
HO = 200
HP = 256
FIELDS = 16
NT = (((1,), (1,)), ((), ()))


def tables():
    place = np.arange(PAD)
    block = np.arange(BLOCKS)
    inside = np.broadcast_to(place < LOCAL, (BLOCKS, PAD)).reshape(-1)
    lon_in = (LOCAL * block[:, None] + place[None]).reshape(-1)
    rim = np.where(place < LOCAL + RIM, place, place - PAD)
    lon_out = (LOCAL * block[:, None] + rim[None]).reshape(-1)
    forward = np.zeros((2, TAB, TAB), np.float64)
    inverse = np.zeros((2, TAB, TAB), np.float64)
    deal = np.zeros((2 * WPAD, TAB), np.float64)
    count = WAVES // 2
    for parity in range(2):
        wave = 2 * np.arange(count) + parity
        angle = 2 * np.pi * (wave[:, None] * lon_in[None] % LON) / LON
        forward[parity, :count] = np.cos(angle) * inside
        forward[parity, WPAD : WPAD + count] = np.sin(angle) * inside
        angle = 2 * np.pi * (lon_out[:, None] * wave[None] % LON) / LON
        inverse[parity, :, :count] = np.cos(angle)
        inverse[parity, :, WPAD : WPAD + count] = np.sin(angle)
        deal[parity * WPAD + np.arange(count), wave] = 1.0
    return [t.astype(np.float32).astype(jnp.bfloat16) for t in (forward, inverse, deal)]


def iota(shape, axis):
    return lax.broadcasted_iota(jnp.int32, shape, axis)


def one_hot(condition):
    return jnp.where(condition, 1.0, 0.0).astype(BF16)


def dot(a, b):
    return jnp.dot(a, b, preferred_element_type=F32)


def dot_nt(a, b):
    return lax.dot_general(a, b, NT, preferred_element_type=F32)


def windows(tile):
    out = []
    for d in range(16):
        lo, hi = max(OWN * d, 128 * tile), min(OWN * d + OWN, 128 * tile + 128)
        if lo < hi:
            out.append((d, lo, hi - lo))
    return out


def body(
    bands,
    cols,
    atm,
    gain,
    w_in,
    w_out,
    flux_t,
    p_rows,
    p_count,
    p_weight,
    ocean,
    force,
    kernel_w,
    o_in,
    o_out_t,
    surf_t,
    land,
    tab_f,
    tab_i,
    deal,
    ao,
    oo,
    so,
    xv,
    st,
    x32,
    rolled,
    send1,
    recv1,
    send2,
    recv2,
    tf,
    ti,
    dl,
    gv,
    gx,
    gt,
    w1,
    w2,
    fpt,
    ocv,
    oc,
    obs,
    obr,
    ohs,
    ohr,
    ahs,
    ahr,
    sel,
    selr,
    wown,
    wr,
    kv,
    kp,
    fp,
    fpc,
    oin,
    oot,
    spt,
    lm,
    lmp,
    s0,
    biga,
    bigb,
    wst,
    xs,
    fxt,
    sxt,
    mx,
    nx,
    flx,
    flr,
    bks,
    bkr,
    waves,
    ld,
    a1s,
    a1r,
    a2s,
    a2r,
    sls,
    slr,
    ws,
    wrs,
    ohss,
    ohrs,
    obss,
    obrs,
    ahss,
    ahrs,
    fls,
    flrs,
    bss,
    brs,
):
    me = lax.axis_index("col")
    band = lax.axis_index("band")
    up_ok = jnp.where(band > 0, 1.0, 0.0).astype(F32)
    down_ok = jnp.where(band < bands - 1, 1.0, 0.0).astype(F32)

    def col_at(k):
        return lax.rem(me + k + cols, cols)

    def exists(k):
        return band >= -k if k < 0 else band < bands - k

    def load(src, dst, k):
        c = pltpu.make_async_copy(src, dst, ld.at[k])
        c.start()
        return c

    l_atm = load(atm, xv, 0)
    l_ocean = load(ocean, ocv, 1)
    l_force = load(force, fp, 2)
    l_kernel = load(kernel_w, kv, 3)
    l_gain = load(gain, gv, 4)
    l_deal = load(deal, dl, 5)
    l_tf = load(tab_f, tf, 6)
    l_flux = load(flux_t, fpt, 7)
    l_surf = load(surf_t, spt, 8)
    l_land = load(land, lm, 9)
    l_ti = load(tab_i, ti, 10)
    l_w1 = load(w_in, w1, 11)
    l_w2 = load(w_out, w2, 12)
    l_oin = load(o_in, oin, 13)
    l_oot = load(o_out_t, oot, 14)

    barrier = pltpu.get_barrier_semaphore()
    for k in range(1, cols):
        pl.semaphore_signal(barrier, inc=1, device_id={"col": col_at(k)}, device_id_type=MESH)
    for k in range(1, SPAN + 1):

        @pl.when(exists(k))
        def _():
            pl.semaphore_signal(barrier, inc=1, device_id={"band": band + k}, device_id_type=MESH)

    def remote(src, dst, send_sem, recv_sem, device):
        return pltpu.make_async_remote_copy(
            src_ref=src,
            dst_ref=dst,
            send_sem=send_sem,
            recv_sem=recv_sem,
            device_id=device,
            device_id_type=MESH,
        )

    def to_band(k, src, dst, send_sem, recv_sem):
        def make():
            return remote(src, dst, send_sem, recv_sem, {"band": band + k})

        def start():
            pl.when(exists(k))(lambda: make().start())

        def wait_send():
            pl.when(exists(k))(lambda: make().wait_send())

        def wait_recv():
            pl.when(exists(-k))(lambda: make().wait_recv())

        return start, wait_send, wait_recv

    def slots_to(o):
        return to_band(1 - o, sel.at[pl.ds(5 - o, 3)], selr.at[o], sls.at[o], slr.at[o])

    def weights_to(side):
        return to_band(1 - 2 * side, wown, wr.at[side], ws.at[side], wrs.at[side])

    def rim_to(side):
        src = obs.at[pl.ds(RIM * (1 - side), RIM)]
        return to_band(1 - 2 * side, src, obr.at[side], obss.at[side], obrs.at[side])

    def flux_to(o):
        return to_band(1 - o, flx, flr.at[o], fls.at[o], flrs.at[o])

    def back_to(o):
        return to_band(o, bks.at[o], bkr.at[o], bss.at[o], brs.at[o])

    lane = iota((PAD, 128), 1)

    def phase_pack():
        st[:, LATS * LOCAL :, :] = jnp.zeros((3, LATS * (PAD - LOCAL), 128), F32)
        for l in range(LOCAL):
            for t in range(3):
                cut = slice(128 * t, 128 * t + 128)
                st[t, LATS * l : LATS * l + LATS, :] = xv[l, :, cut].astype(F32)
        for a in range(LATS):
            for t in range(3):
                part = st.at[t][pl.ds(a, PAD, stride=LATS), :]
                x32[a, :, 128 * t : 128 * t + 128] = part
                rolled[a, t] = pltpu.roll(part, OWN * a, 1) if a else part
        for d in range(cols):
            out = jnp.zeros((PAD, 128), F32)
            for t in range(3):
                for e, lo, n in windows(t):
                    if e == d:
                        for a in range(LATS):
                            mask = ((lane - (lo + OWN * a)) & 127) < n
                            out = jnp.where(mask, rolled[a, t], out)
            send1[d] = out.astype(BF16)
        recv1[me] = send1[me]

    def phase_slots():
        row8 = iota((8, 128), 0)
        lane8 = iota((8, 128), 1)
        zero8 = jnp.zeros((8, 128), F32)
        for q in (0, 1, 6, 7):
            sel[q] = zero8
        for k in range(SPAN):
            other = band - k
            at = jnp.maximum(other, 0)
            used = jnp.where(other >= 0, p_count[0, at], 0)
            vec = zero8
            for p in range(SLOTS):
                target = jnp.where(p < used, SLOTS * p_rows[0, p, at] + p, -1)
                vec = jnp.where(lane8 == target, 1.0, vec)
            sel[5 - k] = vec
        vec = zero8
        for o in range(SPAN):
            at = jnp.minimum(band + o, bands - 1)
            for p in range(SLOTS):
                here = (lane8 // 16 == o) & (lane8 % SLOTS == p)
                for i in range(ROWS):
                    vec = jnp.where(here & (row8 == i), p_weight[i, p, at], vec)
        wown[...] = vec
        selr[1] = sel[4:7]
        for o in range(2, 6):

            @pl.when(jnp.logical_not(exists(o - 1)))
            def _():
                selr[o] = jnp.zeros((3, 8, 128), F32)
                flr[o] = jnp.zeros((PAD, 128), BF16)

        @pl.when(jnp.logical_not(exists(-1)))
        def _():
            selr[0] = jnp.zeros((3, 8, 128), F32)
            flr[0] = jnp.zeros((PAD, 128), BF16)
            wr[0] = zero8
            obr[0] = jnp.zeros((RIM, PAD, HP), BF16)

        @pl.when(jnp.logical_not(exists(1)))
        def _():
            wr[1] = zero8
            obr[1] = jnp.zeros((RIM, PAD, HP), BF16)

        for o in range(1, SPAN):

            @pl.when(jnp.logical_not(exists(-o)))
            def _():
                bkr[o] = jnp.zeros((64, PAD), BF16)

    def phase_rims():
        oc[RIM : RIM + ROWS] = jnp.zeros((ROWS, PAD, HP), F32)
        oc[RIM : RIM + ROWS, 0:LOCAL, 0:HO] = ocv[...].astype(F32)
        for i in range(ROWS):
            ohs[0, i] = pltpu.roll(oc[RIM + i, 0:8, :], 2, 0)
            ohs[1, i] = pltpu.roll(oc[RIM + i, 80:96, :], 6, 0)[8:16]
        for a in range(LATS):
            ahs[0, a] = pltpu.roll(x32[a, 0:8, :], 2, 0)
            ahs[1, a] = pltpu.roll(x32[a, 80:96, :], 6, 0)[8:16]

    def phase_gains():
        gx[...] = jnp.zeros(gx.shape, F32)
        for a in range(LATS):
            for q in range(OWN // 8):
                row = pl.multiple_of(lax.rem(OWN * (me + a) + 8 * q, 128), 8)
                gx[:, pl.ds(row, 8), 0:WAVES] = gv[:, 8 * q : 8 * q + 8, :] * (2.0 / LON)
        for part in range(2):
            g = gx[part]
            high = g.astype(BF16)
            low = (g - high.astype(F32)).astype(BF16)
            both = dot_nt(dl[...], jnp.concatenate([high, low], axis=0))
            gt[part] = both[:, :128] + both[:, 128:]

    def phase_weights():
        kp[...] = jnp.zeros(kp.shape, F32)
        kp[:, 0:KS, 0:HO] = kv[...]
        f32_force = fp[...].astype(F32)
        wst[...] = jnp.zeros(wst.shape, BF16)
        fpc[...] = jnp.zeros(fpc.shape, BF16)
        for dj in range(KS):
            for di in range(KS):
                at = 128 * dj + FIELDS * di
                wst[at : at + FIELDS, 0:HO] = (f32_force * kp[di, dj : dj + 1, 0:HO]).astype(BF16)
        fpc[FIELDS * RIM : FIELDS * RIM + FIELDS, 0:HO] = fp[...]

        r, f = iota((512, FIELDS), 0), iota((512, FIELDS), 1)
        spread = one_hot((r % 64 // 16 == r // 128) & (r % 16 == f))
        fxt[...] = dot(spread, fpt[...]).astype(BF16)
        r, f = iota((768, FIELDS), 0), iota((768, FIELDS), 1)
        spread = one_hot((r % 128 // 16 == r // 128) & (r % 16 == f))
        sxt[...] = dot(spread, spt[...]).astype(BF16)
        lmp[...] = jnp.zeros(lmp.shape, F32)
        lmp[0:ROWS, 0:LOCAL] = lm[...].astype(F32)

    def phase_ocean_rim():
        sub = iota((8, HP), 0)
        for i in range(ROWS):
            tile = oc[RIM + i, 88:96, :]
            oc[RIM + i, 88:96, :] = jnp.where(
                sub < 2, tile, jnp.where(sub < 5, ohr[0, i], ohr[1, i])
            )
        obs[...] = oc[RIM : RIM + ROWS].astype(BF16)

    def phase_matrices():
        blocks = []
        for b in range(3):
            chosen = selr[0, b]
            for o in range(1, 6):
                chosen = chosen + pltpu.roll(selr[o, b], 16 * o, 1)
            if b == 0:
                blocks.append(wr[0] * chosen * up_ok)
            elif b == 1:
                blocks.append(pltpu.roll(wown[...], 16, 1) * chosen)
            else:
                blocks.append(pltpu.roll(wr[1], 32, 1) * chosen * down_ok)
        slots = jnp.concatenate(blocks, axis=0).astype(BF16)
        r, c_ = iota((384, 128), 0), iota((384, 128), 1)
        by_row = dot_nt(one_hot(r // 16 == c_ // 4), slots).astype(BF16)
        r, c_ = iota((24, 768), 0), iota((24, 768), 1)
        tap = c_ % 128 // 16
        need = c_ // 128 + tap
        has = r % 8 + jnp.where(r < 8, -RIM, jnp.where(r < 16, RIM, RIM + ROWS))
        legal = (
            (tap < KS)
            & ((r >= 8) | (r % 8 >= ROWS - RIM))
            & (r % 8 < ROWS)
            & ((r < 16) | (r % 8 < RIM))
        )
        spread = one_hot(legal & (need == has))
        r, c_ = iota((384, 768), 0), iota((384, 768), 1)
        biga[...] = jnp.where(r % 16 == c_ % 16, dot(by_row, spread), 0.0).astype(BF16)
        r, c_ = iota((128, 24), 0), iota((128, 24), 1)
        by_own = dot(one_hot((c_ - 8 == r // 16) & (r // 16 < ROWS)), slots).astype(BF16)
        r, c_ = iota((256, 128), 0), iota((256, 128), 1)
        full = dot_nt(one_hot(c_ // 4 == 4 * (r // 64 + 1) + r % 64 // 16), by_own)
        bigb[...] = jnp.where(r % 16 == c_ % 16, full, 0.0).astype(BF16)

    def phase_spectra():
        first = recv1[0:BLOCKS].reshape(TAB, 128).astype(F32)
        second = recv1[BLOCKS : 2 * BLOCKS].reshape(TAB, 128).astype(F32)
        for parity in range(2):
            mix = first - second if parity else first + second
            spec = dot(tf[parity], mix.astype(BF16))
            real, imag = spec[:WPAD], spec[WPAD:]
            rows = slice(parity * WPAD, parity * WPAD + WPAD)
            g_real, g_imag = gt[0, rows], gt[1, rows]
            waves[parity, :WPAD] = (g_real * real + g_imag * imag).astype(BF16)
            waves[parity, WPAD:] = (g_real * imag - g_imag * real).astype(BF16)

    chunk = 2

    def phase_inverse(k):
        parts = BLOCKS // chunk
        q = lax.rem(me // chunk + k, parts)
        rows = pl.ds(pl.multiple_of(q * (chunk * PAD), chunk * PAD), chunk * PAD)
        even = dot(ti[0, rows, :], waves[0])
        odd = dot(ti[1, rows, :], waves[1])
        send2[pl.ds(q * chunk, chunk)] = (even + odd).astype(BF16).reshape(chunk, PAD, 128)
        send2[pl.ds(q * chunk + BLOCKS, chunk)] = (
            (even - odd).astype(BF16).reshape(chunk, PAD, 128)
        )
        return q

    def phase_stencil():
        oc[0:RIM] = obr[0].astype(F32) * up_ok
        oc[RIM + ROWS :] = obr[1].astype(F32) * down_ok

        def stencil_row(i, carry):
            for t in range(HP // 128):
                cut = slice(128 * t, 128 * t + 128)
                total = None
                for dj in range(KS):
                    line = None
                    for di in range(KS):
                        term = kp[di, dj : dj + 1, cut] * oc[i + di, :, cut]
                        line = term if line is None else line + term
                    shift = (RIM - dj) % PAD
                    line = pltpu.roll(line, shift, 0) if shift else line
                    total = line if total is None else total + line
                s0[i, :, cut] = total
            return carry

        lax.fori_loop(0, ROWS, stencil_row, 0)

    def phase_atm_rim():
        sub = iota((8, CH), 0)
        for a in range(LATS):
            tile = x32[a, 88:96, :]
            x32[a, 88:96, :] = jnp.where(sub < 2, tile, jnp.where(sub < 5, ahr[0, a], ahr[1, a]))

    def phase_unpack():
        for a in range(LATS):
            for t in range(3):
                cut = slice(128 * t, 128 * t + 128)
                zonal = jnp.zeros((PAD, 128), F32)
                for d, lo, n in windows(t):
                    mask = ((lane - (lo + OWN * a)) & 127) < n
                    zonal = jnp.where(mask, recv2[d].astype(F32), zonal)
                if a:
                    zonal = pltpu.roll(zonal, 128 - OWN * a, 1)
                mx[a * PAD : a * PAD + PAD, cut] = x32[a, :, cut] + zonal

    def phase_atm():
        mixed = mx[...]
        centred = mixed - jnp.mean(mixed, axis=-1, keepdims=True)
        spread = jnp.mean(centred * centred, axis=-1, keepdims=True)
        normed = (centred * lax.rsqrt(spread + 1e-05)).astype(BF16)
        inner = jax.nn.gelu(dot(normed, w1[...])).astype(BF16)
        nx[...] = (mx[...] + dot(inner, w2[...])).astype(BF16)
        flux = None
        for a in range(LATS):
            term = dot_nt(nx[a * PAD : a * PAD + PAD, :], fxt[128 * a : 128 * a + 128, :])
            flux = term if flux is None else flux + term
        flx[...] = flux.astype(BF16)
        flr[1] = flx[...]

    def phase_atm_out():
        for t in range(3):
            cut = slice(128 * t, 128 * t + 128)
            for a in range(LATS):
                part = nx[a * PAD : a * PAD + PAD, cut].astype(F32)
                st.at[t][pl.ds(a, PAD, stride=LATS), :] = part
            for l in range(LOCAL):
                ao[l, :, cut] = st[t, LATS * l : LATS * l + LATS, :].astype(BF16)

    def phase_forcing():
        low = iota((PAD, 128), 1) < 64
        tiles = [
            jnp.where(low, flr[2 * q].astype(F32), flr[2 * q + 1].astype(F32)).astype(BF16)
            for q in range(3)
        ]
        forcing = dot(jnp.concatenate(tiles, axis=1), biga[...])
        for i in range(ROWS):
            part = forcing[:, 128 * i : 128 * i + 128]
            for dj in range(KS):
                shift = (RIM - dj) % PAD
                turned = pltpu.roll(part, shift, 0) if shift else part
                xs[PAD * i : PAD * i + PAD, 128 * dj : 128 * dj + 128] = turned.astype(BF16)

    def phase_ocean():
        r, c_ = iota((128, 128), 0), iota((128, 128), 1)
        sea = dot_nt(one_hot(r == c_), lmp[...].astype(BF16))
        rows = ROWS * PAD
        stencil = (dot(xs[...], wst[...]) + s0[...].reshape(rows, HP))[:, :HO]
        centred = stencil - jnp.mean(stencil, axis=-1, keepdims=True)
        spread = jnp.mean(centred * centred, axis=-1, keepdims=True)
        onorm = (centred * lax.rsqrt(spread + 1e-05)).astype(BF16)
        hidden = jax.nn.gelu(dot(onorm, oin[...])).astype(BF16)
        change = dot_nt(hidden, oot[...])
        pushed = dot(xs[:, 128 * RIM : 128 * RIM + 128], fpc[...])
        lifted = (oc[RIM : RIM + ROWS].reshape(rows, HP) + pushed)[:, :HO].astype(BF16).astype(F32)
        result = lifted + change
        surface = None
        for i in range(ROWS):
            part = (result[PAD * i : PAD * i + PAD] * sea[0:PAD, i : i + 1]).astype(BF16)
            oo[i] = part[:LOCAL]
            term = dot_nt(part, sxt[128 * i : 128 * i + 128, :])
            surface = term if surface is None else surface + term
        back = dot_nt(bigb[...], surface.astype(BF16)).astype(BF16)
        for o in range(SPAN):
            bks[o] = back[64 * o : 64 * o + 64]

    def phase_sum():
        total = bks[0].astype(F32)
        for o in range(1, SPAN):
            total = total + bkr[o].astype(F32)
        so[...] = total.reshape(LATS, FIELDS, PAD)[:, :, :LOCAL].astype(BF16)

    l_atm.wait()
    phase_pack()
    phase_slots()
    pl.semaphore_wait(barrier, cols - 1 + jnp.minimum(band, SPAN))

    a1 = []
    for k in range(1, cols):
        d = col_at(k)
        c = remote(send1.at[d], recv1.at[me], a1s.at[k], a1r.at[k], {"col": d})
        c.start()
        a1.append(c)
    for o in range(2, 6):
        slots_to(o)[0]()
    weights_to(1)[0]()
    l_ocean.wait()
    phase_rims()
    oh = []
    for side, k in ((0, -1), (1, 1)):
        c = remote(ohs.at[side], ohr.at[side], ohss.at[side], ohrs.at[side], {"col": col_at(k)})
        c.start()
        oh.append(c)

    l_gain.wait()
    l_deal.wait()
    phase_gains()
    l_force.wait()
    l_kernel.wait()
    l_flux.wait()
    l_surf.wait()
    l_land.wait()
    phase_weights()

    for o in range(2, 6):
        slots_to(o)[2]()
    weights_to(1)[2]()
    slots_to(0)[0]()
    weights_to(0)[0]()
    for c in oh:
        c.wait()
    phase_ocean_rim()
    rim_to(0)[0]()
    rim_to(1)[0]()

    l_tf.wait()
    for c in a1:
        c.wait_recv()
    phase_spectra()
    ah = []
    for side, k in ((0, -1), (1, 1)):
        c = remote(ahs.at[side], ahr.at[side], ahss.at[side], ahrs.at[side], {"col": col_at(k)})
        c.start()
        ah.append(c)
    l_ti.wait()
    for k in range(BLOCKS // chunk):
        q = phase_inverse(k)
        for n in range(2 * chunk):
            to = q * chunk + n % chunk + BLOCKS * (n // chunk)
            step = lax.rem(to - me + cols, cols)

            @pl.when(to != me)
            def _():
                remote(
                    send2.at[to], recv2.at[me], a2s.at[step], a2r.at[step], {"col": to}
                ).start()

    recv2[me] = send2[me]

    slots_to(0)[2]()
    weights_to(0)[2]()
    phase_matrices()
    rim_to(0)[2]()
    rim_to(1)[2]()
    phase_stencil()

    for c in ah:
        c.wait()
    phase_atm_rim()
    for k in range(1, cols):
        remote(send2.at[0], recv2.at[0], a2s.at[k], a2r.at[k], {"col": col_at(k)}).wait_recv()
    phase_unpack()
    l_w1.wait()
    l_w2.wait()
    phase_atm()
    for o in (5, 4, 3, 2, 0):
        flux_to(o)[0]()
    phase_atm_out()

    l_oin.wait()
    l_oot.wait()
    for o in (0, 2, 3, 4, 5):
        flux_to(o)[2]()
    phase_forcing()
    phase_ocean()
    for o in range(1, SPAN):
        back_to(o)[0]()
    for o in range(1, SPAN):
        back_to(o)[2]()
    phase_sum()

    for c in a1:
        c.wait_send()
    for k in range(1, cols):
        remote(send2.at[0], recv2.at[0], a2s.at[k], a2r.at[k], {"col": col_at(k)}).wait_send()
    for o in (0, 2, 3, 4, 5):
        slots_to(o)[1]()
        flux_to(o)[1]()
    for side in range(2):
        weights_to(side)[1]()
        rim_to(side)[1]()
    for o in range(1, SPAN):
        back_to(o)[1]()


def store(a, b, c, a_out, b_out, c_out, sems):
    copies = [
        pltpu.make_async_copy(x, y, sems.at[k])
        for k, (x, y) in enumerate(((a, a_out), (b, b_out), (c, c_out)))
    ]
    for x in copies:
        x.start()
    for x in copies:
        x.wait()


def per_device(
    bands,
    cols,
    consts,
    atm_state,
    spec_gain,
    mlp_in,
    mlp_out,
    flux_proj,
    pair_rows,
    pair_count,
    pair_weight,
    ocean_state,
    force_proj,
    depth_kernel,
    ocean_in,
    ocean_out,
    surf_proj,
    land_mask,
):
    any_spec = pl.BlockSpec(memory_space=ANY)
    smem = pl.BlockSpec(memory_space=pltpu.SMEM)
    vm = pltpu.VMEM
    dma = pltpu.SemaphoreType.DMA
    scratch = [
        vm((LOCAL, LATS, CH), BF16),
        vm((3, LATS * PAD, 128), F32),
        vm((LATS, PAD, CH), F32),
        vm((LATS, 3, PAD, 128), F32),
        vm((16, PAD, 128), BF16),
        vm((16, PAD, 128), BF16),
        vm((16, PAD, 128), BF16),
        vm((16, PAD, 128), BF16),
        vm((2, TAB, TAB), BF16),
        vm((2, TAB, TAB), BF16),
        vm((TAB, TAB), BF16),
        vm((2, OWN, WAVES), F32),
        vm((2, 128, TAB), F32),
        vm((2, TAB, 128), F32),
        vm((CH, 768), BF16),
        vm((768, CH), BF16),
        vm((FIELDS, CH), BF16),
        vm((ROWS, LOCAL, HO), BF16),
        vm((ROWS + 2 * RIM, PAD, HP), F32),
        vm((ROWS, PAD, HP), BF16),
        vm((2, RIM, PAD, HP), BF16),
        vm((2, ROWS, 8, HP), F32),
        vm((2, ROWS, 8, HP), F32),
        vm((2, LATS, 8, CH), F32),
        vm((2, LATS, 8, CH), F32),
        vm((8, 8, 128), F32),
        vm((6, 3, 8, 128), F32),
        vm((8, 128), F32),
        vm((2, 8, 128), F32),
        vm((KS, KS, HO), F32),
        vm((KS, 8, HP), F32),
        vm((FIELDS, HO), BF16),
        vm((128, HP), BF16),
        vm((HO, 800), BF16),
        vm((HO, 800), BF16),
        vm((FIELDS, HO), BF16),
        vm((ROWS, LOCAL), jnp.int32),
        vm((8, 128), F32),
        vm((ROWS, PAD, HP), F32),
        vm((384, 768), BF16),
        vm((256, 128), BF16),
        vm((KS * 128, HP), BF16),
        vm((ROWS * PAD, KS * 128), BF16),
        vm((512, CH), BF16),
        vm((768, HO), BF16),
        vm((LATS * PAD, CH), F32),
        vm((LATS * PAD, CH), BF16),
        vm((PAD, 128), BF16),
        vm((6, PAD, 128), BF16),
        vm((SPAN, 64, PAD), BF16),
        vm((SPAN, 64, PAD), BF16),
        vm((2, TAB, 128), BF16),
        dma((15,)),
        dma((16,)),
        dma((16,)),
        dma((16,)),
        dma((16,)),
        dma((6,)),
        dma((6,)),
        dma((2,)),
        dma((2,)),
        dma((2,)),
        dma((2,)),
        dma((2,)),
        dma((2,)),
        dma((2,)),
        dma((2,)),
        dma((6,)),
        dma((6,)),
        dma((4,)),
        dma((4,)),
    ]
    shapes = (
        jax.ShapeDtypeStruct((LOCAL, LATS, CH), BF16),
        jax.ShapeDtypeStruct((ROWS, LOCAL, HO), BF16),
        jax.ShapeDtypeStruct((LATS, FIELDS, LOCAL), BF16),
    )
    out = pl.pallas_call(
        functools.partial(body, bands, cols),
        out_shape=tuple(vm(x.shape, x.dtype) for x in shapes),
        in_specs=[any_spec] * 5 + [smem] * 3 + [any_spec] * 10,
        out_specs=(pl.BlockSpec(memory_space=vm),) * 3,
        scratch_shapes=scratch,
        compiler_params=pltpu.CompilerParams(
            collective_id=0, has_side_effects=True, vmem_limit_bytes=56 * 1024 * 1024
        ),
    )(
        jnp.transpose(atm_state, (1, 0, 2)),
        jnp.transpose(spec_gain, (0, 2, 1)),
        mlp_in,
        mlp_out,
        jnp.transpose(flux_proj),
        jnp.transpose(pair_rows, (1, 2, 0)),
        jnp.transpose(pair_count),
        jnp.transpose(pair_weight, (0, 2, 1)),
        ocean_state,
        force_proj,
        depth_kernel,
        ocean_in,
        jnp.transpose(ocean_out),
        jnp.transpose(surf_proj),
        land_mask,
        *consts,
    )
    out = pl.pallas_call(
        store,
        out_shape=shapes,
        in_specs=[pl.BlockSpec(memory_space=vm)] * 3,
        out_specs=(any_spec,) * 3,
        scratch_shapes=[dma((3,))],
    )(*out)
    return (
        jnp.transpose(out[0], (1, 0, 2)),
        out[1],
        jnp.transpose(out[2], (0, 2, 1)),
    )


def solution(mesh):
    placed = (
        P("band", "col", None),
        P(None, None, "col"),
        P(),
        P(),
        P(),
        P(None, "band", None),
        P(None, "band"),
        P("band", None, None),
        P("band", "col", None),
        P(),
        P(),
        P(),
        P(),
        P(),
        P("band", "col"),
    )
    consts = tables()
    step = functools.partial(
        per_device, mesh.shape["band"], mesh.shape["col"], [jnp.asarray(t) for t in consts]
    )
    return jax.shard_map(
        step,
        mesh=mesh,
        in_specs=placed,
        out_specs=(P("band", "col", None), P("band", "col", None), P("band", "col", None)),
        check_vma=False,
    )
```

```python
import functools

import jax
import jax.numpy as jnp
import numpy as np
from jax import lax
from jax.experimental import pallas as pl
from jax.experimental.pallas import tpu as pltpu
from jax.sharding import PartitionSpec as P

F32 = jnp.float32
BF16 = jnp.bfloat16
MESH = pl.DeviceIdType.MESH
ANY = pl.ANY

SPAN = 4
LATS = 4
SLOTS = 4
LON = 1440
WAVES = 720
LOCAL = 90
PAD = 96
RIM = 3
KS = 7
CH = 384
OWN = 24
HALF = LON // 2
BLOCKS = 8
TAB = BLOCKS * PAD
WPAD = TAB // 2
ROWS = 6
HO = 200
HP = 256
FIELDS = 16
NT = (((1,), (1,)), ((), ()))


def tables():
    place = np.arange(PAD)
    block = np.arange(BLOCKS)
    inside = np.broadcast_to(place < LOCAL, (BLOCKS, PAD)).reshape(-1)
    lon_in = (LOCAL * block[:, None] + place[None]).reshape(-1)
    rim = np.where(place < LOCAL + RIM, place, place - PAD)
    lon_out = (LOCAL * block[:, None] + rim[None]).reshape(-1)
    forward = np.zeros((2, TAB, TAB), np.float64)
    inverse = np.zeros((2, TAB, TAB), np.float64)
    deal = np.zeros((2 * WPAD, TAB), np.float64)
    count = WAVES // 2
    for parity in range(2):
        wave = 2 * np.arange(count) + parity
        angle = 2 * np.pi * (wave[:, None] * lon_in[None] % LON) / LON
        forward[parity, :count] = np.cos(angle) * inside
        forward[parity, WPAD : WPAD + count] = np.sin(angle) * inside
        angle = 2 * np.pi * (lon_out[:, None] * wave[None] % LON) / LON
        inverse[parity, :, :count] = np.cos(angle)
        inverse[parity, :, WPAD : WPAD + count] = np.sin(angle)
        deal[parity * WPAD + np.arange(count), wave] = 1.0
    return [t.astype(np.float32).astype(jnp.bfloat16) for t in (forward, inverse, deal)]


def iota(shape, axis):
    return lax.broadcasted_iota(jnp.int32, shape, axis)


def one_hot(condition):
    return jnp.where(condition, 1.0, 0.0).astype(BF16)


def dot(a, b):
    return jnp.dot(a, b, preferred_element_type=F32)


def dot_nt(a, b):
    return lax.dot_general(a, b, NT, preferred_element_type=F32)


def windows(tile):
    out = []
    for d in range(16):
        lo, hi = max(OWN * d, 128 * tile), min(OWN * d + OWN, 128 * tile + 128)
        if lo < hi:
            out.append((d, lo, hi - lo))
    return out


def body(
    bands,
    cols,
    atm,
    gain,
    w_in,
    w_out,
    flux_t,
    pair_rows,
    pair_count,
    pair_weight,
    ocean,
    force,
    kernel_w,
    o_in,
    o_out_t,
    surf_t,
    land,
    tab_f,
    tab_i,
    deal,
    ao,
    oo,
    so,
    xv,
    st,
    x32,
    rolled,
    send1,
    recv1,
    send2,
    recv2,
    tf,
    ti,
    dl,
    gv,
    gx,
    gt,
    w1,
    w2,
    fpt,
    ocv,
    oc,
    obs,
    obr,
    side_s,
    side_r,
    sel,
    selr,
    wown,
    wr,
    kv,
    kp,
    fp,
    fpc,
    oin,
    oot,
    spt,
    lm,
    lmp,
    s0,
    biga,
    bigb,
    wst,
    xs,
    fxt,
    sxt,
    mx,
    nx,
    flx,
    flr,
    bks,
    bkr,
    waves,
    p_rows,
    p_count,
    p_weight,
    ld,
    a1s,
    a1r,
    a2s,
    a2r,
    sls,
    slr,
    ws,
    wrs,
    sds,
    sdr,
    obss,
    obrs,
    fls,
    flrs,
    bss,
    brs,
):
    me = lax.axis_index("col")
    band = lax.axis_index("band")
    up_ok = jnp.where(band > 0, 1.0, 0.0).astype(F32)
    down_ok = jnp.where(band < bands - 1, 1.0, 0.0).astype(F32)

    def col_at(k):
        return lax.rem(me + k + cols, cols)

    def away(k):
        return min(k // 4, 4 - k // 4) + min(k % 4, 4 - k % 4)

    partners = [
        lax.rem(me // 4 + k // 4, 4) * 4 + lax.rem(me % 4 + k % 4, 4)
        for k in sorted(range(1, cols), key=lambda k: -away(k))
    ]

    def exists(k):
        return band >= -k if k < 0 else band < bands - k

    def load(src, dst, k):
        c = pltpu.make_async_copy(src, dst, ld.at[k])
        c.start()
        return c

    l_atm = load(atm, xv, 0)
    l_rows = load(pair_rows, p_rows, 15)
    l_count = load(pair_count, p_count, 16)
    l_weight = load(pair_weight, p_weight, 17)
    l_ocean = load(ocean, ocv, 1)
    l_force = load(force, fp, 2)
    l_kernel = load(kernel_w, kv, 3)
    l_gain = load(gain, gv, 4)
    l_deal = load(deal, dl, 5)
    l_tf = load(tab_f, tf, 6)
    l_flux = load(flux_t, fpt, 7)
    l_surf = load(surf_t, spt, 8)
    l_land = load(land, lm, 9)
    l_ti = load(tab_i, ti, 10)
    l_w1 = load(w_in, w1, 11)
    l_w2 = load(w_out, w2, 12)
    l_oin = load(o_in, oin, 13)
    l_oot = load(o_out_t, oot, 14)

    barrier = pltpu.get_barrier_semaphore()
    for d in partners:
        pl.semaphore_signal(barrier, inc=1, device_id={"col": d}, device_id_type=MESH)
    for k in range(1, SPAN + 1):

        @pl.when(exists(k))
        def _():
            pl.semaphore_signal(barrier, inc=1, device_id={"band": band + k}, device_id_type=MESH)

    def remote(src, dst, send_sem, recv_sem, device):
        return pltpu.make_async_remote_copy(
            src_ref=src,
            dst_ref=dst,
            send_sem=send_sem,
            recv_sem=recv_sem,
            device_id=device,
            device_id_type=MESH,
        )

    def to_band(k, src, dst, send_sem, recv_sem):
        def make():
            return remote(src, dst, send_sem, recv_sem, {"band": band + k})

        def start():
            pl.when(exists(k))(lambda: make().start())

        def wait_send():
            pl.when(exists(k))(lambda: make().wait_send())

        def wait_recv():
            pl.when(exists(-k))(lambda: make().wait_recv())

        return start, wait_send, wait_recv

    def slots_to(o):
        return to_band(1 - o, sel.at[pl.ds(5 - o, 3)], selr.at[o], sls.at[o], slr.at[o])

    def weights_to(side):
        return to_band(1 - 2 * side, wown, wr.at[side], ws.at[side], wrs.at[side])

    def rim_to(side):
        src = obs.at[pl.ds(RIM * (1 - side), RIM)]
        return to_band(1 - 2 * side, src, obr.at[side], obss.at[side], obrs.at[side])

    def flux_to(o):
        return to_band(1 - o, flx, flr.at[o], fls.at[o], flrs.at[o])

    def back_to(o):
        return to_band(o, bks.at[o], bkr.at[o], bss.at[o], brs.at[o])

    lane = iota((PAD, 128), 1)

    def phase_pack():
        st[:, LATS * LOCAL :, :] = jnp.zeros((3, LATS * (PAD - LOCAL), 128), F32)
        for l in range(LOCAL):
            for t in range(3):
                cut = slice(128 * t, 128 * t + 128)
                st[t, LATS * l : LATS * l + LATS, :] = xv[l, :, cut].astype(F32)
        for a in range(LATS):
            for t in range(3):
                part = st.at[t][pl.ds(a, PAD, stride=LATS), :]
                x32[a, :, 128 * t : 128 * t + 128] = part
                rolled[a, t] = pltpu.roll(part, OWN * a, 1) if a else part
        for d in range(cols):
            out = jnp.zeros((PAD, 128), F32)
            for t in range(3):
                for e, lo, n in windows(t):
                    if e == d:
                        for a in range(LATS):
                            mask = ((lane - (lo + OWN * a)) & 127) < n
                            out = jnp.where(mask, rolled[a, t], out)
            send1[d] = out.astype(BF16)
        recv1[me] = send1[me]

    def phase_slots():
        row8 = iota((8, 128), 0)
        lane8 = iota((8, 128), 1)
        zero8 = jnp.zeros((8, 128), F32)
        for q in (0, 1, 6, 7):
            sel[q] = zero8
        for k in range(SPAN):
            other = band - k
            at = jnp.maximum(other, 0)
            used = jnp.where(other >= 0, p_count[0, at], 0)
            vec = zero8
            for p in range(SLOTS):
                target = jnp.where(p < used, SLOTS * p_rows[0, p, at] + p, -1)
                vec = jnp.where(lane8 == target, 1.0, vec)
            sel[5 - k] = vec
        vec = zero8
        for o in range(SPAN):
            at = jnp.minimum(band + o, bands - 1)
            for p in range(SLOTS):
                here = (lane8 // 16 == o) & (lane8 % SLOTS == p)
                for i in range(ROWS):
                    vec = jnp.where(here & (row8 == i), p_weight[i, p, at], vec)
        wown[...] = vec
        selr[1] = sel[4:7]
        for o in range(2, 6):

            @pl.when(jnp.logical_not(exists(o - 1)))
            def _():
                selr[o] = jnp.zeros((3, 8, 128), F32)
                flr[o] = jnp.zeros((PAD, 128), BF16)

        @pl.when(jnp.logical_not(exists(-1)))
        def _():
            selr[0] = jnp.zeros((3, 8, 128), F32)
            flr[0] = jnp.zeros((PAD, 128), BF16)
            wr[0] = zero8
            obr[0] = jnp.zeros((RIM, PAD, HP), BF16)

        @pl.when(jnp.logical_not(exists(1)))
        def _():
            wr[1] = zero8
            obr[1] = jnp.zeros((RIM, PAD, HP), BF16)

        for o in range(1, SPAN):

            @pl.when(jnp.logical_not(exists(-o)))
            def _():
                bkr[o] = jnp.zeros((64, PAD), BF16)

    def phase_rims():
        oc[RIM : RIM + ROWS] = jnp.zeros((ROWS, PAD, HP), F32)
        oc[RIM : RIM + ROWS, 0:LOCAL, 0:HO] = ocv[...].astype(F32)
        row = iota((16, HP), 0)
        for b in range(2):
            for side in range(2):
                out = jnp.zeros((16, HP), F32)
                for q in range(3):
                    i = RIM + 3 * b + q
                    part = oc[i, 0:16, :] if side == 0 else oc[i, 80:96, :]
                    shift = (RIM * q - (0 if side == 0 else 7)) % 16
                    part = pltpu.roll(part, shift, 0) if shift else part
                    out = jnp.where((row >= RIM * q) & (row < RIM * q + RIM), part, out)
                side_s[side, :, HP * b : HP * b + HP] = out.astype(BF16)
        row = iota((16, CH), 0)
        for side in range(2):
            out = jnp.zeros((16, CH), F32)
            for a in range(LATS):
                part = x32[a, 0:16, :] if side == 0 else x32[a, 80:96, :]
                shift = (RIM * a - (0 if side == 0 else 7)) % 16
                part = pltpu.roll(part, shift, 0) if shift else part
                out = jnp.where((row >= RIM * a) & (row < RIM * a + RIM), part, out)
            side_s[side, :, 2 * HP :] = out.astype(BF16)

    def phase_gains():
        gx[...] = jnp.zeros(gx.shape, F32)
        for a in range(LATS):
            for q in range(OWN // 8):
                row = pl.multiple_of(lax.rem(OWN * (me + a) + 8 * q, 128), 8)
                gx[:, pl.ds(row, 8), 0:WAVES] = gv[:, 8 * q : 8 * q + 8, :] * (2.0 / LON)
        for part in range(2):
            g = gx[part]
            high = g.astype(BF16)
            low = (g - high.astype(F32)).astype(BF16)
            both = dot_nt(dl[...], jnp.concatenate([high, low], axis=0))
            gt[part] = both[:, :128] + both[:, 128:]

    def phase_weights():
        kp[...] = jnp.zeros(kp.shape, F32)
        kp[:, 0:KS, 0:HO] = kv[...]
        f32_force = fp[...].astype(F32)
        wst[...] = jnp.zeros(wst.shape, BF16)
        fpc[...] = jnp.zeros(fpc.shape, BF16)
        for dj in range(KS):
            for di in range(KS):
                at = 128 * dj + FIELDS * di
                wst[at : at + FIELDS, 0:HO] = (f32_force * kp[di, dj : dj + 1, 0:HO]).astype(BF16)
        fpc[FIELDS * RIM : FIELDS * RIM + FIELDS, 0:HO] = fp[...]

        r, f = iota((512, FIELDS), 0), iota((512, FIELDS), 1)
        spread = one_hot((r % 64 // 16 == r // 128) & (r % 16 == f))
        fxt[...] = dot(spread, fpt[...]).astype(BF16)
        r, f = iota((768, FIELDS), 0), iota((768, FIELDS), 1)
        spread = one_hot((r % 128 // 16 == r // 128) & (r % 16 == f))
        sxt[...] = dot(spread, spt[...]).astype(BF16)
        lmp[...] = jnp.zeros(lmp.shape, F32)
        lmp[0:ROWS, 0:LOCAL] = lm[...].astype(F32)

    def with_rim(own, right, left, row, k):
        right = pltpu.roll(right, (10 - RIM * k) % 16, 0)
        left = pltpu.roll(left, (13 - RIM * k) % 16, 0)
        return jnp.where(row < 10, own, jnp.where(row < 13, right, left))

    def phase_ocean_rim():
        row = iota((16, HP), 0)
        for b in range(2):
            cut = slice(HP * b, HP * b + HP)
            right, left = side_r[0, :, cut].astype(F32), side_r[1, :, cut].astype(F32)
            for q in range(3):
                i = RIM + 3 * b + q
                oc[i, 80:96, :] = with_rim(oc[i, 80:96, :], right, left, row, q)
        obs[...] = oc[RIM : RIM + ROWS].astype(BF16)

    def phase_matrices():
        blocks = []
        for b in range(3):
            chosen = selr[0, b]
            for o in range(1, 6):
                chosen = chosen + pltpu.roll(selr[o, b], 16 * o, 1)
            if b == 0:
                blocks.append(wr[0] * chosen * up_ok)
            elif b == 1:
                blocks.append(pltpu.roll(wown[...], 16, 1) * chosen)
            else:
                blocks.append(pltpu.roll(wr[1], 32, 1) * chosen * down_ok)
        slots = jnp.concatenate(blocks, axis=0).astype(BF16)
        r, c_ = iota((384, 128), 0), iota((384, 128), 1)
        by_row = dot_nt(one_hot(r // 16 == c_ // 4), slots).astype(BF16)
        r, c_ = iota((24, 768), 0), iota((24, 768), 1)
        tap = c_ % 128 // 16
        need = c_ // 128 + tap
        has = r % 8 + jnp.where(r < 8, -RIM, jnp.where(r < 16, RIM, RIM + ROWS))
        legal = (
            (tap < KS)
            & ((r >= 8) | (r % 8 >= ROWS - RIM))
            & (r % 8 < ROWS)
            & ((r < 16) | (r % 8 < RIM))
        )
        spread = one_hot(legal & (need == has))
        r, c_ = iota((384, 768), 0), iota((384, 768), 1)
        biga[...] = jnp.where(r % 16 == c_ % 16, dot(by_row, spread), 0.0).astype(BF16)
        r, c_ = iota((128, 24), 0), iota((128, 24), 1)
        by_own = dot(one_hot((c_ - 8 == r // 16) & (r // 16 < ROWS)), slots).astype(BF16)
        r, c_ = iota((256, 128), 0), iota((256, 128), 1)
        full = dot_nt(one_hot(c_ // 4 == 4 * (r // 64 + 1) + r % 64 // 16), by_own)
        bigb[...] = jnp.where(r % 16 == c_ % 16, full, 0.0).astype(BF16)

    def phase_spectra():
        first = recv1[0:BLOCKS].reshape(TAB, 128).astype(F32)
        second = recv1[BLOCKS : 2 * BLOCKS].reshape(TAB, 128).astype(F32)
        for parity in range(2):
            mix = first - second if parity else first + second
            spec = dot(tf[parity], mix.astype(BF16))
            real, imag = spec[:WPAD], spec[WPAD:]
            rows = slice(parity * WPAD, parity * WPAD + WPAD)
            g_real, g_imag = gt[0, rows], gt[1, rows]
            waves[parity, :WPAD] = (g_real * real + g_imag * imag).astype(BF16)
            waves[parity, WPAD:] = (g_real * imag - g_imag * real).astype(BF16)

    chunk = 2

    def phase_inverse(k):
        parts = BLOCKS // chunk
        q = lax.rem(me // chunk + k + 1, parts)
        rows = pl.ds(pl.multiple_of(q * (chunk * PAD), chunk * PAD), chunk * PAD)
        even = dot(ti[0, rows, :], waves[0])
        odd = dot(ti[1, rows, :], waves[1])
        send2[pl.ds(q * chunk, chunk)] = (even + odd).astype(BF16).reshape(chunk, PAD, 128)
        send2[pl.ds(q * chunk + BLOCKS, chunk)] = (
            (even - odd).astype(BF16).reshape(chunk, PAD, 128)
        )
        return q

    def phase_stencil(half):
        if half:
            oc[RIM + ROWS :] = obr[1].astype(F32) * down_ok
        else:
            oc[0:RIM] = obr[0].astype(F32) * up_ok

        def stencil_row(i, carry):
            for t in range(HP // 128):
                cut = slice(128 * t, 128 * t + 128)
                total = None
                for dj in range(KS):
                    line = None
                    for di in range(KS):
                        term = kp[di, dj : dj + 1, cut] * oc[i + di, :, cut]
                        line = term if line is None else line + term
                    shift = (RIM - dj) % PAD
                    line = pltpu.roll(line, shift, 0) if shift else line
                    total = line if total is None else total + line
                s0[i, :, cut] = total
            return carry

        lax.fori_loop(RIM * half, RIM * half + RIM, stencil_row, 0)

    def phase_atm_rim():
        row = iota((16, CH), 0)
        right, left = side_r[0, :, 2 * HP :].astype(F32), side_r[1, :, 2 * HP :].astype(F32)
        for a in range(LATS):
            x32[a, 80:96, :] = with_rim(x32[a, 80:96, :], right, left, row, a)

    def phase_unpack():
        for a in range(LATS):
            for t in range(3):
                cut = slice(128 * t, 128 * t + 128)
                zonal = jnp.zeros((PAD, 128), F32)
                for d, lo, n in windows(t):
                    mask = ((lane - (lo + OWN * a)) & 127) < n
                    zonal = jnp.where(mask, recv2[d].astype(F32), zonal)
                if a:
                    zonal = pltpu.roll(zonal, 128 - OWN * a, 1)
                mx[a * PAD : a * PAD + PAD, cut] = x32[a, :, cut] + zonal

    def phase_atm():
        mixed = mx[...]
        centred = mixed - jnp.mean(mixed, axis=-1, keepdims=True)
        spread = jnp.mean(centred * centred, axis=-1, keepdims=True)
        normed = (centred * lax.rsqrt(spread + 1e-05)).astype(BF16)
        inner = jax.nn.gelu(dot(normed, w1[...])).astype(BF16)
        nx[...] = (mx[...] + dot(inner, w2[...])).astype(BF16)
        flux = None
        for a in range(LATS):
            term = dot_nt(nx[a * PAD : a * PAD + PAD, :], fxt[128 * a : 128 * a + 128, :])
            flux = term if flux is None else flux + term
        flx[...] = flux.astype(BF16)
        flr[1] = flx[...]

    def phase_atm_out():
        for t in range(3):
            cut = slice(128 * t, 128 * t + 128)
            for a in range(LATS):
                part = nx[a * PAD : a * PAD + PAD, cut].astype(F32)
                st.at[t][pl.ds(a, PAD, stride=LATS), :] = part
            for l in range(LOCAL):
                ao[l, :, cut] = st[t, LATS * l : LATS * l + LATS, :].astype(BF16)

    def phase_forcing():
        low = iota((PAD, 128), 1) < 64
        tiles = [
            jnp.where(low, flr[2 * q].astype(F32), flr[2 * q + 1].astype(F32)).astype(BF16)
            for q in range(3)
        ]
        forcing = dot(jnp.concatenate(tiles, axis=1), biga[...])
        for i in range(ROWS):
            part = forcing[:, 128 * i : 128 * i + 128]
            for dj in range(KS):
                shift = (RIM - dj) % PAD
                turned = pltpu.roll(part, shift, 0) if shift else part
                xs[PAD * i : PAD * i + PAD, 128 * dj : 128 * dj + 128] = turned.astype(BF16)

    def phase_ocean():
        r, c_ = iota((128, 128), 0), iota((128, 128), 1)
        sea = dot_nt(one_hot(r == c_), lmp[...].astype(BF16))
        rows = ROWS * PAD
        stencil = (dot(xs[...], wst[...]) + s0[...].reshape(rows, HP))[:, :HO]
        centred = stencil - jnp.mean(stencil, axis=-1, keepdims=True)
        spread = jnp.mean(centred * centred, axis=-1, keepdims=True)
        onorm = (centred * lax.rsqrt(spread + 1e-05)).astype(BF16)
        hidden = jax.nn.gelu(dot(onorm, oin[...])).astype(BF16)
        change = dot_nt(hidden, oot[...])
        pushed = dot(xs[:, 128 * RIM : 128 * RIM + 128], fpc[...])
        lifted = (oc[RIM : RIM + ROWS].reshape(rows, HP) + pushed)[:, :HO].astype(BF16).astype(F32)
        result = lifted + change
        surface = None
        for i in range(ROWS):
            part = (result[PAD * i : PAD * i + PAD] * sea[0:PAD, i : i + 1]).astype(BF16)
            oo[i] = part[:LOCAL]
            term = dot_nt(part, sxt[128 * i : 128 * i + 128, :])
            surface = term if surface is None else surface + term
        back = dot_nt(bigb[...], surface.astype(BF16)).astype(BF16)
        for o in range(SPAN):
            bks[o] = back[64 * o : 64 * o + 64]

    def phase_sum():
        total = bks[0].astype(F32)
        for o in range(1, SPAN):
            total = total + bkr[o].astype(F32)
        so[...] = total.reshape(LATS, FIELDS, PAD)[:, :, :LOCAL].astype(BF16)

    l_atm.wait()
    phase_pack()
    l_rows.wait()
    l_count.wait()
    l_weight.wait()
    phase_slots()
    l_ocean.wait()
    phase_rims()
    pl.semaphore_wait(barrier, cols - 1 + jnp.minimum(band, SPAN))

    a1 = []
    for d in partners:
        step = lax.rem(d - me + cols, cols)
        c = remote(send1.at[d], recv1.at[me], a1s.at[step], a1r.at[step], {"col": d})
        c.start()
        a1.append(c)
    sides = []
    for side, k in ((0, -1), (1, 1)):
        c = remote(side_s.at[side], side_r.at[side], sds.at[side], sdr.at[side], {"col": col_at(k)})
        c.start()
        sides.append(c)
    weights_to(1)[0]()
    for o in range(2, 6):
        slots_to(o)[0]()

    l_gain.wait()
    l_deal.wait()
    phase_gains()
    l_force.wait()
    l_kernel.wait()
    l_flux.wait()
    l_surf.wait()
    l_land.wait()
    phase_weights()
    for c in sides:
        c.wait_recv()
    phase_ocean_rim()
    phase_atm_rim()
    rim_to(1)[0]()

    l_tf.wait()
    for c in a1:
        c.wait_recv()
    phase_spectra()
    l_ti.wait()
    for k in range(BLOCKS // chunk):
        q = phase_inverse(k)
        for n in range(2 * chunk):
            to = q * chunk + n % chunk + BLOCKS * (n // chunk)
            step = lax.rem(to - me + cols, cols)

            @pl.when(to != me)
            def _():
                remote(
                    send2.at[to], recv2.at[me], a2s.at[step], a2r.at[step], {"col": to}
                ).start()

    recv2[me] = send2[me]

    weights_to(1)[2]()
    for o in range(2, 6):
        slots_to(o)[2]()
    rim_to(0)[0]()
    weights_to(0)[0]()
    slots_to(0)[0]()
    rim_to(1)[2]()
    phase_stencil(1)
    weights_to(0)[2]()
    slots_to(0)[2]()
    phase_matrices()
    rim_to(0)[2]()
    phase_stencil(0)

    for k in range(1, cols):
        remote(send2.at[0], recv2.at[0], a2s.at[k], a2r.at[k], {"col": col_at(k)}).wait_recv()
    phase_unpack()
    l_w1.wait()
    l_w2.wait()
    phase_atm()
    for o in (5, 4, 3, 2, 0):
        flux_to(o)[0]()
    phase_atm_out()

    l_oin.wait()
    l_oot.wait()
    for o in (0, 2, 3, 4, 5):
        flux_to(o)[2]()
    phase_forcing()
    phase_ocean()
    for o in (3, 2, 1):
        back_to(o)[0]()
    for o in range(1, SPAN):
        back_to(o)[2]()
    phase_sum()

    for c in a1:
        c.wait_send()
    for c in sides:
        c.wait_send()
    for k in range(1, cols):
        remote(send2.at[0], recv2.at[0], a2s.at[k], a2r.at[k], {"col": col_at(k)}).wait_send()
    for o in (0, 2, 3, 4, 5):
        slots_to(o)[1]()
        flux_to(o)[1]()
    for side in range(2):
        weights_to(side)[1]()
        rim_to(side)[1]()
    for o in range(1, SPAN):
        back_to(o)[1]()


def store(a, b, c, a_out, b_out, c_out, sems):
    copies = [
        pltpu.make_async_copy(x, y, sems.at[k])
        for k, (x, y) in enumerate(((a, a_out), (b, b_out), (c, c_out)))
    ]
    for x in copies:
        x.start()
    for x in copies:
        x.wait()


def per_device(
    bands,
    cols,
    consts,
    atm_state,
    spec_gain,
    mlp_in,
    mlp_out,
    flux_proj,
    pair_rows,
    pair_count,
    pair_weight,
    ocean_state,
    force_proj,
    depth_kernel,
    ocean_in,
    ocean_out,
    surf_proj,
    land_mask,
):
    any_spec = pl.BlockSpec(memory_space=ANY)
    vm = pltpu.VMEM
    dma = pltpu.SemaphoreType.DMA
    scratch = [
        vm((LOCAL, LATS, CH), BF16),
        vm((3, LATS * PAD, 128), F32),
        vm((LATS, PAD, CH), F32),
        vm((LATS, 3, PAD, 128), F32),
        vm((16, PAD, 128), BF16),
        vm((16, PAD, 128), BF16),
        vm((16, PAD, 128), BF16),
        vm((16, PAD, 128), BF16),
        vm((2, TAB, TAB), BF16),
        vm((2, TAB, TAB), BF16),
        vm((TAB, TAB), BF16),
        vm((2, OWN, WAVES), F32),
        vm((2, 128, TAB), F32),
        vm((2, TAB, 128), F32),
        vm((CH, 768), BF16),
        vm((768, CH), BF16),
        vm((FIELDS, CH), BF16),
        vm((ROWS, LOCAL, HO), BF16),
        vm((ROWS + 2 * RIM, PAD, HP), F32),
        vm((ROWS, PAD, HP), BF16),
        vm((2, RIM, PAD, HP), BF16),
        vm((2, 16, 2 * HP + CH), BF16),
        vm((2, 16, 2 * HP + CH), BF16),
        vm((8, 8, 128), F32),
        vm((6, 3, 8, 128), F32),
        vm((8, 128), F32),
        vm((2, 8, 128), F32),
        vm((KS, KS, HO), F32),
        vm((KS, 8, HP), F32),
        vm((FIELDS, HO), BF16),
        vm((128, HP), BF16),
        vm((HO, 800), BF16),
        vm((HO, 800), BF16),
        vm((FIELDS, HO), BF16),
        vm((ROWS, LOCAL), jnp.int32),
        vm((8, 128), F32),
        vm((ROWS, PAD, HP), F32),
        vm((384, 768), BF16),
        vm((256, 128), BF16),
        vm((KS * 128, HP), BF16),
        vm((ROWS * PAD, KS * 128), BF16),
        vm((512, CH), BF16),
        vm((768, HO), BF16),
        vm((LATS * PAD, CH), F32),
        vm((LATS * PAD, CH), BF16),
        vm((PAD, 128), BF16),
        vm((6, PAD, 128), BF16),
        vm((SPAN, 64, PAD), BF16),
        vm((SPAN, 64, PAD), BF16),
        vm((2, TAB, 128), BF16),
        pltpu.SMEM((1, SLOTS, bands), jnp.int32),
        pltpu.SMEM((1, bands), jnp.int32),
        pltpu.SMEM((ROWS, SLOTS, bands), F32),
        dma((18,)),
        dma((16,)),
        dma((16,)),
        dma((16,)),
        dma((16,)),
        dma((6,)),
        dma((6,)),
        dma((2,)),
        dma((2,)),
        dma((2,)),
        dma((2,)),
        dma((2,)),
        dma((2,)),
        dma((6,)),
        dma((6,)),
        dma((4,)),
        dma((4,)),
    ]
    shapes = (
        jax.ShapeDtypeStruct((LOCAL, LATS, CH), BF16),
        jax.ShapeDtypeStruct((ROWS, LOCAL, HO), BF16),
        jax.ShapeDtypeStruct((LATS, FIELDS, LOCAL), BF16),
    )
    out = pl.pallas_call(
        functools.partial(body, bands, cols),
        out_shape=tuple(vm(x.shape, x.dtype) for x in shapes),
        in_specs=[any_spec] * 18,
        out_specs=(pl.BlockSpec(memory_space=vm),) * 3,
        scratch_shapes=scratch,
        compiler_params=pltpu.CompilerParams(
            collective_id=0, has_side_effects=True, vmem_limit_bytes=56 * 1024 * 1024
        ),
    )(
        jnp.transpose(atm_state, (1, 0, 2)),
        jnp.transpose(spec_gain, (0, 2, 1)),
        mlp_in,
        mlp_out,
        jnp.transpose(flux_proj),
        jnp.transpose(pair_rows, (1, 2, 0)),
        jnp.transpose(pair_count),
        jnp.transpose(pair_weight, (0, 2, 1)),
        ocean_state,
        force_proj,
        depth_kernel,
        ocean_in,
        jnp.transpose(ocean_out),
        jnp.transpose(surf_proj),
        land_mask,
        *consts,
    )
    out = pl.pallas_call(
        store,
        out_shape=shapes,
        in_specs=[pl.BlockSpec(memory_space=vm)] * 3,
        out_specs=(any_spec,) * 3,
        scratch_shapes=[dma((3,))],
    )(*[pltpu.with_memory_space_constraint(x, vm) for x in out])
    return (
        jnp.transpose(out[0], (1, 0, 2)),
        out[1],
        jnp.transpose(out[2], (0, 2, 1)),
    )


def solution(mesh):
    placed = (
        P("band", "col", None),
        P(None, None, "col"),
        P(),
        P(),
        P(),
        P(None, "band", None),
        P(None, "band"),
        P("band", None, None),
        P("band", "col", None),
        P(),
        P(),
        P(),
        P(),
        P(),
        P("band", "col"),
    )
    consts = tables()
    step = functools.partial(
        per_device, mesh.shape["band"], mesh.shape["col"], [jnp.asarray(t) for t in consts]
    )
    return jax.shard_map(
        step,
        mesh=mesh,
        in_specs=placed,
        out_specs=(P("band", "col", None), P("band", "col", None), P("band", "col", None)),
        check_vma=False,
    )
```

```python
import functools

import jax
import jax.numpy as jnp
import numpy as np
from jax import lax
from jax.experimental import pallas as pl
from jax.experimental.pallas import tpu as pltpu
from jax.sharding import PartitionSpec as P

F32 = jnp.float32
BF16 = jnp.bfloat16
MESH = pl.DeviceIdType.MESH
ANY = pl.ANY

SPAN = 4
LATS = 4
SLOTS = 4
LON = 1440
WAVES = 720
LOCAL = 90
PAD = 96
RIM = 3
MAIN = 80
TAIL = PAD - MAIN
FIRST = 48
REST = MAIN - FIRST
HEAD = FIRST + TAIL
KS = 7
CH = 384
OWN = 24
HALF = LON // 2
BLOCKS = 8
TAB = BLOCKS * PAD
WPAD = TAB // 2
ROWS = 6
HO = 200
HP = 256
FIELDS = 16
NT = (((1,), (1,)), ((), ()))


def tables():
    block = np.arange(BLOCKS)[:, None]

    def places(*spans):
        pieces = [(block * LON // 16 + 0 * np.arange(a, b), np.arange(a, b) + 0 * block) for a, b in spans]
        start = np.concatenate([p[0].reshape(-1) for p in pieces])
        return start, np.concatenate([p[1].reshape(-1) for p in pieces])

    start, place = places((0, MAIN), (MAIN, PAD))
    inside = place < LOCAL
    lon_in = start + place
    start, place = places((0, FIRST), (MAIN, PAD), (FIRST, MAIN))
    lon_out = start + np.where(place < LOCAL + RIM, place, place - PAD)
    forward = np.zeros((2, TAB, TAB), np.float64)
    inverse = np.zeros((2, TAB, TAB), np.float64)
    deal = np.zeros((2 * WPAD, TAB), np.float64)
    count = WAVES // 2
    for parity in range(2):
        wave = 2 * np.arange(count) + parity
        angle = 2 * np.pi * (wave[:, None] * lon_in[None] % LON) / LON
        forward[parity, :count] = np.cos(angle) * inside
        forward[parity, WPAD : WPAD + count] = np.sin(angle) * inside
        angle = 2 * np.pi * (lon_out[:, None] * wave[None] % LON) / LON
        inverse[parity, :, :count] = np.cos(angle)
        inverse[parity, :, WPAD : WPAD + count] = np.sin(angle)
        deal[parity * WPAD + np.arange(count), wave] = 1.0
    return [t.astype(np.float32).astype(jnp.bfloat16) for t in (forward, inverse, deal)]


def iota(shape, axis):
    return lax.broadcasted_iota(jnp.int32, shape, axis)


def one_hot(condition):
    return jnp.where(condition, 1.0, 0.0).astype(BF16)


def dot(a, b):
    return jnp.dot(a, b, preferred_element_type=F32)


def dot_nt(a, b):
    return lax.dot_general(a, b, NT, preferred_element_type=F32)


def gelu(x):
    half = 0.5 * x
    inner = x * (0.7978845608028654 + 0.035677408136300125 * (x * x))
    return (half + half * jnp.tanh(inner)).astype(BF16)


def fold(main, tail, free):
    return [
        jnp.where(free, pltpu.roll(tail, 96 - 32 * g, 1), main[TAIL * g : TAIL * g + TAIL])
        for g in range(3)
    ]


def unfold(main, lane, first):
    out = None
    for g in range(3):
        part = pltpu.roll(main[TAIL * g : TAIL * g + TAIL], 32 + 32 * g, 1)
        out = part if out is None else jnp.where(((lane - first) & 127) // 32 == g, part, out)
    return out


def windows(tile):
    out = []
    for d in range(16):
        lo, hi = max(OWN * d, 128 * tile), min(OWN * d + OWN, 128 * tile + 128)
        if lo < hi:
            out.append((d, lo, hi - lo))
    return out


def body(
    bands,
    cols,
    atm,
    gain,
    w_in,
    w_out,
    flux_t,
    pair_rows,
    pair_count,
    pair_weight,
    ocean,
    force,
    kernel_w,
    o_in,
    o_out_t,
    surf_t,
    land,
    tab_f,
    tab_i,
    deal,
    ao,
    oo,
    so,
    xv,
    st,
    x32,
    rolled,
    send1,
    recv1,
    send2,
    recv2,
    send2b,
    recv2b,
    tails,
    tails2,
    tf,
    ti,
    dl,
    gv,
    gx,
    gt,
    w1,
    w2,
    fpt,
    ocv,
    oc,
    obs,
    obr,
    side_s,
    side_r,
    sel,
    selr,
    wown,
    wr,
    kv,
    kp,
    fp,
    fpc,
    oin,
    oot,
    spt,
    lm,
    lmp,
    s0,
    biga,
    bigb,
    wst,
    xs,
    fxt,
    sxt,
    mx,
    nx,
    flx32,
    flx,
    flr,
    bks,
    bkr,
    waves,
    sea,
    p_rows,
    p_count,
    p_weight,
    ld,
    a1s,
    a1r,
    a2s,
    a2r,
    a3s,
    a3r,
    sls,
    slr,
    ws,
    wrs,
    sds,
    sdr,
    obss,
    obrs,
    fls,
    flrs,
    bss,
    brs,
):
    me = lax.axis_index("col")
    band = lax.axis_index("band")
    up_ok = jnp.where(band > 0, 1.0, 0.0).astype(F32)
    down_ok = jnp.where(band < bands - 1, 1.0, 0.0).astype(F32)

    def col_at(k):
        return lax.rem(me + k + cols, cols)

    def away(k):
        return min(k // 4, 4 - k // 4) + min(k % 4, 4 - k % 4)

    partners = [
        lax.rem(me // 4 + k // 4, 4) * 4 + lax.rem(me % 4 + k % 4, 4)
        for k in sorted(range(1, cols), key=lambda k: -away(k))
    ]

    def exists(k):
        return band >= -k if k < 0 else band < bands - k

    def load(src, dst, k):
        c = pltpu.make_async_copy(src, dst, ld.at[k])
        c.start()
        return c

    l_atm = load(atm, xv, 0)
    l_rows = load(pair_rows, p_rows, 15)
    l_count = load(pair_count, p_count, 16)
    l_weight = load(pair_weight, p_weight, 17)
    l_ocean = load(ocean, ocv, 1)
    l_force = load(force, fp, 2)
    l_kernel = load(kernel_w, kv, 3)
    l_gain = load(gain, gv, 4)
    l_deal = load(deal, dl, 5)
    l_tf = load(tab_f, tf, 6)
    l_flux = load(flux_t, fpt, 7)
    l_surf = load(surf_t, spt, 8)
    l_land = load(land, lm, 9)
    l_ti = load(tab_i, ti, 10)
    l_w1 = load(w_in, w1, 11)
    l_w2 = load(w_out, w2, 12)
    l_oin = load(o_in, oin, 13)
    l_oot = load(o_out_t, oot, 14)

    barrier = pltpu.get_barrier_semaphore()
    for d in partners:
        pl.semaphore_signal(barrier, inc=1, device_id={"col": d}, device_id_type=MESH)
    for k in range(1, SPAN + 1):

        @pl.when(exists(k))
        def _():
            pl.semaphore_signal(barrier, inc=1, device_id={"band": band + k}, device_id_type=MESH)

    def remote(src, dst, send_sem, recv_sem, device):
        return pltpu.make_async_remote_copy(
            src_ref=src,
            dst_ref=dst,
            send_sem=send_sem,
            recv_sem=recv_sem,
            device_id=device,
            device_id_type=MESH,
        )

    def to_band(k, src, dst, send_sem, recv_sem):
        def make():
            return remote(src, dst, send_sem, recv_sem, {"band": band + k})

        def start():
            pl.when(exists(k))(lambda: make().start())

        def wait_send():
            pl.when(exists(k))(lambda: make().wait_send())

        def wait_recv():
            pl.when(exists(-k))(lambda: make().wait_recv())

        return start, wait_send, wait_recv

    def slots_to(o):
        return to_band(1 - o, sel.at[pl.ds(5 - o, 3)], selr.at[o], sls.at[o], slr.at[o])

    def weights_to(side):
        return to_band(1 - 2 * side, wown, wr.at[side], ws.at[side], wrs.at[side])

    def rim_to(side):
        src = obs.at[pl.ds(RIM * (1 - side), RIM)]
        return to_band(1 - 2 * side, src, obr.at[side], obss.at[side], obrs.at[side])

    def flux_to(o):
        return to_band(1 - o, flx, flr.at[o], fls.at[o], flrs.at[o])

    def back_to(o):
        return to_band(o, bks.at[o], bkr.at[o], bss.at[o], brs.at[o])

    lane = iota((PAD, 128), 1)
    lane16 = iota((TAIL, 128), 1)

    def phase_pack():
        st[:, LATS * LOCAL :, :] = jnp.zeros((3, LATS * (PAD - LOCAL), 128), F32)
        for l in range(LOCAL):
            for t in range(3):
                cut = slice(128 * t, 128 * t + 128)
                st[t, LATS * l : LATS * l + LATS, :] = xv[l, :, cut].astype(F32)
        for a in range(LATS):
            for t in range(3):
                part = st.at[t][pl.ds(a, PAD, stride=LATS), :]
                x32[a, :, 128 * t : 128 * t + 128] = part
                rolled[a, t] = pltpu.roll(part, OWN * a, 1) if a else part
        for d in range(cols):
            out = jnp.zeros((PAD, 128), F32)
            for t in range(3):
                for e, lo, n in windows(t):
                    if e == d:
                        for a in range(LATS):
                            mask = ((lane - (lo + OWN * a)) & 127) < n
                            out = jnp.where(mask, rolled[a, t], out)
            free = ((lane16 - OWN * d) & 127) >= 96
            for g, piece in enumerate(fold(out, out[MAIN:], free)):
                send1[d, TAIL * g : TAIL * g + TAIL] = piece.astype(BF16)
            send1[d, FIRST:] = out[FIRST:MAIN].astype(BF16)
        recv1[me] = send1[me]

    def phase_slots():
        row8 = iota((8, 128), 0)
        lane8 = iota((8, 128), 1)
        zero8 = jnp.zeros((8, 128), F32)
        for q in (0, 1, 6, 7):
            sel[q] = zero8
        for k in range(SPAN):
            other = band - k
            at = jnp.maximum(other, 0)
            used = jnp.where(other >= 0, p_count[0, at], 0)
            vec = zero8
            for p in range(SLOTS):
                target = jnp.where(p < used, SLOTS * p_rows[0, p, at] + p, -1)
                vec = jnp.where(lane8 == target, 1.0, vec)
            sel[5 - k] = vec
        vec = zero8
        for o in range(SPAN):
            at = jnp.minimum(band + o, bands - 1)
            for p in range(SLOTS):
                here = (lane8 // 16 == o) & (lane8 % SLOTS == p)
                for i in range(ROWS):
                    vec = jnp.where(here & (row8 == i), p_weight[i, p, at], vec)
        wown[...] = vec
        selr[1] = sel[4:7]
        for o in range(2, 6):

            @pl.when(jnp.logical_not(exists(o - 1)))
            def _():
                selr[o] = jnp.zeros((3, 8, 128), F32)
                flr[o] = jnp.zeros((FIRST, 128), BF16)

        @pl.when(jnp.logical_not(exists(-1)))
        def _():
            selr[0] = jnp.zeros((3, 8, 128), F32)
            flr[0] = jnp.zeros((FIRST, 128), BF16)
            wr[0] = zero8
            obr[0] = jnp.zeros((RIM, PAD, HP), BF16)

        @pl.when(jnp.logical_not(exists(1)))
        def _():
            wr[1] = zero8
            obr[1] = jnp.zeros((RIM, PAD, HP), BF16)

        for o in range(1, SPAN):

            @pl.when(jnp.logical_not(exists(-o)))
            def _():
                bkr[o] = jnp.zeros((FIRST, 128), BF16)

    def phase_rims():
        oc[RIM : RIM + ROWS] = jnp.zeros((ROWS, PAD, HP), F32)
        oc[RIM : RIM + ROWS, 0:LOCAL, 0:HO] = ocv[...].astype(F32)
        row = iota((16, HP), 0)
        for b in range(2):
            for side in range(2):
                out = jnp.zeros((16, HP), F32)
                for q in range(3):
                    i = RIM + 3 * b + q
                    part = oc[i, 0:16, :] if side == 0 else oc[i, 80:96, :]
                    shift = (RIM * q - (0 if side == 0 else 7)) % 16
                    part = pltpu.roll(part, shift, 0) if shift else part
                    out = jnp.where((row >= RIM * q) & (row < RIM * q + RIM), part, out)
                side_s[side, :, HP * b : HP * b + HP] = out.astype(BF16)
        row = iota((16, CH), 0)
        for side in range(2):
            out = jnp.zeros((16, CH), F32)
            for a in range(LATS):
                part = x32[a, 0:16, :] if side == 0 else x32[a, 80:96, :]
                shift = (RIM * a - (0 if side == 0 else 7)) % 16
                part = pltpu.roll(part, shift, 0) if shift else part
                out = jnp.where((row >= RIM * a) & (row < RIM * a + RIM), part, out)
            side_s[side, :, 2 * HP :] = out.astype(BF16)

    def phase_gains():
        gx[...] = jnp.zeros(gx.shape, F32)
        for a in range(LATS):
            for q in range(OWN // 8):
                row = pl.multiple_of(lax.rem(OWN * (me + a) + 8 * q, 128), 8)
                gx[:, pl.ds(row, 8), 0:WAVES] = gv[:, 8 * q : 8 * q + 8, :] * (2.0 / LON)
        for part in range(2):
            g = gx[part]
            high = g.astype(BF16)
            low = (g - high.astype(F32)).astype(BF16)
            both = dot_nt(dl[...], jnp.concatenate([high, low], axis=0))
            gt[part] = both[:, :128] + both[:, 128:]

    def phase_weights():
        kp[...] = jnp.zeros(kp.shape, F32)
        kp[:, 0:KS, 0:HO] = kv[...]
        f32_force = fp[...].astype(F32)
        wst[...] = jnp.zeros(wst.shape, BF16)
        fpc[...] = jnp.zeros(fpc.shape, BF16)
        for dj in range(KS):
            for di in range(KS):
                at = 128 * dj + FIELDS * di
                weight = f32_force * kp[di, dj : dj + 1, 0:HO]
                weight = weight - jnp.mean(weight, axis=-1, keepdims=True)
                wst[at : at + FIELDS, 0:HO] = weight.astype(BF16)
        fpc[FIELDS * RIM : FIELDS * RIM + FIELDS, 0:HO] = fp[...]

        r, f = iota((512, FIELDS), 0), iota((512, FIELDS), 1)
        spread = one_hot((r % 64 // 16 == r // 128) & (r % 16 == f))
        fxt[...] = dot(spread, fpt[...]).astype(BF16)
        r, f = iota((768, FIELDS), 0), iota((768, FIELDS), 1)
        spread = one_hot((r % 128 // 16 == r // 128) & (r % 16 == f))
        sxt[...] = dot(spread, spt[...]).astype(BF16)
        lmp[...] = jnp.zeros(lmp.shape, F32)
        lmp[0:ROWS, 0:LOCAL] = lm[...].astype(F32)
        r, c_ = iota((128, 128), 0), iota((128, 128), 1)
        sea[...] = dot_nt(one_hot(r == c_), lmp[...].astype(BF16))

    def with_rim(own, right, left, row, k):
        right = pltpu.roll(right, (10 - RIM * k) % 16, 0)
        left = pltpu.roll(left, (13 - RIM * k) % 16, 0)
        return jnp.where(row < 10, own, jnp.where(row < 13, right, left))

    def phase_ocean_rim():
        row = iota((16, HP), 0)
        for b in range(2):
            cut = slice(HP * b, HP * b + HP)
            right, left = side_r[0, :, cut].astype(F32), side_r[1, :, cut].astype(F32)
            for q in range(3):
                i = RIM + 3 * b + q
                oc[i, 80:96, :] = with_rim(oc[i, 80:96, :], right, left, row, q)
        obs[...] = oc[RIM : RIM + ROWS].astype(BF16)

    def phase_matrices():
        blocks = []
        for b in range(3):
            chosen = selr[0, b]
            for o in range(1, 6):
                chosen = chosen + pltpu.roll(selr[o, b], 16 * o, 1)
            if b == 0:
                blocks.append(wr[0] * chosen * up_ok)
            elif b == 1:
                blocks.append(pltpu.roll(wown[...], 16, 1) * chosen)
            else:
                blocks.append(pltpu.roll(wr[1], 32, 1) * chosen * down_ok)
        slots = jnp.concatenate(blocks, axis=0).astype(BF16)
        r, c_ = iota((384, 128), 0), iota((384, 128), 1)
        by_row = dot_nt(one_hot(r // 16 == c_ // 4), slots).astype(BF16)
        r, c_ = iota((24, 768), 0), iota((24, 768), 1)
        tap = c_ % 128 // 16
        need = c_ // 128 + tap
        has = r % 8 + jnp.where(r < 8, -RIM, jnp.where(r < 16, RIM, RIM + ROWS))
        legal = (
            (tap < KS)
            & ((r >= 8) | (r % 8 >= ROWS - RIM))
            & (r % 8 < ROWS)
            & ((r < 16) | (r % 8 < RIM))
        )
        spread = one_hot(legal & (need == has))
        r, c_ = iota((384, 768), 0), iota((384, 768), 1)
        biga[...] = jnp.where(r % 16 == c_ % 16, dot(by_row, spread), 0.0).astype(BF16)
        r, c_ = iota((128, 24), 0), iota((128, 24), 1)
        by_own = dot(one_hot((c_ - 8 == r // 16) & (r // 16 < ROWS)), slots).astype(BF16)
        r, c_ = iota((256, 128), 0), iota((256, 128), 1)
        full = dot_nt(one_hot(c_ // 4 == 4 * (r // 64 + 1) + r % 64 // 16), by_own)
        bigb[...] = jnp.where(r % 16 == c_ % 16, full, 0.0).astype(BF16)

    def phase_spectra():
        for j in range(cols):
            tails[j] = unfold(recv1[j, :FIRST].astype(F32), lane16, OWN * me).astype(BF16)

        def half_circle(k):
            at = slice(BLOCKS * k, BLOCKS * k + BLOCKS)
            main = recv1[at].reshape(BLOCKS * MAIN, 128)
            tail = tails[at].reshape(BLOCKS * TAIL, 128)
            return jnp.concatenate([main, tail], axis=0).astype(F32)

        first, second = half_circle(0), half_circle(1)
        for parity in range(2):
            mix = first - second if parity else first + second
            spec = dot(tf[parity], mix.astype(BF16))
            real, imag = spec[:WPAD], spec[WPAD:]
            rows = slice(parity * WPAD, parity * WPAD + WPAD)
            g_real, g_imag = gt[0, rows], gt[1, rows]
            waves[parity, :WPAD] = (g_real * real + g_imag * imag).astype(BF16)
            waves[parity, WPAD:] = (g_real * imag - g_imag * real).astype(BF16)

    def phase_inverse(part):
        low, high = (0, BLOCKS * HEAD) if part == 0 else (BLOCKS * HEAD, TAB)
        even = dot(ti[0, low:high, :], waves[0])
        odd = dot(ti[1, low:high, :], waves[1])
        free = ((lane16 - OWN * me) & 127) >= 96
        for k, field in enumerate((even + odd, even - odd)):
            for j in range(BLOCKS):
                if part:
                    send2b[BLOCKS * k + j] = field[REST * j : REST * j + REST].astype(BF16)
                else:
                    at = BLOCKS * FIRST + TAIL * j
                    main = field[FIRST * j : FIRST * j + FIRST]
                    for g, piece in enumerate(fold(main, field[at : at + TAIL], free)):
                        rows = slice(TAIL * g, TAIL * g + TAIL)
                        send2[BLOCKS * k + j, rows] = piece.astype(BF16)

    def phase_stencil(half):
        if half:
            oc[RIM + ROWS :] = obr[1].astype(F32) * down_ok
        else:
            oc[0:RIM] = obr[0].astype(F32) * up_ok

        def stencil_row(i, carry):
            totals = []
            for t in range(HP // 128):
                cut = slice(128 * t, 128 * t + 128)
                total = None
                for dj in range(KS):
                    line = None
                    for di in range(KS):
                        term = kp[di, dj : dj + 1, cut] * oc[i + di, :, cut]
                        line = term if line is None else line + term
                    shift = (RIM - dj) % PAD
                    line = pltpu.roll(line, shift, 0) if shift else line
                    total = line if total is None else total + line
                totals.append(total)
            mean = sum(jnp.sum(x, axis=-1, keepdims=True) for x in totals) * (1.0 / HO)
            for t, total in enumerate(totals):
                s0[i, :, 128 * t : 128 * t + 128] = total - mean
            return carry

        lax.fori_loop(RIM * half, RIM * half + RIM, stencil_row, 0)

    def phase_atm_rim():
        row = iota((16, CH), 0)
        right, left = side_r[0, :, 2 * HP :].astype(F32), side_r[1, :, 2 * HP :].astype(F32)
        for a in range(LATS):
            x32[a, 80:96, :] = with_rim(x32[a, 80:96, :], right, left, row, a)

    def phase_unpack(part):
        if part == 0:
            for d in range(cols):
                tails2[d] = unfold(recv2[d].astype(F32), lane16, OWN * d)
        for a in range(LATS):
            for t in range(3):
                cut = slice(128 * t, 128 * t + 128)

                def gather(read, rows):
                    zonal = jnp.zeros((rows, 128), F32)
                    for d, lo, n in windows(t):
                        mask = ((lane[:rows] - (lo + OWN * a)) & 127) < n
                        zonal = jnp.where(mask, read(d), zonal)
                    return pltpu.roll(zonal, 128 - OWN * a, 1) if a else zonal

                if part == 0:
                    at = HEAD * a
                    main = gather(lambda d: recv2[d].astype(F32), FIRST)
                    mx[at : at + FIRST, cut] = x32[a, :FIRST, cut] + main
                    tail = gather(lambda d: tails2[d], TAIL)
                    mx[at + FIRST : at + HEAD, cut] = x32[a, MAIN:, cut] + tail
                else:
                    at = LATS * HEAD + REST * a
                    rest = gather(lambda d: recv2b[d].astype(F32), REST)
                    mx[at : at + REST, cut] = x32[a, FIRST:MAIN, cut] + rest

    def phase_atm(part):
        low, n = (0, HEAD) if part == 0 else (LATS * HEAD, REST)
        rows = slice(low, low + LATS * n)
        mixed = mx[rows]
        centred = mixed - jnp.mean(mixed, axis=-1, keepdims=True)
        spread = jnp.mean(centred * centred, axis=-1, keepdims=True)
        normed = (centred * lax.rsqrt(spread + 1e-05)).astype(BF16)
        inner = gelu(dot(normed, w1[...]))
        nx[rows] = (mx[rows] + dot(inner, w2[...])).astype(BF16)
        flux = None
        for a in range(LATS):
            at = low + n * a
            term = dot_nt(nx[at : at + n, :], fxt[128 * a : 128 * a + 128, :])
            flux = term if flux is None else flux + term
        if part == 0:
            flx32[...] = flux
        else:
            lower = iota((FIRST, 128), 1) < 64
            upper = jnp.concatenate([flux, flx32[FIRST:]], axis=0)
            flx[...] = jnp.where(lower, flx32[:FIRST], upper).astype(BF16)
            flr[1] = flx[...]

    def phase_atm_out():
        for t in range(3):
            cut = slice(128 * t, 128 * t + 128)
            for a in range(LATS):
                at = HEAD * a
                rest = LATS * HEAD + REST * a
                for place, first, n in (
                    (0, at, FIRST),
                    (MAIN, at + FIRST, TAIL),
                    (FIRST, rest, REST),
                ):
                    part = nx[first : first + n, cut].astype(F32)
                    st.at[t][pl.ds(a + LATS * place, n, stride=LATS), :] = part
            for l in range(LOCAL):
                ao[l, :, cut] = st[t, LATS * l : LATS * l + LATS, :].astype(BF16)

    def phase_forcing():
        low = iota((FIRST, 128), 1) < 64
        tiles = []
        for q in range(3):
            even, odd = flr[2 * q].astype(F32), flr[2 * q + 1].astype(F32)
            upper = jnp.where(low, even, pltpu.roll(odd, 64, 1))
            lower = jnp.where(low, pltpu.roll(even, 64, 1), odd)
            tiles.append(jnp.concatenate([upper, lower], axis=0).astype(BF16))
        forcing = dot(jnp.concatenate(tiles, axis=1), biga[...])
        for i in range(ROWS):
            part = forcing[:, 128 * i : 128 * i + 128]
            for dj in range(KS):
                shift = (RIM - dj) % PAD
                turned = pltpu.roll(part, shift, 0) if shift else part
                xs[PAD * i : PAD * i + PAD, 128 * dj : 128 * dj + 128] = turned.astype(BF16)

    def phase_ocean():
        rows = ROWS * PAD
        stencil = (dot(xs[...], wst[...]) + s0[...].reshape(rows, HP))[:, :HO]
        spread = jnp.mean(stencil * stencil, axis=-1, keepdims=True)
        onorm = (stencil * lax.rsqrt(spread + 1e-05)).astype(BF16)
        hidden = gelu(dot(onorm, oin[...]))
        change = dot_nt(hidden, oot[...])
        pushed = dot(xs[:, 128 * RIM : 128 * RIM + 128], fpc[...])
        lifted = (oc[RIM : RIM + ROWS].reshape(rows, HP) + pushed)[:, :HO].astype(BF16).astype(F32)
        result = lifted + change
        surface = None
        for i in range(ROWS):
            part = (result[PAD * i : PAD * i + PAD] * sea[0:PAD, i : i + 1]).astype(BF16)
            oo[i] = part[:LOCAL]
            term = dot_nt(part, sxt[128 * i : 128 * i + 128, :])
            surface = term if surface is None else surface + term
        back = dot_nt(bigb[...], jnp.concatenate([surface.astype(BF16), jnp.zeros((32, 128), BF16)], axis=0))
        for o in range(SPAN):
            main, tail = back[64 * o : 64 * o + FIRST], back[64 * o + FIRST : 64 * o + 64]
            for g, piece in enumerate(fold(main, tail, lane16 >= 96)):
                bks[o, TAIL * g : TAIL * g + TAIL] = piece.astype(BF16)

    def phase_sum():
        total = bks[0].astype(F32)
        for o in range(1, SPAN):
            total = total + bkr[o].astype(F32)
        for a in range(3):
            so[a] = total[FIELDS * a : FIELDS * a + FIELDS, :LOCAL].astype(BF16)
        so[3] = unfold(total, lane16, 0)[:, :LOCAL].astype(BF16)

    l_atm.wait()
    phase_pack()
    l_rows.wait()
    l_count.wait()
    l_weight.wait()
    phase_slots()
    l_ocean.wait()
    phase_rims()
    pl.semaphore_wait(barrier, cols - 1 + jnp.minimum(band, SPAN))

    a1 = []
    for d in partners:
        step = lax.rem(d - me + cols, cols)
        c = remote(send1.at[d], recv1.at[me], a1s.at[step], a1r.at[step], {"col": d})
        c.start()
        a1.append(c)
    sides = []
    for side, k in ((0, -1), (1, 1)):
        c = remote(side_s.at[side], side_r.at[side], sds.at[side], sdr.at[side], {"col": col_at(k)})
        c.start()
        sides.append(c)
    weights_to(1)[0]()
    for o in range(2, 6):
        slots_to(o)[0]()

    l_gain.wait()
    l_deal.wait()
    phase_gains()
    l_force.wait()
    l_kernel.wait()
    l_flux.wait()
    l_surf.wait()
    l_land.wait()
    phase_weights()
    for c in sides:
        c.wait_recv()
    phase_ocean_rim()
    phase_atm_rim()
    rim_to(1)[0]()

    l_tf.wait()
    for c in a1:
        c.wait_recv()
    phase_spectra()
    l_ti.wait()
    phase_inverse(0)
    a2 = []
    for d in partners:
        step = lax.rem(d - me + cols, cols)
        c = remote(send2.at[d], recv2.at[me], a2s.at[step], a2r.at[step], {"col": d})
        c.start()
        a2.append(c)
    phase_inverse(1)
    a3 = []
    for d in partners:
        step = lax.rem(d - me + cols, cols)
        c = remote(send2b.at[d], recv2b.at[me], a3s.at[step], a3r.at[step], {"col": d})
        c.start()
        a3.append(c)
    recv2[me] = send2[me]
    recv2b[me] = send2b[me]

    weights_to(1)[2]()
    for o in range(2, 6):
        slots_to(o)[2]()
    rim_to(0)[0]()
    weights_to(0)[0]()
    slots_to(0)[0]()
    rim_to(1)[2]()
    phase_stencil(1)
    weights_to(0)[2]()
    slots_to(0)[2]()
    phase_matrices()
    rim_to(0)[2]()
    phase_stencil(0)

    l_w1.wait()
    l_w2.wait()
    for c in a2:
        c.wait_recv()
    phase_unpack(0)
    phase_atm(0)
    for c in a3:
        c.wait_recv()
    phase_unpack(1)
    phase_atm(1)
    for o in (5, 4, 3, 2, 0):
        flux_to(o)[0]()
    phase_atm_out()

    l_oin.wait()
    l_oot.wait()
    for o in (0, 2, 3, 4, 5):
        flux_to(o)[2]()
    phase_forcing()
    phase_ocean()
    for o in (3, 2, 1):
        back_to(o)[0]()
    for o in range(1, SPAN):
        back_to(o)[2]()
    phase_sum()

    for c in a1:
        c.wait_send()
    for c in sides:
        c.wait_send()
    for c in a2 + a3:
        c.wait_send()
    for o in (0, 2, 3, 4, 5):
        slots_to(o)[1]()
        flux_to(o)[1]()
    for side in range(2):
        weights_to(side)[1]()
        rim_to(side)[1]()
    for o in range(1, SPAN):
        back_to(o)[1]()


def store(a, b, c, a_out, b_out, c_out, sems):
    copies = [
        pltpu.make_async_copy(x, y, sems.at[k])
        for k, (x, y) in enumerate(((a, a_out), (b, b_out), (c, c_out)))
    ]
    for x in copies:
        x.start()
    for x in copies:
        x.wait()


def per_device(
    bands,
    cols,
    consts,
    atm_state,
    spec_gain,
    mlp_in,
    mlp_out,
    flux_proj,
    pair_rows,
    pair_count,
    pair_weight,
    ocean_state,
    force_proj,
    depth_kernel,
    ocean_in,
    ocean_out,
    surf_proj,
    land_mask,
):
    any_spec = pl.BlockSpec(memory_space=ANY)
    vm = pltpu.VMEM
    dma = pltpu.SemaphoreType.DMA
    scratch = [
        vm((LOCAL, LATS, CH), BF16),
        vm((3, LATS * PAD, 128), F32),
        vm((LATS, PAD, CH), F32),
        vm((LATS, 3, PAD, 128), F32),
        vm((16, MAIN, 128), BF16),
        vm((16, MAIN, 128), BF16),
        vm((16, FIRST, 128), BF16),
        vm((16, FIRST, 128), BF16),
        vm((16, REST, 128), BF16),
        vm((16, REST, 128), BF16),
        vm((16, TAIL, 128), BF16),
        vm((16, TAIL, 128), F32),
        vm((2, TAB, TAB), BF16),
        vm((2, TAB, TAB), BF16),
        vm((TAB, TAB), BF16),
        vm((2, OWN, WAVES), F32),
        vm((2, 128, TAB), F32),
        vm((2, TAB, 128), F32),
        vm((CH, 768), BF16),
        vm((768, CH), BF16),
        vm((FIELDS, CH), BF16),
        vm((ROWS, LOCAL, HO), BF16),
        vm((ROWS + 2 * RIM, PAD, HP), F32),
        vm((ROWS, PAD, HP), BF16),
        vm((2, RIM, PAD, HP), BF16),
        vm((2, 16, 2 * HP + CH), BF16),
        vm((2, 16, 2 * HP + CH), BF16),
        vm((8, 8, 128), F32),
        vm((6, 3, 8, 128), F32),
        vm((8, 128), F32),
        vm((2, 8, 128), F32),
        vm((KS, KS, HO), F32),
        vm((KS, 8, HP), F32),
        vm((FIELDS, HO), BF16),
        vm((128, HP), BF16),
        vm((HO, 800), BF16),
        vm((HO, 800), BF16),
        vm((FIELDS, HO), BF16),
        vm((ROWS, LOCAL), jnp.int32),
        vm((8, 128), F32),
        vm((ROWS, PAD, HP), F32),
        vm((384, 768), BF16),
        vm((256, 128), BF16),
        vm((KS * 128, HP), BF16),
        vm((ROWS * PAD, KS * 128), BF16),
        vm((512, CH), BF16),
        vm((768, HO), BF16),
        vm((LATS * PAD, CH), F32),
        vm((LATS * PAD, CH), BF16),
        vm((HEAD, 128), F32),
        vm((FIRST, 128), BF16),
        vm((6, FIRST, 128), BF16),
        vm((SPAN, FIRST, 128), BF16),
        vm((SPAN, FIRST, 128), BF16),
        vm((2, TAB, 128), BF16),
        vm((128, 8), F32),
        pltpu.SMEM((1, SLOTS, bands), jnp.int32),
        pltpu.SMEM((1, bands), jnp.int32),
        pltpu.SMEM((ROWS, SLOTS, bands), F32),
        dma((18,)),
        dma((16,)),
        dma((16,)),
        dma((16,)),
        dma((16,)),
        dma((16,)),
        dma((16,)),
        dma((6,)),
        dma((6,)),
        dma((2,)),
        dma((2,)),
        dma((2,)),
        dma((2,)),
        dma((2,)),
        dma((2,)),
        dma((6,)),
        dma((6,)),
        dma((4,)),
        dma((4,)),
    ]
    shapes = (
        jax.ShapeDtypeStruct((LOCAL, LATS, CH), BF16),
        jax.ShapeDtypeStruct((ROWS, LOCAL, HO), BF16),
        jax.ShapeDtypeStruct((LATS, FIELDS, LOCAL), BF16),
    )
    out = pl.pallas_call(
        functools.partial(body, bands, cols),
        out_shape=tuple(vm(x.shape, x.dtype) for x in shapes),
        in_specs=[any_spec] * 18,
        out_specs=(pl.BlockSpec(memory_space=vm),) * 3,
        scratch_shapes=scratch,
        compiler_params=pltpu.CompilerParams(
            collective_id=0, has_side_effects=True, vmem_limit_bytes=56 * 1024 * 1024
        ),
    )(
        jnp.transpose(atm_state, (1, 0, 2)),
        jnp.transpose(spec_gain, (0, 2, 1)),
        mlp_in,
        mlp_out,
        jnp.transpose(flux_proj),
        jnp.transpose(pair_rows, (1, 2, 0)),
        jnp.transpose(pair_count),
        jnp.transpose(pair_weight, (0, 2, 1)),
        ocean_state,
        force_proj,
        depth_kernel,
        ocean_in,
        jnp.transpose(ocean_out),
        jnp.transpose(surf_proj),
        land_mask,
        *consts,
    )
    out = pl.pallas_call(
        store,
        out_shape=shapes,
        in_specs=[pl.BlockSpec(memory_space=vm)] * 3,
        out_specs=(any_spec,) * 3,
        scratch_shapes=[dma((3,))],
    )(*[pltpu.with_memory_space_constraint(x, vm) for x in out])
    return (
        jnp.transpose(out[0], (1, 0, 2)),
        out[1],
        jnp.transpose(out[2], (0, 2, 1)),
    )


def solution(mesh):
    placed = (
        P("band", "col", None),
        P(None, None, "col"),
        P(),
        P(),
        P(),
        P(None, "band", None),
        P(None, "band"),
        P("band", None, None),
        P("band", "col", None),
        P(),
        P(),
        P(),
        P(),
        P(),
        P("band", "col"),
    )
    consts = tables()
    step = functools.partial(
        per_device, mesh.shape["band"], mesh.shape["col"], [jnp.asarray(t) for t in consts]
    )
    return jax.shard_map(
        step,
        mesh=mesh,
        in_specs=placed,
        out_specs=(P("band", "col", None), P("band", "col", None), P("band", "col", None)),
        check_vma=False,
    )
```

```python
import functools

import jax
import jax.numpy as jnp
import numpy as np
from jax import lax
from jax.experimental import pallas as pl
from jax.experimental.pallas import tpu as pltpu
from jax.sharding import PartitionSpec as P

F32 = jnp.float32
BF16 = jnp.bfloat16
MESH = pl.DeviceIdType.MESH
ANY = pl.ANY

SPAN = 4
LATS = 4
SLOTS = 4
LON = 1440
WAVES = 720
LOCAL = 90
PAD = 96
RIM = 3
MAIN = 80
TAIL = PAD - MAIN
FIRST = 48
REST = MAIN - FIRST
HEAD = FIRST + TAIL
KS = 7
CH = 384
OWN = 24
HALF = LON // 2
BLOCKS = 8
TAB = BLOCKS * PAD
WPAD = TAB // 2
ROWS = 6
HO = 200
HP = 256
FIELDS = 16
NT = (((1,), (1,)), ((), ()))


def tables():
    block = np.arange(BLOCKS)[:, None]

    def places(*spans):
        pieces = [(block * LON // 16 + 0 * np.arange(a, b), np.arange(a, b) + 0 * block) for a, b in spans]
        start = np.concatenate([p[0].reshape(-1) for p in pieces])
        return start, np.concatenate([p[1].reshape(-1) for p in pieces])

    start, place = places((0, MAIN), (MAIN, PAD))
    inside = place < LOCAL
    lon_in = start + place
    start, place = places((0, FIRST), (MAIN, PAD), (FIRST, MAIN))
    lon_out = start + np.where(place < LOCAL + RIM, place, place - PAD)
    forward = np.zeros((2, TAB, TAB), np.float64)
    inverse = np.zeros((2, TAB, TAB), np.float64)
    deal = np.zeros((2 * WPAD, TAB), np.float64)
    count = WAVES // 2
    for parity in range(2):
        wave = 2 * np.arange(count) + parity
        angle = 2 * np.pi * (wave[:, None] * lon_in[None] % LON) / LON
        forward[parity, :count] = np.cos(angle) * inside
        forward[parity, WPAD : WPAD + count] = np.sin(angle) * inside
        angle = 2 * np.pi * (lon_out[:, None] * wave[None] % LON) / LON
        inverse[parity, :, :count] = np.cos(angle)
        inverse[parity, :, WPAD : WPAD + count] = np.sin(angle)
        deal[parity * WPAD + np.arange(count), wave] = 1.0
    return [t.astype(np.float32).astype(jnp.bfloat16) for t in (forward, inverse, deal)]


def iota(shape, axis):
    return lax.broadcasted_iota(jnp.int32, shape, axis)


def one_hot(condition):
    return jnp.where(condition, 1.0, 0.0).astype(BF16)


def dot(a, b):
    return jnp.dot(a, b, preferred_element_type=F32)


def dot_nt(a, b):
    return lax.dot_general(a, b, NT, preferred_element_type=F32)


def gelu(x):
    half = 0.5 * x
    inner = x * (0.7978845608028654 + 0.035677408136300125 * (x * x))
    return (half + half * jnp.tanh(inner)).astype(BF16)


def fold(main, tail, free):
    return [
        jnp.where(free, pltpu.roll(tail, 96 - 32 * g, 1), main[TAIL * g : TAIL * g + TAIL])
        for g in range(3)
    ]


def unfold(main, lane, first):
    out = None
    for g in range(3):
        part = pltpu.roll(main[TAIL * g : TAIL * g + TAIL], 32 + 32 * g, 1)
        out = part if out is None else jnp.where(((lane - first) & 127) // 32 == g, part, out)
    return out


def windows(tile):
    out = []
    for d in range(16):
        lo, hi = max(OWN * d, 128 * tile), min(OWN * d + OWN, 128 * tile + 128)
        if lo < hi:
            out.append((d, lo, hi - lo))
    return out


def body(
    bands,
    cols,
    atm,
    gain,
    w_in,
    w_out,
    flux_t,
    pair_rows,
    pair_count,
    pair_weight,
    ocean,
    force,
    kernel_w,
    o_in,
    o_out_t,
    surf_t,
    land,
    tab_f,
    tab_i,
    deal,
    ao,
    oo,
    so,
    xv,
    st,
    x32,
    rolled,
    send1,
    recv1,
    send2,
    recv2,
    send2b,
    recv2b,
    tails,
    tails2,
    tf,
    ti,
    dl,
    gv,
    gx,
    gt,
    w1,
    w2,
    fpt,
    ocv,
    oc,
    obs,
    obr,
    side_s,
    side_r,
    sel,
    selr,
    wown,
    wr,
    kv,
    kp,
    fp,
    fpc,
    oin,
    oot,
    spt,
    lm,
    lmp,
    s0,
    biga,
    bigb,
    wst,
    xs,
    fxt,
    sxt,
    mx,
    nx,
    flx,
    flr,
    bks,
    bkr,
    waves,
    sea,
    p_rows,
    p_count,
    p_weight,
    ld,
    a1s,
    a1r,
    a2s,
    a2r,
    a3s,
    a3r,
    sls,
    slr,
    ws,
    wrs,
    sds,
    sdr,
    obss,
    obrs,
    fls,
    flrs,
    bss,
    brs,
):
    me = lax.axis_index("col")
    band = lax.axis_index("band")
    up_ok = jnp.where(band > 0, 1.0, 0.0).astype(F32)
    down_ok = jnp.where(band < bands - 1, 1.0, 0.0).astype(F32)

    def col_at(k):
        return lax.rem(me + k + cols, cols)

    def away(k):
        return min(k // 4, 4 - k // 4) + min(k % 4, 4 - k % 4)

    partners = [
        lax.rem(me // 4 + k // 4, 4) * 4 + lax.rem(me % 4 + k % 4, 4)
        for k in sorted(range(1, cols), key=lambda k: -away(k))
    ]

    def exists(k):
        return band >= -k if k < 0 else band < bands - k

    def load(src, dst, k):
        c = pltpu.make_async_copy(src, dst, ld.at[k])
        c.start()
        return c

    l_atm = load(atm, xv, 0)
    barrier = pltpu.get_barrier_semaphore()
    for d in partners:
        pl.semaphore_signal(barrier, inc=1, device_id={"col": d}, device_id_type=MESH)
    for k in range(1, SPAN + 1):

        @pl.when(exists(k))
        def _():
            pl.semaphore_signal(barrier, inc=1, device_id={"band": band + k}, device_id_type=MESH)

    l_rows = load(pair_rows, p_rows, 15)
    l_count = load(pair_count, p_count, 16)
    l_weight = load(pair_weight, p_weight, 17)
    l_ocean = load(ocean, ocv, 1)
    l_force = load(force, fp, 2)
    l_kernel = load(kernel_w, kv, 3)
    l_gain = load(gain, gv, 4)
    l_deal = load(deal, dl, 5)
    l_tf = load(tab_f, tf, 6)
    l_flux = load(flux_t, fpt, 7)
    l_surf = load(surf_t, spt, 8)
    l_land = load(land, lm, 9)
    l_ti = load(tab_i, ti, 10)
    l_w1 = load(w_in, w1, 11)
    l_w2 = load(w_out, w2, 12)
    l_oin = load(o_in, oin, 13)
    l_oot = load(o_out_t, oot, 14)

    def remote(src, dst, send_sem, recv_sem, device):
        return pltpu.make_async_remote_copy(
            src_ref=src,
            dst_ref=dst,
            send_sem=send_sem,
            recv_sem=recv_sem,
            device_id=device,
            device_id_type=MESH,
        )

    def to_band(k, src, dst, send_sem, recv_sem):
        def make():
            return remote(src, dst, send_sem, recv_sem, {"band": band + k})

        def start():
            pl.when(exists(k))(lambda: make().start())

        def wait_send():
            pl.when(exists(k))(lambda: make().wait_send())

        def wait_recv():
            pl.when(exists(-k))(lambda: make().wait_recv())

        return start, wait_send, wait_recv

    def slots_to(o):
        return to_band(1 - o, sel.at[pl.ds(5 - o, 3)], selr.at[o], sls.at[o], slr.at[o])

    def weights_to(side):
        return to_band(1 - 2 * side, wown, wr.at[side], ws.at[side], wrs.at[side])

    def rim_to(side):
        src = obs.at[pl.ds(RIM * (1 - side), RIM)]
        return to_band(1 - 2 * side, src, obr.at[side], obss.at[side], obrs.at[side])

    def flux_to(o):
        return to_band(1 - o, flx, flr.at[o], fls.at[o], flrs.at[o])

    def back_to(o):
        return to_band(o, bks.at[o], bkr.at[o], bss.at[o], brs.at[o])

    lane = iota((PAD, 128), 1)
    lane16 = iota((TAIL, 128), 1)

    def phase_pack():
        st[:, LATS * LOCAL :, :] = jnp.zeros((3, LATS * (PAD - LOCAL), 128), F32)
        for l in range(LOCAL):
            for t in range(3):
                cut = slice(128 * t, 128 * t + 128)
                st[t, LATS * l : LATS * l + LATS, :] = xv[l, :, cut].astype(F32)
        for a in range(LATS):
            for t in range(3):
                part = st.at[t][pl.ds(a, PAD, stride=LATS), :]
                x32[a, :, 128 * t : 128 * t + 128] = part
                rolled[a, t] = pltpu.roll(part, OWN * a, 1) if a else part
        for d in range(cols):
            out = jnp.zeros((PAD, 128), F32)
            for t in range(3):
                for e, lo, n in windows(t):
                    if e == d:
                        for a in range(LATS):
                            mask = ((lane - (lo + OWN * a)) & 127) < n
                            out = jnp.where(mask, rolled[a, t], out)
            free = ((lane16 - OWN * d) & 127) >= 96
            for g, piece in enumerate(fold(out, out[MAIN:], free)):
                send1[d, TAIL * g : TAIL * g + TAIL] = piece.astype(BF16)
            send1[d, FIRST:] = out[FIRST:MAIN].astype(BF16)
        recv1[me] = send1[me]

    def phase_slots():
        row8 = iota((8, 128), 0)
        lane8 = iota((8, 128), 1)
        zero8 = jnp.zeros((8, 128), F32)
        for q in (0, 1, 6, 7):
            sel[q] = zero8
        for k in range(SPAN):
            other = band - k
            at = jnp.maximum(other, 0)
            used = jnp.where(other >= 0, p_count[0, at], 0)
            vec = zero8
            for p in range(SLOTS):
                target = jnp.where(p < used, SLOTS * p_rows[0, p, at] + p, -1)
                vec = jnp.where(lane8 == target, 1.0, vec)
            sel[5 - k] = vec
        vec = zero8
        for o in range(SPAN):
            at = jnp.minimum(band + o, bands - 1)
            for p in range(SLOTS):
                here = (lane8 // 16 == o) & (lane8 % SLOTS == p)
                for i in range(ROWS):
                    vec = jnp.where(here & (row8 == i), p_weight[i, p, at], vec)
        wown[...] = vec
        selr[1] = sel[4:7]
        for o in range(2, 6):

            @pl.when(jnp.logical_not(exists(o - 1)))
            def _():
                selr[o] = jnp.zeros((3, 8, 128), F32)
                flr[o] = jnp.zeros((FIRST, 128), BF16)

        @pl.when(jnp.logical_not(exists(-1)))
        def _():
            selr[0] = jnp.zeros((3, 8, 128), F32)
            flr[0] = jnp.zeros((FIRST, 128), BF16)
            wr[0] = zero8
            obr[0] = jnp.zeros((RIM, PAD, HP), BF16)

        @pl.when(jnp.logical_not(exists(1)))
        def _():
            wr[1] = zero8
            obr[1] = jnp.zeros((RIM, PAD, HP), BF16)

        for o in range(1, SPAN):

            @pl.when(jnp.logical_not(exists(-o)))
            def _():
                bkr[o] = jnp.zeros((FIRST, 128), BF16)

    def phase_rims():
        oc[RIM : RIM + ROWS] = jnp.zeros((ROWS, PAD, HP), F32)
        oc[RIM : RIM + ROWS, 0:LOCAL, 0:HO] = ocv[...].astype(F32)
        row = iota((16, HP), 0)
        for b in range(2):
            for side in range(2):
                out = jnp.zeros((16, HP), F32)
                for q in range(3):
                    i = RIM + 3 * b + q
                    part = oc[i, 0:16, :] if side == 0 else oc[i, 80:96, :]
                    shift = (RIM * q - (0 if side == 0 else 7)) % 16
                    part = pltpu.roll(part, shift, 0) if shift else part
                    out = jnp.where((row >= RIM * q) & (row < RIM * q + RIM), part, out)
                side_s[side, :, HP * b : HP * b + HP] = out.astype(BF16)
        row = iota((16, CH), 0)
        for side in range(2):
            out = jnp.zeros((16, CH), F32)
            for a in range(LATS):
                part = x32[a, 0:16, :] if side == 0 else x32[a, 80:96, :]
                shift = (RIM * a - (0 if side == 0 else 7)) % 16
                part = pltpu.roll(part, shift, 0) if shift else part
                out = jnp.where((row >= RIM * a) & (row < RIM * a + RIM), part, out)
            side_s[side, :, 2 * HP :] = out.astype(BF16)

    def phase_gains():
        gx[...] = jnp.zeros(gx.shape, F32)
        for a in range(LATS):
            for q in range(OWN // 8):
                row = pl.multiple_of(lax.rem(OWN * (me + a) + 8 * q, 128), 8)
                gx[:, pl.ds(row, 8), 0:WAVES] = gv[:, 8 * q : 8 * q + 8, :] * (2.0 / LON)
        for part in range(2):
            g = gx[part]
            high = g.astype(BF16)
            low = (g - high.astype(F32)).astype(BF16)
            both = dot_nt(dl[...], jnp.concatenate([high, low], axis=0))
            gt[part] = both[:, :128] + both[:, 128:]

    def phase_weights():
        kp[...] = jnp.zeros(kp.shape, F32)
        kp[:, 0:KS, 0:HO] = kv[...]
        f32_force = fp[...].astype(F32)
        wst[...] = jnp.zeros(wst.shape, BF16)
        fpc[...] = jnp.zeros(fpc.shape, BF16)
        for dj in range(KS):
            for di in range(KS):
                at = 128 * dj + FIELDS * di
                weight = f32_force * kp[di, dj : dj + 1, 0:HO]
                weight = weight - jnp.mean(weight, axis=-1, keepdims=True)
                wst[at : at + FIELDS, 0:HO] = weight.astype(BF16)
        fpc[FIELDS * RIM : FIELDS * RIM + FIELDS, 0:HO] = fp[...]

        r, f = iota((512, FIELDS), 0), iota((512, FIELDS), 1)
        spread = one_hot((r % 64 // 16 == r // 128) & (r % 16 == f))
        fxt[...] = dot(spread, fpt[...]).astype(BF16)
        r, f = iota((768, FIELDS), 0), iota((768, FIELDS), 1)
        spread = one_hot((r % 128 // 16 == r // 128) & (r % 16 == f))
        sxt[...] = dot(spread, spt[...]).astype(BF16)
        lmp[...] = jnp.zeros(lmp.shape, F32)
        lmp[0:ROWS, 0:LOCAL] = lm[...].astype(F32)
        r, c_ = iota((128, 128), 0), iota((128, 128), 1)
        sea[...] = dot_nt(one_hot(r == c_), lmp[...].astype(BF16))

    def with_rim(own, right, left, row, k):
        right = pltpu.roll(right, (10 - RIM * k) % 16, 0)
        left = pltpu.roll(left, (13 - RIM * k) % 16, 0)
        return jnp.where(row < 10, own, jnp.where(row < 13, right, left))

    def phase_ocean_rim():
        row = iota((16, HP), 0)
        for b in range(2):
            cut = slice(HP * b, HP * b + HP)
            right, left = side_r[0, :, cut].astype(F32), side_r[1, :, cut].astype(F32)
            for q in range(3):
                i = RIM + 3 * b + q
                oc[i, 80:96, :] = with_rim(oc[i, 80:96, :], right, left, row, q)
        obs[...] = oc[RIM : RIM + ROWS].astype(BF16)

    def phase_matrices():
        blocks = []
        for b in range(3):
            chosen = selr[0, b]
            for o in range(1, 6):
                chosen = chosen + pltpu.roll(selr[o, b], 16 * o, 1)
            if b == 0:
                blocks.append(wr[0] * chosen * up_ok)
            elif b == 1:
                blocks.append(pltpu.roll(wown[...], 16, 1) * chosen)
            else:
                blocks.append(pltpu.roll(wr[1], 32, 1) * chosen * down_ok)
        slots = jnp.concatenate(blocks, axis=0).astype(BF16)
        r, c_ = iota((384, 128), 0), iota((384, 128), 1)
        by_row = dot_nt(one_hot(r // 16 == c_ // 4), slots).astype(BF16)
        r, c_ = iota((24, 768), 0), iota((24, 768), 1)
        tap = c_ % 128 // 16
        need = c_ // 128 + tap
        has = r % 8 + jnp.where(r < 8, -RIM, jnp.where(r < 16, RIM, RIM + ROWS))
        legal = (
            (tap < KS)
            & ((r >= 8) | (r % 8 >= ROWS - RIM))
            & (r % 8 < ROWS)
            & ((r < 16) | (r % 8 < RIM))
        )
        spread = one_hot(legal & (need == has))
        r, c_ = iota((384, 768), 0), iota((384, 768), 1)
        biga[...] = jnp.where(r % 16 == c_ % 16, dot(by_row, spread), 0.0).astype(BF16)
        r, c_ = iota((128, 24), 0), iota((128, 24), 1)
        by_own = dot(one_hot((c_ - 8 == r // 16) & (r // 16 < ROWS)), slots).astype(BF16)
        r, c_ = iota((256, 128), 0), iota((256, 128), 1)
        full = dot_nt(one_hot(c_ // 4 == 4 * (r // 64 + 1) + r % 64 // 16), by_own)
        bigb[...] = jnp.where(r % 16 == c_ % 16, full, 0.0).astype(BF16)

    def phase_spectra():
        for j in range(cols):
            tails[j] = unfold(recv1[j, :FIRST].astype(F32), lane16, OWN * me).astype(BF16)

        def half_circle(k):
            at = slice(BLOCKS * k, BLOCKS * k + BLOCKS)
            main = recv1[at].reshape(BLOCKS * MAIN, 128)
            tail = tails[at].reshape(BLOCKS * TAIL, 128)
            return jnp.concatenate([main, tail], axis=0).astype(F32)

        first, second = half_circle(0), half_circle(1)
        for parity in range(2):
            mix = first - second if parity else first + second
            spec = dot(tf[parity], mix.astype(BF16))
            real, imag = spec[:WPAD], spec[WPAD:]
            rows = slice(parity * WPAD, parity * WPAD + WPAD)
            g_real, g_imag = gt[0, rows], gt[1, rows]
            waves[parity, :WPAD] = (g_real * real + g_imag * imag).astype(BF16)
            waves[parity, WPAD:] = (g_real * imag - g_imag * real).astype(BF16)

    def phase_inverse(part):
        low, high = (0, BLOCKS * HEAD) if part == 0 else (BLOCKS * HEAD, TAB)
        even = dot(ti[0, low:high, :], waves[0])
        odd = dot(ti[1, low:high, :], waves[1])
        free = ((lane16 - OWN * me) & 127) >= 96
        for k, field in enumerate((even + odd, even - odd)):
            for j in range(BLOCKS):
                if part:
                    send2b[BLOCKS * k + j] = field[REST * j : REST * j + REST].astype(BF16)
                else:
                    at = BLOCKS * FIRST + TAIL * j
                    main = field[FIRST * j : FIRST * j + FIRST]
                    for g, piece in enumerate(fold(main, field[at : at + TAIL], free)):
                        rows = slice(TAIL * g, TAIL * g + TAIL)
                        send2[BLOCKS * k + j, rows] = piece.astype(BF16)

    def phase_stencil(half):
        if half:
            oc[RIM + ROWS :] = obr[1].astype(F32) * down_ok
        else:
            oc[0:RIM] = obr[0].astype(F32) * up_ok

        def stencil_row(i, carry):
            totals = []
            for t in range(HP // 128):
                cut = slice(128 * t, 128 * t + 128)
                total = None
                for dj in range(KS):
                    line = None
                    for di in range(KS):
                        term = kp[di, dj : dj + 1, cut] * oc[i + di, :, cut]
                        line = term if line is None else line + term
                    shift = (RIM - dj) % PAD
                    line = pltpu.roll(line, shift, 0) if shift else line
                    total = line if total is None else total + line
                totals.append(total)
            mean = sum(jnp.sum(x, axis=-1, keepdims=True) for x in totals) * (1.0 / HO)
            for t, total in enumerate(totals):
                s0[i, :, 128 * t : 128 * t + 128] = total - mean
            return carry

        lax.fori_loop(RIM * half, RIM * half + RIM, stencil_row, 0)

    def phase_atm_rim():
        row = iota((16, CH), 0)
        right, left = side_r[0, :, 2 * HP :].astype(F32), side_r[1, :, 2 * HP :].astype(F32)
        for a in range(LATS):
            x32[a, 80:96, :] = with_rim(x32[a, 80:96, :], right, left, row, a)

    def phase_unpack(part):
        if part == 0:
            for d in range(cols):
                tails2[d] = unfold(recv2[d].astype(F32), lane16, OWN * d)
        for a in range(LATS):
            for t in range(3):
                cut = slice(128 * t, 128 * t + 128)

                def gather(read, rows):
                    zonal = jnp.zeros((rows, 128), F32)
                    for d, lo, n in windows(t):
                        mask = ((lane[:rows] - (lo + OWN * a)) & 127) < n
                        zonal = jnp.where(mask, read(d), zonal)
                    return pltpu.roll(zonal, 128 - OWN * a, 1) if a else zonal

                if part == 0:
                    at = HEAD * a
                    main = gather(lambda d: recv2[d].astype(F32), FIRST)
                    mx[at : at + FIRST, cut] = x32[a, :FIRST, cut] + main
                    tail = gather(lambda d: tails2[d], TAIL)
                    mx[at + FIRST : at + HEAD, cut] = x32[a, MAIN:, cut] + tail
                else:
                    at = LATS * HEAD + REST * a
                    rest = gather(lambda d: recv2b[d].astype(F32), REST)
                    mx[at : at + REST, cut] = x32[a, FIRST:MAIN, cut] + rest

    def phase_atm():
        mixed = mx[...]
        centred = mixed - jnp.mean(mixed, axis=-1, keepdims=True)
        spread = jnp.mean(centred * centred, axis=-1, keepdims=True)
        normed = (centred * lax.rsqrt(spread + 1e-05)).astype(BF16)
        inner = gelu(dot(normed, w1[...]))
        nx[...] = (mx[...] + dot(inner, w2[...])).astype(BF16)
        flux = None
        for a in range(LATS):
            near, rest = HEAD * a, LATS * HEAD + REST * a
            rows = jnp.concatenate([nx[near : near + HEAD], nx[rest : rest + REST]], axis=0)
            term = dot_nt(rows, fxt[128 * a : 128 * a + 128, :])
            flux = term if flux is None else flux + term
        lower = iota((FIRST, 128), 1) < 64
        upper = jnp.concatenate([flux[HEAD:], flux[FIRST:HEAD]], axis=0)
        flx[...] = jnp.where(lower, flux[:FIRST], upper).astype(BF16)
        flr[1] = flx[...]

    def phase_atm_out():
        for t in range(3):
            cut = slice(128 * t, 128 * t + 128)
            for a in range(LATS):
                at = HEAD * a
                rest = LATS * HEAD + REST * a
                for place, first, n in (
                    (0, at, FIRST),
                    (MAIN, at + FIRST, TAIL),
                    (FIRST, rest, REST),
                ):
                    part = nx[first : first + n, cut].astype(F32)
                    st.at[t][pl.ds(a + LATS * place, n, stride=LATS), :] = part
            for l in range(LOCAL):
                ao[l, :, cut] = st[t, LATS * l : LATS * l + LATS, :].astype(BF16)

    def phase_forcing():
        low = iota((FIRST, 128), 1) < 64
        tiles = []
        for q in range(3):
            even, odd = flr[2 * q].astype(F32), flr[2 * q + 1].astype(F32)
            upper = jnp.where(low, even, pltpu.roll(odd, 64, 1))
            lower = jnp.where(low, pltpu.roll(even, 64, 1), odd)
            tiles.append(jnp.concatenate([upper, lower], axis=0).astype(BF16))
        forcing = dot(jnp.concatenate(tiles, axis=1), biga[...])
        for i in range(ROWS):
            part = forcing[:, 128 * i : 128 * i + 128]
            for dj in range(KS):
                shift = (RIM - dj) % PAD
                turned = pltpu.roll(part, shift, 0) if shift else part
                xs[PAD * i : PAD * i + PAD, 128 * dj : 128 * dj + 128] = turned.astype(BF16)

    def phase_ocean():
        rows = ROWS * PAD
        stencil = (dot(xs[...], wst[...]) + s0[...].reshape(rows, HP))[:, :HO]
        spread = jnp.mean(stencil * stencil, axis=-1, keepdims=True)
        onorm = (stencil * lax.rsqrt(spread + 1e-05)).astype(BF16)
        hidden = gelu(dot(onorm, oin[...]))
        change = dot_nt(hidden, oot[...])
        pushed = dot(xs[:, 128 * RIM : 128 * RIM + 128], fpc[...])
        lifted = (oc[RIM : RIM + ROWS].reshape(rows, HP) + pushed)[:, :HO].astype(BF16).astype(F32)
        result = lifted + change
        surface = None
        for i in range(ROWS):
            part = (result[PAD * i : PAD * i + PAD] * sea[0:PAD, i : i + 1]).astype(BF16)
            oo[i] = part[:LOCAL]
            term = dot_nt(part, sxt[128 * i : 128 * i + 128, :])
            surface = term if surface is None else surface + term
        back = dot_nt(bigb[...], jnp.concatenate([surface.astype(BF16), jnp.zeros((32, 128), BF16)], axis=0))
        for o in range(SPAN):
            main, tail = back[64 * o : 64 * o + FIRST], back[64 * o + FIRST : 64 * o + 64]
            for g, piece in enumerate(fold(main, tail, lane16 >= 96)):
                bks[o, TAIL * g : TAIL * g + TAIL] = piece.astype(BF16)

    def phase_sum():
        total = bks[0].astype(F32)
        for o in range(1, SPAN):
            total = total + bkr[o].astype(F32)
        for a in range(3):
            so[a] = total[FIELDS * a : FIELDS * a + FIELDS, :LOCAL].astype(BF16)
        so[3] = unfold(total, lane16, 0)[:, :LOCAL].astype(BF16)

    l_atm.wait()
    phase_pack()
    pl.semaphore_wait(barrier, cols - 1 + jnp.minimum(band, SPAN))

    a1 = []
    for d in partners:
        step = lax.rem(d - me + cols, cols)
        c = remote(send1.at[d], recv1.at[me], a1s.at[step], a1r.at[step], {"col": d})
        c.start()
        a1.append(c)
    l_rows.wait()
    l_count.wait()
    l_weight.wait()
    phase_slots()
    weights_to(1)[0]()
    for o in range(2, 6):
        slots_to(o)[0]()
    l_ocean.wait()
    phase_rims()
    sides = []
    for side, k in ((0, -1), (1, 1)):
        c = remote(side_s.at[side], side_r.at[side], sds.at[side], sdr.at[side], {"col": col_at(k)})
        c.start()
        sides.append(c)
    l_gain.wait()
    l_deal.wait()
    phase_gains()
    l_force.wait()
    l_kernel.wait()
    l_flux.wait()
    l_surf.wait()
    l_land.wait()
    phase_weights()
    for c in sides:
        c.wait_recv()
    phase_ocean_rim()
    rim_to(1)[0]()
    weights_to(1)[2]()
    rim_to(0)[0]()
    weights_to(0)[0]()
    slots_to(0)[0]()
    phase_atm_rim()

    l_tf.wait()
    for c in a1:
        c.wait_recv()
    phase_spectra()
    l_ti.wait()
    phase_inverse(0)
    a2 = []
    for d in partners:
        step = lax.rem(d - me + cols, cols)
        c = remote(send2.at[d], recv2.at[me], a2s.at[step], a2r.at[step], {"col": d})
        c.start()
        a2.append(c)
    phase_inverse(1)
    a3 = []
    for d in partners:
        step = lax.rem(d - me + cols, cols)
        c = remote(send2b.at[d], recv2b.at[me], a3s.at[step], a3r.at[step], {"col": d})
        c.start()
        a3.append(c)
    recv2[me] = send2[me]
    recv2b[me] = send2b[me]

    rim_to(1)[2]()
    phase_stencil(1)
    rim_to(0)[2]()
    phase_stencil(0)

    l_w1.wait()
    l_w2.wait()
    for c in a2:
        c.wait_recv()
    phase_unpack(0)
    for c in a3:
        c.wait_recv()
    phase_unpack(1)
    phase_atm()
    for o in (5, 4, 3, 2, 0):
        flux_to(o)[0]()
    phase_atm_out()
    for o in (0, 2, 3, 4, 5):
        slots_to(o)[2]()
    weights_to(0)[2]()
    phase_matrices()

    l_oin.wait()
    l_oot.wait()
    for o in (0, 2, 3, 4, 5):
        flux_to(o)[2]()
    phase_forcing()
    phase_ocean()
    for o in (3, 2, 1):
        back_to(o)[0]()
    for o in range(1, SPAN):
        back_to(o)[2]()
    phase_sum()

    for c in a1:
        c.wait_send()
    for c in sides:
        c.wait_send()
    for c in a2 + a3:
        c.wait_send()
    for o in (0, 2, 3, 4, 5):
        slots_to(o)[1]()
        flux_to(o)[1]()
    for side in range(2):
        weights_to(side)[1]()
        rim_to(side)[1]()
    for o in range(1, SPAN):
        back_to(o)[1]()


def store(a, b, c, a_out, b_out, c_out, sems):
    copies = [
        pltpu.make_async_copy(x, y, sems.at[k])
        for k, (x, y) in enumerate(((a, a_out), (b, b_out), (c, c_out)))
    ]
    for x in copies:
        x.start()
    for x in copies:
        x.wait()


def per_device(
    bands,
    cols,
    consts,
    atm_state,
    spec_gain,
    mlp_in,
    mlp_out,
    flux_proj,
    pair_rows,
    pair_count,
    pair_weight,
    ocean_state,
    force_proj,
    depth_kernel,
    ocean_in,
    ocean_out,
    surf_proj,
    land_mask,
):
    any_spec = pl.BlockSpec(memory_space=ANY)
    vm = pltpu.VMEM
    dma = pltpu.SemaphoreType.DMA
    scratch = [
        vm((LOCAL, LATS, CH), BF16),
        vm((3, LATS * PAD, 128), F32),
        vm((LATS, PAD, CH), F32),
        vm((LATS, 3, PAD, 128), F32),
        vm((16, MAIN, 128), BF16),
        vm((16, MAIN, 128), BF16),
        vm((16, FIRST, 128), BF16),
        vm((16, FIRST, 128), BF16),
        vm((16, REST, 128), BF16),
        vm((16, REST, 128), BF16),
        vm((16, TAIL, 128), BF16),
        vm((16, TAIL, 128), F32),
        vm((2, TAB, TAB), BF16),
        vm((2, TAB, TAB), BF16),
        vm((TAB, TAB), BF16),
        vm((2, OWN, WAVES), F32),
        vm((2, 128, TAB), F32),
        vm((2, TAB, 128), F32),
        vm((CH, 768), BF16),
        vm((768, CH), BF16),
        vm((FIELDS, CH), BF16),
        vm((ROWS, LOCAL, HO), BF16),
        vm((ROWS + 2 * RIM, PAD, HP), F32),
        vm((ROWS, PAD, HP), BF16),
        vm((2, RIM, PAD, HP), BF16),
        vm((2, 16, 2 * HP + CH), BF16),
        vm((2, 16, 2 * HP + CH), BF16),
        vm((8, 8, 128), F32),
        vm((6, 3, 8, 128), F32),
        vm((8, 128), F32),
        vm((2, 8, 128), F32),
        vm((KS, KS, HO), F32),
        vm((KS, 8, HP), F32),
        vm((FIELDS, HO), BF16),
        vm((128, HP), BF16),
        vm((HO, 800), BF16),
        vm((HO, 800), BF16),
        vm((FIELDS, HO), BF16),
        vm((ROWS, LOCAL), jnp.int32),
        vm((8, 128), F32),
        vm((ROWS, PAD, HP), F32),
        vm((384, 768), BF16),
        vm((256, 128), BF16),
        vm((KS * 128, HP), BF16),
        vm((ROWS * PAD, KS * 128), BF16),
        vm((512, CH), BF16),
        vm((768, HO), BF16),
        vm((LATS * PAD, CH), F32),
        vm((LATS * PAD, CH), BF16),
        vm((FIRST, 128), BF16),
        vm((6, FIRST, 128), BF16),
        vm((SPAN, FIRST, 128), BF16),
        vm((SPAN, FIRST, 128), BF16),
        vm((2, TAB, 128), BF16),
        vm((128, 8), F32),
        pltpu.SMEM((1, SLOTS, bands), jnp.int32),
        pltpu.SMEM((1, bands), jnp.int32),
        pltpu.SMEM((ROWS, SLOTS, bands), F32),
        dma((18,)),
        dma((16,)),
        dma((16,)),
        dma((16,)),
        dma((16,)),
        dma((16,)),
        dma((16,)),
        dma((6,)),
        dma((6,)),
        dma((2,)),
        dma((2,)),
        dma((2,)),
        dma((2,)),
        dma((2,)),
        dma((2,)),
        dma((6,)),
        dma((6,)),
        dma((4,)),
        dma((4,)),
    ]
    shapes = (
        jax.ShapeDtypeStruct((LOCAL, LATS, CH), BF16),
        jax.ShapeDtypeStruct((ROWS, LOCAL, HO), BF16),
        jax.ShapeDtypeStruct((LATS, FIELDS, LOCAL), BF16),
    )
    out = pl.pallas_call(
        functools.partial(body, bands, cols),
        out_shape=tuple(vm(x.shape, x.dtype) for x in shapes),
        in_specs=[any_spec] * 18,
        out_specs=(pl.BlockSpec(memory_space=vm),) * 3,
        scratch_shapes=scratch,
        compiler_params=pltpu.CompilerParams(
            collective_id=0, has_side_effects=True, vmem_limit_bytes=56 * 1024 * 1024
        ),
    )(
        jnp.transpose(atm_state, (1, 0, 2)),
        jnp.transpose(spec_gain, (0, 2, 1)),
        mlp_in,
        mlp_out,
        jnp.transpose(flux_proj),
        jnp.transpose(pair_rows, (1, 2, 0)),
        jnp.transpose(pair_count),
        jnp.transpose(pair_weight, (0, 2, 1)),
        ocean_state,
        force_proj,
        depth_kernel,
        ocean_in,
        jnp.transpose(ocean_out),
        jnp.transpose(surf_proj),
        land_mask,
        *consts,
    )
    out = pl.pallas_call(
        store,
        out_shape=shapes,
        in_specs=[pl.BlockSpec(memory_space=vm)] * 3,
        out_specs=(any_spec,) * 3,
        scratch_shapes=[dma((3,))],
    )(*[pltpu.with_memory_space_constraint(x, vm) for x in out])
    return (
        jnp.transpose(out[0], (1, 0, 2)),
        out[1],
        jnp.transpose(out[2], (0, 2, 1)),
    )


def solution(mesh):
    placed = (
        P("band", "col", None),
        P(None, None, "col"),
        P(),
        P(),
        P(),
        P(None, "band", None),
        P(None, "band"),
        P("band", None, None),
        P("band", "col", None),
        P(),
        P(),
        P(),
        P(),
        P(),
        P("band", "col"),
    )
    consts = tables()
    step = functools.partial(
        per_device, mesh.shape["band"], mesh.shape["col"], [jnp.asarray(t) for t in consts]
    )
    return jax.shard_map(
        step,
        mesh=mesh,
        in_specs=placed,
        out_specs=(P("band", "col", None), P("band", "col", None), P("band", "col", None)),
        check_vma=False,
    )
```

```python
import functools

import jax
import jax.numpy as jnp
import numpy as np
from jax import lax
from jax.experimental import pallas as pl
from jax.experimental.pallas import tpu as pltpu
from jax.sharding import PartitionSpec as P

F32 = jnp.float32
BF16 = jnp.bfloat16
MESH = pl.DeviceIdType.MESH
ANY = pl.ANY

SPAN = 4
LATS = 4
SLOTS = 4
LON = 1440
WAVES = 720
LOCAL = 90
PAD = 96
RIM = 3
MAIN = 80
TAIL = PAD - MAIN
FIRST = 48
REST = MAIN - FIRST
HEAD = FIRST + TAIL
KS = 7
CH = 384
OWN = 24
HALF = LON // 2
BLOCKS = 8
TAB = BLOCKS * PAD
WPAD = TAB // 2
ROWS = 6
HO = 200
HP = 256
FIELDS = 16
NT = (((1,), (1,)), ((), ()))


def tables():
    block = np.arange(BLOCKS)[:, None]

    def places(*spans, block=block):
        pieces = [(block * LON // 16 + 0 * np.arange(a, b), np.arange(a, b) + 0 * block) for a, b in spans]
        start = np.concatenate([p[0].reshape(-1) for p in pieces])
        return start, np.concatenate([p[1].reshape(-1) for p in pieces])

    start, place = places((0, MAIN), (MAIN, PAD))
    inside = place < LOCAL
    lon_in = start + place
    spans = ((0, FIRST), (MAIN, PAD), (FIRST, MAIN))
    halves = [places(*spans, block=block[h : h + BLOCKS // 2]) for h in (0, BLOCKS // 2)]
    start, place = [np.concatenate([half[n] for half in halves]) for n in range(2)]
    lon_out = start + np.where(place < LOCAL + RIM, place, place - PAD)
    forward = np.zeros((2, TAB, TAB), np.float64)
    inverse = np.zeros((2, TAB, TAB), np.float64)
    deal = np.zeros((2 * WPAD, TAB), np.float64)
    count = WAVES // 2
    for parity in range(2):
        wave = 2 * np.arange(count) + parity
        angle = 2 * np.pi * (wave[:, None] * lon_in[None] % LON) / LON
        forward[parity, :count] = np.cos(angle) * inside
        forward[parity, WPAD : WPAD + count] = np.sin(angle) * inside
        angle = 2 * np.pi * (lon_out[:, None] * wave[None] % LON) / LON
        inverse[parity, :, :count] = np.cos(angle)
        inverse[parity, :, WPAD : WPAD + count] = np.sin(angle)
        deal[parity * WPAD + np.arange(count), wave] = 1.0
    return [t.astype(np.float32).astype(jnp.bfloat16) for t in (forward, inverse, deal)]


def iota(shape, axis):
    return lax.broadcasted_iota(jnp.int32, shape, axis)


def one_hot(condition):
    return jnp.where(condition, 1.0, 0.0).astype(BF16)


def dot(a, b):
    return jnp.dot(a, b, preferred_element_type=F32)


def dot_nt(a, b):
    return lax.dot_general(a, b, NT, preferred_element_type=F32)


def gelu(x):
    half = 0.5 * x
    inner = x * (0.7978845608028654 + 0.035677408136300125 * (x * x))
    return (half + half * jnp.tanh(inner)).astype(BF16)


def fold(main, tail, free):
    return [
        jnp.where(free, pltpu.roll(tail, 96 - 32 * g, 1), main[TAIL * g : TAIL * g + TAIL])
        for g in range(3)
    ]


def unfold(main, lane, first):
    out = None
    for g in range(3):
        part = pltpu.roll(main[TAIL * g : TAIL * g + TAIL], 32 + 32 * g, 1)
        out = part if out is None else jnp.where(((lane - first) & 127) // 32 == g, part, out)
    return out


def windows(tile):
    out = []
    for d in range(16):
        lo, hi = max(OWN * d, 128 * tile), min(OWN * d + OWN, 128 * tile + 128)
        if lo < hi:
            out.append((d, lo, hi - lo))
    return out


def body(
    bands,
    cols,
    atm,
    gain,
    w_in,
    w_out,
    flux_t,
    pair_rows,
    pair_count,
    pair_weight,
    ocean,
    force,
    kernel_w,
    o_in,
    o_out_t,
    surf_t,
    land,
    tab_f,
    tab_i,
    deal,
    ao,
    oo,
    so,
    xv,
    st,
    x32,
    rolled,
    send1,
    recv1,
    send2,
    recv2,
    tails,
    tails2,
    tf,
    ti,
    dl,
    gv,
    gx,
    gt,
    w1,
    w2,
    fpt,
    ocv,
    oc,
    obs,
    obr,
    side_s,
    side_r,
    sel,
    selr,
    wown,
    wr,
    kv,
    kp,
    fp,
    fpc,
    oin,
    oot,
    spt,
    lm,
    lmp,
    s0,
    biga,
    bigb,
    wst,
    xs,
    fxt,
    sxt,
    mx,
    nx,
    flx,
    flr,
    bks,
    bkr,
    waves,
    sea,
    p_rows,
    p_count,
    p_weight,
    ld,
    a1s,
    a1r,
    a2s,
    a2r,
    sls,
    slr,
    ws,
    wrs,
    sds,
    sdr,
    obss,
    obrs,
    fls,
    flrs,
    bss,
    brs,
):
    me = lax.axis_index("col")
    band = lax.axis_index("band")
    up_ok = jnp.where(band > 0, 1.0, 0.0).astype(F32)
    down_ok = jnp.where(band < bands - 1, 1.0, 0.0).astype(F32)

    def col_at(k):
        return lax.rem(me + k + cols, cols)

    def away(k):
        return min(k // 4, 4 - k // 4) + min(k % 4, 4 - k % 4)

    partners = [
        lax.rem(me // 4 + k // 4, 4) * 4 + lax.rem(me % 4 + k % 4, 4)
        for k in sorted(range(1, cols), key=lambda k: -away(k))
    ]

    def exists(k):
        return band >= -k if k < 0 else band < bands - k

    def load(src, dst, k):
        c = pltpu.make_async_copy(src, dst, ld.at[k])
        c.start()
        return c

    l_atm = load(atm, xv, 0)
    barrier = pltpu.get_barrier_semaphore()
    for d in partners:
        pl.semaphore_signal(barrier, inc=1, device_id={"col": d}, device_id_type=MESH)
    for k in range(1, SPAN + 1):

        @pl.when(exists(k))
        def _():
            pl.semaphore_signal(barrier, inc=1, device_id={"band": band + k}, device_id_type=MESH)

    l_rows = load(pair_rows, p_rows, 15)
    l_count = load(pair_count, p_count, 16)
    l_weight = load(pair_weight, p_weight, 17)
    l_ocean = load(ocean, ocv, 1)
    l_force = load(force, fp, 2)
    l_kernel = load(kernel_w, kv, 3)
    l_gain = load(gain, gv, 4)
    l_deal = load(deal, dl, 5)
    l_tf = load(tab_f, tf, 6)
    l_flux = load(flux_t, fpt, 7)
    l_surf = load(surf_t, spt, 8)
    l_land = load(land, lm, 9)
    l_ti = load(tab_i, ti, 10)
    l_w1 = load(w_in, w1, 11)
    l_w2 = load(w_out, w2, 12)
    l_oin = load(o_in, oin, 13)
    l_oot = load(o_out_t, oot, 14)

    def remote(src, dst, send_sem, recv_sem, device):
        return pltpu.make_async_remote_copy(
            src_ref=src,
            dst_ref=dst,
            send_sem=send_sem,
            recv_sem=recv_sem,
            device_id=device,
            device_id_type=MESH,
        )

    def to_band(k, src, dst, send_sem, recv_sem):
        def make():
            return remote(src, dst, send_sem, recv_sem, {"band": band + k})

        def start():
            pl.when(exists(k))(lambda: make().start())

        def wait_send():
            pl.when(exists(k))(lambda: make().wait_send())

        def wait_recv():
            pl.when(exists(-k))(lambda: make().wait_recv())

        return start, wait_send, wait_recv

    def slots_to(o):
        return to_band(1 - o, sel.at[pl.ds(5 - o, 3)], selr.at[o], sls.at[o], slr.at[o])

    def weights_to(side):
        return to_band(1 - 2 * side, wown, wr.at[side], ws.at[side], wrs.at[side])

    def rim_to(side):
        src = obs.at[pl.ds(RIM * (1 - side), RIM)]
        return to_band(1 - 2 * side, src, obr.at[side], obss.at[side], obrs.at[side])

    def flux_to(o):
        return to_band(1 - o, flx, flr.at[o], fls.at[o], flrs.at[o])

    def back_to(o):
        return to_band(o, bks.at[o], bkr.at[o], bss.at[o], brs.at[o])

    lane = iota((PAD, 128), 1)
    lane16 = iota((TAIL, 128), 1)

    def phase_pack():
        st[:, LATS * LOCAL :, :] = jnp.zeros((3, LATS * (PAD - LOCAL), 128), F32)
        for l in range(LOCAL):
            for t in range(3):
                cut = slice(128 * t, 128 * t + 128)
                st[t, LATS * l : LATS * l + LATS, :] = xv[l, :, cut].astype(F32)
        for a in range(LATS):
            for t in range(3):
                part = st.at[t][pl.ds(a, PAD, stride=LATS), :]
                x32[a, :, 128 * t : 128 * t + 128] = part
                rolled[a, t] = pltpu.roll(part, OWN * a, 1) if a else part
        for d in range(cols):
            out = jnp.zeros((PAD, 128), F32)
            for t in range(3):
                for e, lo, n in windows(t):
                    if e == d:
                        for a in range(LATS):
                            mask = ((lane - (lo + OWN * a)) & 127) < n
                            out = jnp.where(mask, rolled[a, t], out)
            free = ((lane16 - OWN * d) & 127) >= 96
            for g, piece in enumerate(fold(out, out[MAIN:], free)):
                send1[d, TAIL * g : TAIL * g + TAIL] = piece.astype(BF16)
            send1[d, FIRST:] = out[FIRST:MAIN].astype(BF16)
        recv1[me] = send1[me]

    def phase_slots():
        row8 = iota((8, 128), 0)
        lane8 = iota((8, 128), 1)
        zero8 = jnp.zeros((8, 128), F32)
        for q in (0, 1, 6, 7):
            sel[q] = zero8
        for k in range(SPAN):
            other = band - k
            at = jnp.maximum(other, 0)
            used = jnp.where(other >= 0, p_count[0, at], 0)
            vec = zero8
            for p in range(SLOTS):
                target = jnp.where(p < used, SLOTS * p_rows[0, p, at] + p, -1)
                vec = jnp.where(lane8 == target, 1.0, vec)
            sel[5 - k] = vec
        vec = zero8
        for o in range(SPAN):
            at = jnp.minimum(band + o, bands - 1)
            for p in range(SLOTS):
                here = (lane8 // 16 == o) & (lane8 % SLOTS == p)
                for i in range(ROWS):
                    vec = jnp.where(here & (row8 == i), p_weight[i, p, at], vec)
        wown[...] = vec
        selr[1] = sel[4:7]
        for o in range(2, 6):

            @pl.when(jnp.logical_not(exists(o - 1)))
            def _():
                selr[o] = jnp.zeros((3, 8, 128), F32)
                flr[o] = jnp.zeros((FIRST, 128), BF16)

        @pl.when(jnp.logical_not(exists(-1)))
        def _():
            selr[0] = jnp.zeros((3, 8, 128), F32)
            flr[0] = jnp.zeros((FIRST, 128), BF16)
            wr[0] = zero8
            obr[0] = jnp.zeros((RIM, PAD, HP), BF16)

        @pl.when(jnp.logical_not(exists(1)))
        def _():
            wr[1] = zero8
            obr[1] = jnp.zeros((RIM, PAD, HP), BF16)

        for o in range(1, SPAN):

            @pl.when(jnp.logical_not(exists(-o)))
            def _():
                bkr[o] = jnp.zeros((FIRST, 128), BF16)

    def phase_rims():
        oc[RIM : RIM + ROWS] = jnp.zeros((ROWS, PAD, HP), F32)
        oc[RIM : RIM + ROWS, 0:LOCAL, 0:HO] = ocv[...].astype(F32)
        row = iota((16, HP), 0)
        for b in range(2):
            for side in range(2):
                out = jnp.zeros((16, HP), F32)
                for q in range(3):
                    i = RIM + 3 * b + q
                    part = oc[i, 0:16, :] if side == 0 else oc[i, 80:96, :]
                    shift = (RIM * q - (0 if side == 0 else 7)) % 16
                    part = pltpu.roll(part, shift, 0) if shift else part
                    out = jnp.where((row >= RIM * q) & (row < RIM * q + RIM), part, out)
                side_s[side, :, HP * b : HP * b + HP] = out.astype(BF16)
        row = iota((16, CH), 0)
        for side in range(2):
            out = jnp.zeros((16, CH), F32)
            for a in range(LATS):
                part = x32[a, 0:16, :] if side == 0 else x32[a, 80:96, :]
                shift = (RIM * a - (0 if side == 0 else 7)) % 16
                part = pltpu.roll(part, shift, 0) if shift else part
                out = jnp.where((row >= RIM * a) & (row < RIM * a + RIM), part, out)
            side_s[side, :, 2 * HP :] = out.astype(BF16)

    def phase_gains():
        gx[...] = jnp.zeros(gx.shape, F32)
        for a in range(LATS):
            for q in range(OWN // 8):
                row = pl.multiple_of(lax.rem(OWN * (me + a) + 8 * q, 128), 8)
                gx[:, pl.ds(row, 8), 0:WAVES] = gv[:, 8 * q : 8 * q + 8, :] * (2.0 / LON)
        for part in range(2):
            g = gx[part]
            high = g.astype(BF16)
            low = (g - high.astype(F32)).astype(BF16)
            both = dot_nt(dl[...], jnp.concatenate([high, low], axis=0))
            gt[part] = both[:, :128] + both[:, 128:]

    def phase_weights():
        kp[...] = jnp.zeros(kp.shape, F32)
        kp[:, 0:KS, 0:HO] = kv[...]
        f32_force = fp[...].astype(F32)
        wst[...] = jnp.zeros(wst.shape, BF16)
        fpc[...] = jnp.zeros(fpc.shape, BF16)
        for dj in range(KS):
            for di in range(KS):
                at = 128 * dj + FIELDS * di
                weight = f32_force * kp[di, dj : dj + 1, 0:HO]
                weight = weight - jnp.mean(weight, axis=-1, keepdims=True)
                wst[at : at + FIELDS, 0:HO] = weight.astype(BF16)
        fpc[FIELDS * RIM : FIELDS * RIM + FIELDS, 0:HO] = fp[...]

        r, f = iota((512, FIELDS), 0), iota((512, FIELDS), 1)
        spread = one_hot((r % 64 // 16 == r // 128) & (r % 16 == f))
        fxt[...] = dot(spread, fpt[...]).astype(BF16)
        r, f = iota((768, FIELDS), 0), iota((768, FIELDS), 1)
        spread = one_hot((r % 128 // 16 == r // 128) & (r % 16 == f))
        sxt[...] = dot(spread, spt[...]).astype(BF16)
        lmp[...] = jnp.zeros(lmp.shape, F32)
        lmp[0:ROWS, 0:LOCAL] = lm[...].astype(F32)
        r, c_ = iota((128, 128), 0), iota((128, 128), 1)
        sea[...] = dot_nt(one_hot(r == c_), lmp[...].astype(BF16))

    def with_rim(own, right, left, row, k):
        right = pltpu.roll(right, (10 - RIM * k) % 16, 0)
        left = pltpu.roll(left, (13 - RIM * k) % 16, 0)
        return jnp.where(row < 10, own, jnp.where(row < 13, right, left))

    def phase_ocean_rim():
        row = iota((16, HP), 0)
        for b in range(2):
            cut = slice(HP * b, HP * b + HP)
            right, left = side_r[0, :, cut].astype(F32), side_r[1, :, cut].astype(F32)
            for q in range(3):
                i = RIM + 3 * b + q
                oc[i, 80:96, :] = with_rim(oc[i, 80:96, :], right, left, row, q)
        obs[...] = oc[RIM : RIM + ROWS].astype(BF16)

    def phase_matrices():
        blocks = []
        for b in range(3):
            chosen = selr[0, b]
            for o in range(1, 6):
                chosen = chosen + pltpu.roll(selr[o, b], 16 * o, 1)
            if b == 0:
                blocks.append(wr[0] * chosen * up_ok)
            elif b == 1:
                blocks.append(pltpu.roll(wown[...], 16, 1) * chosen)
            else:
                blocks.append(pltpu.roll(wr[1], 32, 1) * chosen * down_ok)
        slots = jnp.concatenate(blocks, axis=0).astype(BF16)
        r, c_ = iota((384, 128), 0), iota((384, 128), 1)
        by_row = dot_nt(one_hot(r // 16 == c_ // 4), slots).astype(BF16)
        r, c_ = iota((24, 768), 0), iota((24, 768), 1)
        tap = c_ % 128 // 16
        need = c_ // 128 + tap
        has = r % 8 + jnp.where(r < 8, -RIM, jnp.where(r < 16, RIM, RIM + ROWS))
        legal = (
            (tap < KS)
            & ((r >= 8) | (r % 8 >= ROWS - RIM))
            & (r % 8 < ROWS)
            & ((r < 16) | (r % 8 < RIM))
        )
        spread = one_hot(legal & (need == has))
        r, c_ = iota((384, 768), 0), iota((384, 768), 1)
        biga[...] = jnp.where(r % 16 == c_ % 16, dot(by_row, spread), 0.0).astype(BF16)
        r, c_ = iota((128, 24), 0), iota((128, 24), 1)
        by_own = dot(one_hot((c_ - 8 == r // 16) & (r // 16 < ROWS)), slots).astype(BF16)
        r, c_ = iota((256, 128), 0), iota((256, 128), 1)
        full = dot_nt(one_hot(c_ // 4 == 4 * (r // 64 + 1) + r % 64 // 16), by_own)
        bigb[...] = jnp.where(r % 16 == c_ % 16, full, 0.0).astype(BF16)

    def phase_spectra():
        for j in range(cols):
            tails[j] = unfold(recv1[j, :FIRST].astype(F32), lane16, OWN * me).astype(BF16)

        def half_circle(k):
            at = slice(BLOCKS * k, BLOCKS * k + BLOCKS)
            main = recv1[at].reshape(BLOCKS * MAIN, 128)
            tail = tails[at].reshape(BLOCKS * TAIL, 128)
            return jnp.concatenate([main, tail], axis=0).astype(F32)

        first, second = half_circle(0), half_circle(1)
        for parity in range(2):
            mix = first - second if parity else first + second
            spec = dot(tf[parity], mix.astype(BF16))
            real, imag = spec[:WPAD], spec[WPAD:]
            rows = slice(parity * WPAD, parity * WPAD + WPAD)
            g_real, g_imag = gt[0, rows], gt[1, rows]
            waves[parity, :WPAD] = (g_real * real + g_imag * imag).astype(BF16)
            waves[parity, WPAD:] = (g_real * imag - g_imag * real).astype(BF16)

    def phase_inverse(k):
        each = BLOCKS // 2
        q = lax.rem(me // 4 + k + 1, 2)
        at = pl.ds(pl.multiple_of(q * (each * PAD), each * PAD), each * PAD)
        even = dot(ti[0, at, :], waves[0])
        odd = dot(ti[1, at, :], waves[1])
        free = ((lane16 - OWN * me) & 127) >= 96
        for n, field in enumerate((even + odd, even - odd)):
            for j in range(each):
                to = BLOCKS * n + each * q + j
                tail = each * FIRST + TAIL * j
                rest = each * HEAD + REST * j
                main = field[FIRST * j : FIRST * j + FIRST]
                for g, piece in enumerate(fold(main, field[tail : tail + TAIL], free)):
                    send2[to, TAIL * g : TAIL * g + TAIL] = piece.astype(BF16)
                send2[to, FIRST:] = field[rest : rest + REST].astype(BF16)

    def phase_stencil(half):
        if half:
            oc[RIM + ROWS :] = obr[1].astype(F32) * down_ok
        else:
            oc[0:RIM] = obr[0].astype(F32) * up_ok

        def stencil_row(i, carry):
            totals = []
            for t in range(HP // 128):
                cut = slice(128 * t, 128 * t + 128)
                total = None
                for dj in range(KS):
                    line = None
                    for di in range(KS):
                        term = kp[di, dj : dj + 1, cut] * oc[i + di, :, cut]
                        line = term if line is None else line + term
                    shift = (RIM - dj) % PAD
                    line = pltpu.roll(line, shift, 0) if shift else line
                    total = line if total is None else total + line
                totals.append(total)
            mean = sum(jnp.sum(x, axis=-1, keepdims=True) for x in totals) * (1.0 / HO)
            for t, total in enumerate(totals):
                s0[i, :, 128 * t : 128 * t + 128] = total - mean
            return carry

        lax.fori_loop(RIM * half, RIM * half + RIM, stencil_row, 0)

    def phase_atm_rim():
        row = iota((16, CH), 0)
        right, left = side_r[0, :, 2 * HP :].astype(F32), side_r[1, :, 2 * HP :].astype(F32)
        for a in range(LATS):
            x32[a, 80:96, :] = with_rim(x32[a, 80:96, :], right, left, row, a)

    def phase_unpack(part):
        if part == 0:
            for d in range(cols):
                tails2[d] = unfold(recv2[d, :FIRST].astype(F32), lane16, OWN * d)
        for a in range(LATS):
            for t in range(3):
                cut = slice(128 * t, 128 * t + 128)

                def gather(read, rows):
                    zonal = jnp.zeros((rows, 128), F32)
                    for d, lo, n in windows(t):
                        mask = ((lane[:rows] - (lo + OWN * a)) & 127) < n
                        zonal = jnp.where(mask, read(d), zonal)
                    return pltpu.roll(zonal, 128 - OWN * a, 1) if a else zonal

                if part == 0:
                    at = HEAD * a
                    main = gather(lambda d: recv2[d, :FIRST].astype(F32), FIRST)
                    mx[at : at + FIRST, cut] = x32[a, :FIRST, cut] + main
                    tail = gather(lambda d: tails2[d], TAIL)
                    mx[at + FIRST : at + HEAD, cut] = x32[a, MAIN:, cut] + tail
                else:
                    at = LATS * HEAD + REST * a
                    rest = gather(lambda d: recv2[d, FIRST:].astype(F32), REST)
                    mx[at : at + REST, cut] = x32[a, FIRST:MAIN, cut] + rest

    def phase_atm():
        mixed = mx[...]
        centred = mixed - jnp.mean(mixed, axis=-1, keepdims=True)
        spread = jnp.mean(centred * centred, axis=-1, keepdims=True)
        normed = (centred * lax.rsqrt(spread + 1e-05)).astype(BF16)
        inner = gelu(dot(normed, w1[...]))
        nx[...] = (mx[...] + dot(inner, w2[...])).astype(BF16)
        flux = None
        for a in range(LATS):
            near, rest = HEAD * a, LATS * HEAD + REST * a
            rows = jnp.concatenate([nx[near : near + HEAD], nx[rest : rest + REST]], axis=0)
            term = dot_nt(rows, fxt[128 * a : 128 * a + 128, :])
            flux = term if flux is None else flux + term
        lower = iota((FIRST, 128), 1) < 64
        upper = jnp.concatenate([flux[HEAD:], flux[FIRST:HEAD]], axis=0)
        flx[...] = jnp.where(lower, flux[:FIRST], upper).astype(BF16)
        flr[1] = flx[...]

    def phase_atm_out():
        for t in range(3):
            cut = slice(128 * t, 128 * t + 128)
            for a in range(LATS):
                at = HEAD * a
                rest = LATS * HEAD + REST * a
                for place, first, n in (
                    (0, at, FIRST),
                    (MAIN, at + FIRST, TAIL),
                    (FIRST, rest, REST),
                ):
                    part = nx[first : first + n, cut].astype(F32)
                    st.at[t][pl.ds(a + LATS * place, n, stride=LATS), :] = part
            for l in range(LOCAL):
                ao[l, :, cut] = st[t, LATS * l : LATS * l + LATS, :].astype(BF16)

    def phase_forcing():
        low = iota((FIRST, 128), 1) < 64
        tiles = []
        for q in range(3):
            even, odd = flr[2 * q].astype(F32), flr[2 * q + 1].astype(F32)
            upper = jnp.where(low, even, pltpu.roll(odd, 64, 1))
            lower = jnp.where(low, pltpu.roll(even, 64, 1), odd)
            tiles.append(jnp.concatenate([upper, lower], axis=0).astype(BF16))
        forcing = dot(jnp.concatenate(tiles, axis=1), biga[...])
        for i in range(ROWS):
            part = forcing[:, 128 * i : 128 * i + 128]
            for dj in range(KS):
                shift = (RIM - dj) % PAD
                turned = pltpu.roll(part, shift, 0) if shift else part
                xs[PAD * i : PAD * i + PAD, 128 * dj : 128 * dj + 128] = turned.astype(BF16)

    def phase_ocean():
        rows = ROWS * PAD
        stencil = (dot(xs[...], wst[...]) + s0[...].reshape(rows, HP))[:, :HO]
        spread = jnp.mean(stencil * stencil, axis=-1, keepdims=True)
        onorm = (stencil * lax.rsqrt(spread + 1e-05)).astype(BF16)
        hidden = gelu(dot(onorm, oin[...]))
        change = dot_nt(hidden, oot[...])
        pushed = dot(xs[:, 128 * RIM : 128 * RIM + 128], fpc[...])
        lifted = (oc[RIM : RIM + ROWS].reshape(rows, HP) + pushed)[:, :HO].astype(BF16).astype(F32)
        result = lifted + change
        surface = None
        for i in range(ROWS):
            part = (result[PAD * i : PAD * i + PAD] * sea[0:PAD, i : i + 1]).astype(BF16)
            oo[i] = part[:LOCAL]
            term = dot_nt(part, sxt[128 * i : 128 * i + 128, :])
            surface = term if surface is None else surface + term
        back = dot_nt(bigb[...], jnp.concatenate([surface.astype(BF16), jnp.zeros((32, 128), BF16)], axis=0))
        for o in range(SPAN):
            main, tail = back[64 * o : 64 * o + FIRST], back[64 * o + FIRST : 64 * o + 64]
            for g, piece in enumerate(fold(main, tail, lane16 >= 96)):
                bks[o, TAIL * g : TAIL * g + TAIL] = piece.astype(BF16)

    def phase_sum():
        total = bks[0].astype(F32)
        for o in range(1, SPAN):
            total = total + bkr[o].astype(F32)
        for a in range(3):
            so[a] = total[FIELDS * a : FIELDS * a + FIELDS, :LOCAL].astype(BF16)
        so[3] = unfold(total, lane16, 0)[:, :LOCAL].astype(BF16)

    l_atm.wait()
    phase_pack()
    pl.semaphore_wait(barrier, cols - 1 + jnp.minimum(band, SPAN))

    a1 = []
    for d in partners:
        step = lax.rem(d - me + cols, cols)
        c = remote(send1.at[d], recv1.at[me], a1s.at[step], a1r.at[step], {"col": d})
        c.start()
        a1.append(c)
    l_rows.wait()
    l_count.wait()
    l_weight.wait()
    phase_slots()
    weights_to(1)[0]()
    for o in range(2, 6):
        slots_to(o)[0]()
    l_ocean.wait()
    phase_rims()
    sides = []
    for side, k in ((0, -1), (1, 1)):
        c = remote(side_s.at[side], side_r.at[side], sds.at[side], sdr.at[side], {"col": col_at(k)})
        c.start()
        sides.append(c)
    l_gain.wait()
    l_deal.wait()
    phase_gains()
    l_force.wait()
    l_kernel.wait()
    l_flux.wait()
    l_surf.wait()
    l_land.wait()
    phase_weights()
    for c in sides:
        c.wait_recv()
    phase_ocean_rim()
    rim_to(1)[0]()
    weights_to(1)[2]()
    rim_to(0)[0]()
    weights_to(0)[0]()
    slots_to(0)[0]()
    phase_atm_rim()

    l_tf.wait()
    for c in a1:
        c.wait_recv()
    phase_spectra()
    l_ti.wait()
    a2 = []
    for k, across in enumerate(((1, 3), (2, 0))):
        phase_inverse(k)
        for dy in across:
            for dx in (2, 1, 3, 0):
                if dy or dx:
                    d = lax.rem(me // 4 + dy, 4) * 4 + lax.rem(me % 4 + dx, 4)
                    step = lax.rem(d - me + cols, cols)
                    c = remote(send2.at[d], recv2.at[me], a2s.at[step], a2r.at[step], {"col": d})
                    c.start()
                    a2.append(c)
    recv2[me] = send2[me]

    rim_to(1)[2]()
    phase_stencil(1)
    rim_to(0)[2]()
    phase_stencil(0)

    l_w1.wait()
    l_w2.wait()
    for c in a2:
        c.wait_recv()
    phase_unpack(0)
    phase_unpack(1)
    phase_atm()
    for o in (5, 4, 3, 2, 0):
        flux_to(o)[0]()
    phase_atm_out()
    for o in (0, 2, 3, 4, 5):
        slots_to(o)[2]()
    weights_to(0)[2]()
    phase_matrices()

    l_oin.wait()
    l_oot.wait()
    for o in (0, 2, 3, 4, 5):
        flux_to(o)[2]()
    phase_forcing()
    phase_ocean()
    for o in (3, 2, 1):
        back_to(o)[0]()
    for o in range(1, SPAN):
        back_to(o)[2]()
    phase_sum()

    for c in a1:
        c.wait_send()
    for c in sides:
        c.wait_send()
    for c in a2:
        c.wait_send()
    for o in (0, 2, 3, 4, 5):
        slots_to(o)[1]()
        flux_to(o)[1]()
    for side in range(2):
        weights_to(side)[1]()
        rim_to(side)[1]()
    for o in range(1, SPAN):
        back_to(o)[1]()


def store(a, b, c, a_out, b_out, c_out, sems):
    copies = [
        pltpu.make_async_copy(x, y, sems.at[k])
        for k, (x, y) in enumerate(((a, a_out), (b, b_out), (c, c_out)))
    ]
    for x in copies:
        x.start()
    for x in copies:
        x.wait()


def per_device(
    bands,
    cols,
    consts,
    atm_state,
    spec_gain,
    mlp_in,
    mlp_out,
    flux_proj,
    pair_rows,
    pair_count,
    pair_weight,
    ocean_state,
    force_proj,
    depth_kernel,
    ocean_in,
    ocean_out,
    surf_proj,
    land_mask,
):
    any_spec = pl.BlockSpec(memory_space=ANY)
    vm = pltpu.VMEM
    dma = pltpu.SemaphoreType.DMA
    scratch = [
        vm((LOCAL, LATS, CH), BF16),
        vm((3, LATS * PAD, 128), F32),
        vm((LATS, PAD, CH), F32),
        vm((LATS, 3, PAD, 128), F32),
        vm((16, MAIN, 128), BF16),
        vm((16, MAIN, 128), BF16),
        vm((16, MAIN, 128), BF16),
        vm((16, MAIN, 128), BF16),
        vm((16, TAIL, 128), BF16),
        vm((16, TAIL, 128), F32),
        vm((2, TAB, TAB), BF16),
        vm((2, TAB, TAB), BF16),
        vm((TAB, TAB), BF16),
        vm((2, OWN, WAVES), F32),
        vm((2, 128, TAB), F32),
        vm((2, TAB, 128), F32),
        vm((CH, 768), BF16),
        vm((768, CH), BF16),
        vm((FIELDS, CH), BF16),
        vm((ROWS, LOCAL, HO), BF16),
        vm((ROWS + 2 * RIM, PAD, HP), F32),
        vm((ROWS, PAD, HP), BF16),
        vm((2, RIM, PAD, HP), BF16),
        vm((2, 16, 2 * HP + CH), BF16),
        vm((2, 16, 2 * HP + CH), BF16),
        vm((8, 8, 128), F32),
        vm((6, 3, 8, 128), F32),
        vm((8, 128), F32),
        vm((2, 8, 128), F32),
        vm((KS, KS, HO), F32),
        vm((KS, 8, HP), F32),
        vm((FIELDS, HO), BF16),
        vm((128, HP), BF16),
        vm((HO, 800), BF16),
        vm((HO, 800), BF16),
        vm((FIELDS, HO), BF16),
        vm((ROWS, LOCAL), jnp.int32),
        vm((8, 128), F32),
        vm((ROWS, PAD, HP), F32),
        vm((384, 768), BF16),
        vm((256, 128), BF16),
        vm((KS * 128, HP), BF16),
        vm((ROWS * PAD, KS * 128), BF16),
        vm((512, CH), BF16),
        vm((768, HO), BF16),
        vm((LATS * PAD, CH), F32),
        vm((LATS * PAD, CH), BF16),
        vm((FIRST, 128), BF16),
        vm((6, FIRST, 128), BF16),
        vm((SPAN, FIRST, 128), BF16),
        vm((SPAN, FIRST, 128), BF16),
        vm((2, TAB, 128), BF16),
        vm((128, 8), F32),
        pltpu.SMEM((1, SLOTS, bands), jnp.int32),
        pltpu.SMEM((1, bands), jnp.int32),
        pltpu.SMEM((ROWS, SLOTS, bands), F32),
        dma((18,)),
        dma((16,)),
        dma((16,)),
        dma((16,)),
        dma((16,)),
        dma((6,)),
        dma((6,)),
        dma((2,)),
        dma((2,)),
        dma((2,)),
        dma((2,)),
        dma((2,)),
        dma((2,)),
        dma((6,)),
        dma((6,)),
        dma((4,)),
        dma((4,)),
    ]
    shapes = (
        jax.ShapeDtypeStruct((LOCAL, LATS, CH), BF16),
        jax.ShapeDtypeStruct((ROWS, LOCAL, HO), BF16),
        jax.ShapeDtypeStruct((LATS, FIELDS, LOCAL), BF16),
    )
    out = pl.pallas_call(
        functools.partial(body, bands, cols),
        out_shape=tuple(vm(x.shape, x.dtype) for x in shapes),
        in_specs=[any_spec] * 18,
        out_specs=(pl.BlockSpec(memory_space=vm),) * 3,
        scratch_shapes=scratch,
        compiler_params=pltpu.CompilerParams(
            collective_id=0, has_side_effects=True, vmem_limit_bytes=56 * 1024 * 1024
        ),
    )(
        jnp.transpose(atm_state, (1, 0, 2)),
        jnp.transpose(spec_gain, (0, 2, 1)),
        mlp_in,
        mlp_out,
        jnp.transpose(flux_proj),
        jnp.transpose(pair_rows, (1, 2, 0)),
        jnp.transpose(pair_count),
        jnp.transpose(pair_weight, (0, 2, 1)),
        ocean_state,
        force_proj,
        depth_kernel,
        ocean_in,
        jnp.transpose(ocean_out),
        jnp.transpose(surf_proj),
        land_mask,
        *consts,
    )
    out = pl.pallas_call(
        store,
        out_shape=shapes,
        in_specs=[pl.BlockSpec(memory_space=vm)] * 3,
        out_specs=(any_spec,) * 3,
        scratch_shapes=[dma((3,))],
    )(*[pltpu.with_memory_space_constraint(x, vm) for x in out])
    return (
        jnp.transpose(out[0], (1, 0, 2)),
        out[1],
        jnp.transpose(out[2], (0, 2, 1)),
    )


def solution(mesh):
    placed = (
        P("band", "col", None),
        P(None, None, "col"),
        P(),
        P(),
        P(),
        P(None, "band", None),
        P(None, "band"),
        P("band", None, None),
        P("band", "col", None),
        P(),
        P(),
        P(),
        P(),
        P(),
        P("band", "col"),
    )
    consts = tables()
    step = functools.partial(
        per_device, mesh.shape["band"], mesh.shape["col"], [jnp.asarray(t) for t in consts]
    )
    return jax.shard_map(
        step,
        mesh=mesh,
        in_specs=placed,
        out_specs=(P("band", "col", None), P("band", "col", None), P("band", "col", None)),
        check_vma=False,
    )
```
